128 devices in a mesh: batch: 8 (over x, core), seq: 16 (over z, y).
Axes of the slice: x: 4, y: 4, z: 4, core: 2. Of those that a mesh axis runs over, the one named last changes fastest.
Arguments:
- latents: bfloat16 [8, 64, 1024], P('batch'), may hold values from -16 to 16
- frames: bfloat16 [512, 128, 1152], P(('batch', 'seq')), may hold values from -40 to 40
- counts: int32 [512], P(('batch', 'seq')), may hold values from 1 to 128, as said below
- groups: int32 [512], P(('batch', 'seq')), may hold values from 0 to 7, as said below
- w_query: bfloat16 [1024, 1024], replicated, may hold values from -0.5 to 0.5
- w_kv: bfloat16 [1152, 2048], replicated, may hold values from -0.5 to 0.5
- w_out: bfloat16 [1024, 1024], replicated, may hold values from -0.1875 to 0.1875
- d_out: bfloat16 [8, 64, 1024], P('batch'), may hold values from -6 to 6
Outputs:
- out: bfloat16 [8, 64, 1024], P('batch')
- d_latents: bfloat16 [8, 64, 1024], P('batch')
- grad_query: float32 [1024, 1024], P('seq')
- grad_outproj: float32 [1024, 1024], P('seq')
- grad_kv: float32 [1152, 2048], P(('batch', 'seq'))
The draws below stay inside these ranges and needn't reach their ends.
Inputs may be any that keep to these rules, and one draw needn't show every extreme that they name: Rows 0 to counts[i] - 1 of block i hold tokens, the rest is padding; the first block of every source device is full. `groups`: the blocks of one source device name no group more than 2 times. At every seq index one group is named exactly 2 times by every source device at that seq index, and every group is that group at some seq index.
All inputs are finite; a program needn't handle non-finite values.
Results may differ from the reference program's by a relative error of at most 0.0055.
The reference program's roundings to bfloat16 on the way count: a program that leaves them out, or rounds other values in their place, can miss the bound.
Values may be sent and summed in bfloat16 or wider, within the bound.
No kernel may reach another device: no remote copies, remote signals or barrier semaphores. Data moves between devices by JAX's collectives and lax.ppermute only.
A program may use at most 128 MiB of HBM per device.

```python
import math
import jax
import jax.numpy as jnp
from jax import lax

D = 1024
H = 16
HD = 64
FD = 1152
LAT = 64
BLK = 128
CAP = 2
SRC_BLK = 4
GROUPS = 8
DEVICES = 128


def draw_latents(key, part):
    key = jax.random.fold_in(key, 3)
    value_key, scale_key = jax.random.split(key)
    scales = jnp.exp(jax.random.uniform(scale_key, (GROUPS, LAT, 1), minval=math.log(0.4), maxval=math.log(4.0)))
    values = jax.random.normal(value_key, (GROUPS, LAT, D)) * scales
    return jnp.clip(values, -16.0, 16.0).astype(jnp.bfloat16)


def draw_frames(key, part):
    key = jax.random.fold_in(key, 5)
    value_key, scale_key = jax.random.split(key, 2)
    shape = (DEVICES * SRC_BLK, BLK, FD)
    scales = jnp.exp(jax.random.uniform(scale_key, (DEVICES * SRC_BLK, BLK, 1), minval=0.0, maxval=math.log(10.0)))
    values = jax.random.normal(value_key, shape) * scales
    return jnp.clip(values, -40.0, 40.0).astype(jnp.bfloat16)


def draw_w_query(key, part):
    key = jax.random.fold_in(key, 9)
    values = jax.random.normal(key, (D, D)) / math.sqrt(D)
    return jnp.clip(values, -0.5, 0.5).astype(jnp.bfloat16)


def draw_w_kv(key, part):
    key = jax.random.fold_in(key, 13)
    values = jax.random.normal(key, (FD, 2 * D)) / math.sqrt(FD)
    return jnp.clip(values, -0.5, 0.5).astype(jnp.bfloat16)


def draw_counts(key, part):
    key = jax.random.fold_in(key, 11)
    values = jax.random.randint(key, (DEVICES * SRC_BLK,), 1, BLK + 1)
    leading = jnp.arange(DEVICES * SRC_BLK) % SRC_BLK == 0
    return jnp.where(leading, BLK, values).astype(jnp.int32)


def draw_groups(key, part):
    key = jax.random.fold_in(key, 7)
    offset_key, spread_key, shuffle_key = jax.random.split(key, 3)
    seq_count = DEVICES // GROUPS
    offset = jax.random.randint(offset_key, (), 0, GROUPS)
    device = jnp.arange(DEVICES, dtype=jnp.int32)
    crowded = (device % seq_count + offset) % GROUPS
    others = (GROUPS - 1) * CAP
    candidates = (crowded[:, None] + 1 + jnp.arange(others, dtype=jnp.int32)[None, :] // CAP) % GROUPS
    ranking = jax.random.randint(spread_key, (DEVICES, others), 0, 1 << 20) * others + jnp.arange(others, dtype=jnp.int32)[None, :]
    picked = jnp.take_along_axis(candidates, jnp.argsort(ranking, axis=1)[:, :CAP], axis=1)
    chosen = jnp.concatenate([jnp.broadcast_to(crowded[:, None], (DEVICES, CAP)), picked], axis=1)
    mixing = jax.random.randint(shuffle_key, (DEVICES, 2 * CAP), 0, 1 << 20) * (2 * CAP) + jnp.arange(2 * CAP, dtype=jnp.int32)[None, :]
    chosen = jnp.take_along_axis(chosen, jnp.argsort(mixing, axis=1), axis=1)
    return chosen.reshape(DEVICES * SRC_BLK).astype(jnp.int32)


def levels(stream_key, extent, pieces, least, top_value):
    gain = 1.0
    for axis_at, shards_of in pieces:
        steps = jax.random.uniform(jax.random.fold_in(jax.random.fold_in(stream_key, 6), axis_at), (shards_of,), jnp.float32, least / len(pieces), top_value / len(pieces))
        gain = gain * jnp.repeat(jnp.exp(steps), extent[axis_at] // shards_of).reshape((-1,) + (1,) * (len(extent) - 1 - axis_at))
    return gain


def normal_values(own_key, dims, spread, limit, cuts=(), kind=jnp.bfloat16):
    gain = levels(own_key, dims, cuts, -0.22, 0.18) if cuts else 1.0
    drawn = jax.random.normal(own_key, dims, jnp.float32) * spread * gain
    return jnp.minimum(jnp.maximum(drawn, -limit), limit).astype(kind)


def setup_inputs(seed: int = 0) -> dict:
    seeds = jax.random.split(jax.random.key(seed), 9)
    return {
        "latents": draw_latents(jax.random.fold_in(seeds[8], 71), 0),
        "frames": draw_frames(jax.random.fold_in(seeds[8], 71), 0),
        "counts": draw_counts(jax.random.fold_in(seeds[8], 71), 0),
        "groups": draw_groups(jax.random.fold_in(seeds[8], 71), 0),
        "w_query": draw_w_query(jax.random.fold_in(seeds[8], 71), 0),
        "w_kv": draw_w_kv(jax.random.fold_in(seeds[8], 71), 0),
        "w_out": normal_values(seeds[6], (D, D), D ** -0.5, 0.1875),
        "d_out": normal_values(seeds[7], (GROUPS, LAT, D), 1.0, 6.0, ((0, 8),)),
    }


epsilon = 1e-06

def rms_rows(values):
    return values * lax.rsqrt(lax.optimization_barrier(jnp.mean(values * values, axis=-1, keepdims=True)) + epsilon)

def rms_back(values, grads):
    factor = lax.rsqrt(lax.optimization_barrier(jnp.mean(values * values, axis=-1, keepdims=True)) + epsilon)
    normed = values * factor
    return factor * (grads - normed * lax.optimization_barrier(jnp.mean(grads * normed, axis=-1, keepdims=True)))

def rounded(values):
    return lax.optimization_barrier(values.astype(jnp.bfloat16)).astype(jnp.float32)

def reference(latents, frames, counts, groups, w_query, w_kv, w_out, d_out):
    score_scale = HD ** (-0.5)
    flat_frames = frames.reshape(-1, FD).astype(jnp.float32)
    token_total = flat_frames.shape[0]
    normed_frames = rms_rows(flat_frames).astype(jnp.bfloat16)
    pairs = jnp.dot(normed_frames, w_kv, preferred_element_type=jnp.float32)
    pairs = rounded(pairs)
    key_heads = pairs[:, :D].reshape(token_total, H, HD)
    value_heads = pairs[:, D:].reshape(token_total, H, HD)
    positions = jnp.arange(BLK, dtype=jnp.int32)
    usable = (positions[None, :] < counts[:, None]).reshape(-1)
    owner_group = jnp.repeat(groups, BLK)
    latent_values = latents.astype(jnp.float32)
    normed_latents = rms_rows(latent_values).astype(jnp.bfloat16)
    queries = jnp.dot(normed_latents.reshape(-1, D), w_query, preferred_element_type=jnp.float32)
    queries = queries.astype(jnp.bfloat16).reshape(GROUPS, LAT, D)

    def one_group(running, inputs):
        grad_rows, query_acc, outproj_acc = running
        group_index, query_rows, latent, normed_one, cotangent = inputs
        query_heads = lax.optimization_barrier(query_rows).astype(jnp.float32).reshape(LAT, H, HD)
        member = usable & (owner_group == group_index)
        scores = jnp.einsum('lhd,thd->hlt', query_heads, key_heads) * score_scale
        masked = jnp.where(member[None, None, :], scores, -1e+30)
        row_top = lax.optimization_barrier(jnp.max(masked, axis=-1, keepdims=True))
        raw_weights = jnp.where(member[None, None, :], jnp.exp(masked - row_top), 0.0)
        weights = raw_weights / lax.optimization_barrier(jnp.sum(raw_weights, axis=-1, keepdims=True))
        weights_b = rounded(weights)
        attended = jnp.einsum('hlt,thd->lhd', weights_b, value_heads).reshape(LAT, D)
        mixed_b = attended.astype(jnp.bfloat16)
        update = jnp.dot(mixed_b, w_out, preferred_element_type=jnp.float32)
        result = (latent.astype(jnp.float32) + update).astype(jnp.bfloat16)
        outproj_acc = outproj_acc + jnp.dot(mixed_b.T, cotangent, preferred_element_type=jnp.float32)
        d_mixed = rounded(jnp.dot(cotangent, w_out.T, preferred_element_type=jnp.float32))
        d_heads = d_mixed.reshape(LAT, H, HD)
        d_weights = jnp.einsum('lhd,thd->hlt', d_heads, value_heads)
        row_delta = jnp.einsum('lhd,lhd->hl', d_heads, attended.reshape(LAT, H, HD))
        d_scores = rounded(weights * (d_weights - row_delta[:, :, None]) * score_scale)
        d_query = jnp.einsum('hlt,thd->lhd', d_scores, key_heads).reshape(LAT, D).astype(jnp.bfloat16)
        d_keys = jnp.einsum('hlt,lhd->thd', d_scores, query_heads).reshape(token_total, D)
        d_values = jnp.einsum('hlt,lhd->thd', weights_b, d_heads).reshape(token_total, D)
        d_pairs = rounded(jnp.concatenate([d_keys, d_values], axis=1))
        grad_rows = grad_rows + d_pairs
        query_acc = query_acc + jnp.dot(normed_one.T, d_query, preferred_element_type=jnp.float32)
        d_normed = jnp.dot(d_query, w_query.T, preferred_element_type=jnp.float32)
        d_latent = (cotangent.astype(jnp.float32) + rms_back(latent.astype(jnp.float32), d_normed)).astype(jnp.bfloat16)
        return ((grad_rows, query_acc, outproj_acc), (result, d_latent))
    start_state = (jnp.zeros((token_total, 2 * D), jnp.float32), jnp.zeros((D, D), jnp.float32), jnp.zeros((D, D), jnp.float32))
    inputs = (jnp.arange(GROUPS, dtype=jnp.int32), queries, latents, normed_latents, d_out)
    final_state, outputs = lax.scan(one_group, start_state, inputs)
    grad_rows, grad_query, grad_outproj = final_state
    out, d_latents = outputs
    grad_kv = jnp.dot(normed_frames.T, grad_rows.astype(jnp.bfloat16), preferred_element_type=jnp.float32)
    return (out, d_latents, grad_query, grad_outproj, grad_kv)
```

```python
import jax
import jax.numpy as jnp
from jax import lax
from jax.sharding import Mesh, PartitionSpec as P

H = 16
BATCH = ("x", "core")
SEQ = ("z", "y")
CHIPS = ("x", "z", "y")
ALL = BATCH + SEQ
SLOTS = 3

epsilon = 1e-06
f32 = jnp.float32
bf16 = jnp.bfloat16


def rms_rows(values):
    return values * lax.rsqrt(jnp.mean(values * values, axis=-1, keepdims=True) + epsilon)


def rms_back(values, grads):
    factor = lax.rsqrt(jnp.mean(values * values, axis=-1, keepdims=True) + epsilon)
    normed = values * factor
    return factor * (grads - normed * jnp.mean(grads * normed, axis=-1, keepdims=True))


def normalize(values):
    return rms_rows(values.astype(f32)).astype(bf16)


def exchange(values, axes):
    return lax.all_to_all(values, axes, 0, 0, tiled=True)


def share(values, axes, count):
    return exchange(jnp.broadcast_to(values[None], (count,) + values.shape), axes)


def other_core(values):
    return lax.ppermute(values, "core", [(0, 1), (1, 0)])


def chip_step(values, step):
    return lax.ppermute(values, "x", [(i, (i + step) % 4) for i in range(4)])


def gather_batch(values):
    near = jnp.stack([values, chip_step(values, 1), chip_step(values, 2), chip_step(values, 3)])
    return jnp.concatenate([near, other_core(near)], axis=0)


def place_of(group):
    chip = lax.rem(lax.axis_index("x") - group // 2 + 4, 4)
    return jnp.where(group % 2 == lax.axis_index("core"), 0, 4) + chip


def pick(values, places):
    return jnp.stack([lax.dynamic_index_in_dim(values, place, 0, False) for place in places])


def local(latents, frames, counts, groups, w_query, w_kv, w_out, d_out):
    blocks, block_rows, feature = frames.shape
    latent_count, model_width = latents.shape[1:]
    head_dim = model_width // H
    scale = head_dim ** (-0.5)
    group_count, seq_count = 8, 16
    rows = blocks * block_rows
    core = lax.axis_index("core")
    batch_at = lax.axis_index(BATCH)
    seq_at = lax.axis_index(SEQ)

    latents_all = gather_batch(latents[0])
    d_out_all = gather_batch(d_out[0])

    normed = normalize(frames).reshape(rows, feature)
    normed_both = jnp.concatenate([normed, other_core(normed)], axis=0)
    pairs = jnp.dot(normed, w_kv, preferred_element_type=f32).astype(bf16)
    keys = pairs[:, :model_width].reshape(blocks, block_rows, H, head_dim)
    values = pairs[:, model_width:].reshape(blocks, block_rows, H, head_dim)

    places = [place_of(groups[i]) for i in range(blocks)]
    picked = normalize(pick(latents_all, places))
    queries = jnp.dot(
        picked.reshape(-1, model_width), w_query, preferred_element_type=f32
    ).astype(bf16).reshape(blocks, latent_count, H, head_dim)
    d_mixed = lax.dot_general(
        pick(d_out_all, places).reshape(-1, model_width),
        w_out,
        (((1,), (1,)), ((), ())),
        preferred_element_type=f32,
    ).astype(bf16).reshape(blocks, latent_count, H, head_dim)

    order = jnp.arange(blocks)
    same = groups[:, None] == groups[None, :]
    first = jnp.min(jnp.where(same, order[None, :], blocks), axis=1)
    leads = first == order
    slot = jnp.sum(leads[None, :] & (order[None, :] < first[:, None]), axis=1)
    slot_groups = jnp.max(
        jnp.where(slot[None, :] == jnp.arange(SLOTS)[:, None], groups[None, :], -1), axis=1
    )

    usable = (jnp.arange(block_rows)[None, :] < counts[:, None])[:, None, None, :]
    scores = jnp.einsum("blhd,bthd->bhlt", queries, keys, preferred_element_type=f32) * scale
    masked = jnp.where(usable, scores, -1e30)
    top = jnp.max(masked, axis=3)
    raw = jnp.where(usable, jnp.exp(masked - top[..., None]), 0.0)
    total = jnp.sum(raw, axis=3)
    d_weights = jnp.einsum("blhd,bthd->bhlt", d_mixed, values, preferred_element_type=f32)
    moment = jnp.sum(raw * d_weights, axis=3)

    mine = (jnp.arange(group_count)[:, None] == groups[None, :])[:, :, None, None]
    tops = jnp.where(mine, top[None], -1e30)
    group_top = jnp.max(tops, axis=1)
    factor = jnp.where(mine, jnp.exp(tops - group_top[:, None]), 0.0)
    note = jnp.zeros((1, 1, latent_count), f32).at[0, 0, :SLOTS].set(slot_groups.astype(f32))
    stats = jnp.stack(
        [
            group_top,
            jnp.sum(factor * total[None], axis=1),
            jnp.sum(factor * moment[None], axis=1),
            jnp.broadcast_to(note, group_top.shape),
        ],
        axis=2,
    )
    stats = exchange(stats.reshape(128, 2, 128), ALL).reshape(128, 4, latent_count)
    far_top = jnp.max(stats[:, 0], axis=0)
    far_factor = jnp.exp(stats[:, 0] - far_top)
    far_total = jnp.sum(far_factor * stats[:, 1], axis=0)
    far_moment = jnp.sum(far_factor * stats[:, 2], axis=0)
    source_groups = lax.dynamic_index_in_dim(
        stats[:, 3, :SLOTS].reshape(group_count, seq_count, SLOTS), batch_at, 0, False
    )
    reply = jnp.stack([far_top, 1.0 / far_total, far_moment / far_total, far_total])
    reply = share(reply.reshape(2, 128), ALL, 128).reshape(group_count, H, 4, latent_count)
    reply = pick(reply, [groups[i] for i in range(blocks)])

    weights = jnp.where(
        usable, jnp.exp(masked - reply[:, :, 0, :, None]) * reply[:, :, 1, :, None], 0.0
    )
    weights_b = weights.astype(bf16)
    d_scores = (weights * (d_weights - reply[:, :, 2, :, None]) * scale).astype(bf16)
    mixed = jnp.einsum("bhlt,bthd->bhld", weights_b, values, preferred_element_type=f32)
    query_term = jnp.einsum("bhlt,bthd->bhld", d_scores, keys, preferred_element_type=f32)
    d_keys = jnp.einsum("bhlt,blhd->bthd", d_scores, queries, preferred_element_type=f32)
    d_values = jnp.einsum("bhlt,blhd->bthd", weights_b, d_mixed, preferred_element_type=f32)
    d_keys = d_keys.astype(bf16).reshape(rows, model_width)
    d_values = d_values.astype(bf16).reshape(rows, model_width)

    kept = jnp.where(core == 0, d_keys, d_values)
    sent = jnp.where(core == 0, d_values, d_keys)
    d_half = jnp.concatenate([kept, other_core(sent)], axis=0)
    term = lax.dot_general(
        normed_both, d_half, (((0,), (0,)), ((), ())), preferred_element_type=f32
    ).astype(bf16)
    share_rows = feature // 128
    term = term.reshape(4, 2, seq_count, share_rows, 8, 128).transpose(0, 2, 1, 3, 4, 5)
    term = exchange(term.reshape(64, 2 * share_rows, 8, 128), CHIPS)
    chip_sum = jnp.sum(term.astype(f32), axis=0).reshape(2, share_rows, model_width)
    kept_sum = lax.dynamic_index_in_dim(chip_sum, core, 0, False)
    got_sum = other_core(lax.dynamic_index_in_dim(chip_sum, 1 - core, 0, False))
    grad_kv = jnp.where(
        core == 0,
        jnp.concatenate([kept_sum, got_sum], axis=1),
        jnp.concatenate([got_sum, kept_sum], axis=1),
    )

    both = jnp.concatenate([mixed, query_term], axis=3)
    slotted = jnp.stack(
        [
            jnp.sum(jnp.where((slot == k)[:, None, None, None], both, 0.0), axis=0)
            for k in range(SLOTS)
        ],
        axis=1,
    ).astype(bf16)
    slotted = exchange(slotted, SEQ)
    chosen = (
        jnp.arange(group_count, dtype=f32)[:, None, None] == source_groups[None]
    ).astype(bf16)
    by_group = jnp.einsum("gsk,sklc->glc", chosen, slotted, preferred_element_type=f32)
    owned = jnp.sum(exchange(by_group, BATCH), axis=0).astype(bf16)
    over_seq = share(owned, SEQ, seq_count)
    mixed_b = over_seq[:, :, :head_dim].transpose(1, 0, 2).reshape(latent_count, model_width)
    d_query = over_seq[:, :, head_dim:].transpose(1, 0, 2).reshape(latent_count, model_width)
    latent = latents[0].astype(f32)
    cotangent = d_out[0]
    out = (latent + jnp.dot(mixed_b, w_out, preferred_element_type=f32)).astype(bf16)
    d_normed = lax.dot_general(
        d_query, w_query, (((1,), (1,)), ((), ())), preferred_element_type=f32
    )
    d_latents = (cotangent.astype(f32) + rms_back(latent, d_normed)).astype(bf16)

    group_places = [place_of(jnp.int32(g)) for g in range(group_count)]
    mixed_heads = share(owned[:, :head_dim], BATCH, group_count)
    grad_outproj = jnp.einsum(
        "glr,glc->rc", mixed_heads, pick(d_out_all, group_places), preferred_element_type=f32
    )
    latent_cols = lax.dynamic_slice_in_dim(
        normalize(latents_all), seq_at * head_dim, head_dim, 2
    )
    d_query_all = share(d_query, BATCH, group_count)
    grad_query = jnp.einsum(
        "glr,glc->rc", pick(latent_cols, group_places), d_query_all, preferred_element_type=f32
    )
    return (out[None], d_latents[None], grad_query, grad_outproj, grad_kv)


def solution(mesh):
    chips = Mesh(mesh.devices.reshape(4, 2, 4, 4), ("x", "core", "z", "y"))
    in_specs = (
        P(BATCH, None, None),
        P(ALL, None, None),
        P(ALL),
        P(ALL),
        P(),
        P(),
        P(),
        P(BATCH, None, None),
    )
    out_specs = (
        P(BATCH, None, None),
        P(BATCH, None, None),
        P(SEQ, None),
        P(SEQ, None),
        P(ALL, None),
    )
    return jax.shard_map(local, mesh=chips, in_specs=in_specs, out_specs=out_specs, check_vma=False)
```

```python
import functools

import jax
import jax.numpy as jnp
from jax import lax
from jax.experimental import pallas as pl
from jax.experimental.pallas import tpu as pltpu
from jax.sharding import Mesh, PartitionSpec as P

H = 16
BATCH = ("x", "core")
SEQ = ("z", "y")
CHIPS = ("x", "z", "y")
ALL = BATCH + SEQ
SLOTS = 3

epsilon = 1e-06
f32 = jnp.float32
bf16 = jnp.bfloat16


def rms_rows(values):
    return values * lax.rsqrt(jnp.mean(values * values, axis=-1, keepdims=True) + epsilon)


def rms_back(values, grads):
    factor = lax.rsqrt(jnp.mean(values * values, axis=-1, keepdims=True) + epsilon)
    normed = values * factor
    return factor * (grads - normed * jnp.mean(grads * normed, axis=-1, keepdims=True))


def normalize(values):
    return rms_rows(values.astype(f32)).astype(bf16)


def exchange(values, axes):
    return lax.all_to_all(values, axes, 0, 0, tiled=True)


def share(values, axes, count):
    return exchange(jnp.broadcast_to(values[None], (count,) + values.shape), axes)


def other_core(values):
    return lax.ppermute(values, "core", [(0, 1), (1, 0)])


def chip_step(values, step):
    return lax.ppermute(values, "x", [(i, (i + step) % 4) for i in range(4)])


def gather_batch(values):
    near = [values, chip_step(values, 1), chip_step(values, 2), chip_step(values, 3)]
    return near + [other_core(piece) for piece in near]


def place_of(group):
    chip = lax.rem(lax.axis_index("x") - group // 2 + 4, 4)
    return jnp.where(group % 2 == lax.axis_index("core"), 0, 4) + chip


def group_at(place):
    chip = lax.rem(lax.axis_index("x") - place % 4 + 4, 4)
    core = lax.axis_index("core")
    return 2 * chip + (core if place < 4 else 1 - core)


SMEM = pl.BlockSpec(memory_space=pltpu.SMEM)
VMEM = pl.BlockSpec(memory_space=pltpu.VMEM)
LAST = (((1,), (1,)), ((), ()))
FIRST = (((0,), (0,)), ((), ()))


def project_kernel(norm, transposed, places, *refs):
    pieces, (w_ref, out_ref, picked) = refs[:8], refs[8:]
    rows = pieces[0].shape[0]
    for i in range(out_ref.shape[0] // rows):
        for j in range(8):

            @pl.when(places[i] == j)
            def _():
                picked[i * rows : (i + 1) * rows, :] = pieces[j][...]

    x = picked[...]
    if norm:
        x = normalize(x)
    numbers = LAST if transposed else (((1,), (0,)), ((), ()))
    out_ref[...] = lax.dot_general(x, w_ref[...], numbers, preferred_element_type=f32).astype(bf16)


def project(places, pieces, weight, norm, transposed):
    rows, width = pieces[0].shape
    out = jax.ShapeDtypeStruct((places.shape[0] * rows, weight.shape[0]), bf16)
    return pl.pallas_call(
        functools.partial(project_kernel, norm, transposed),
        out_shape=out,
        in_specs=[SMEM] + [VMEM] * 9,
        out_specs=VMEM,
        scratch_shapes=[pltpu.VMEM((out.shape[0], width), bf16)],
        cost_estimate=pl.CostEstimate(
            flops=2 * out.shape[0] * width * weight.shape[0],
            bytes_accessed=4 * 1024 * 1024,
            transcendentals=0,
        ),
    )(places, *pieces, weight)


def low_lanes(shape):
    return lax.broadcasted_iota(jnp.int32, shape, len(shape) - 1) < 64


def spread(pair, low, high):
    return jnp.concatenate([pair * low, pair * high], axis=0)


def half_masks():
    lane = low_lanes((1, 128))
    return jnp.where(lane, 1.0, 0.0).astype(bf16), jnp.where(lane, 0.0, 1.0).astype(bf16)


def slots_of(groups):
    slots, used = [0], 1
    for i in range(1, 4):
        slot = used
        fresh = True
        for j in reversed(range(i)):
            slot = jnp.where(groups[i] == groups[j], slots[j], slot)
            fresh = fresh & (groups[i] != groups[j])
        slots.append(slot)
        used = used + jnp.where(fresh, 1, 0)
    return slots


def stats_kernel(counts, groups, q_ref, d_ref, pairs_ref, out_ref, top_ref, total_ref, moment_ref):
    block = pl.program_id(0)
    low, high = half_masks()
    width = q_ref.shape[1]
    scale = (width // H) ** (-0.5)
    usable = lax.broadcasted_iota(jnp.int32, (128, 128), 0) < counts[block]
    for p in range(width // 128):
        cols = slice(128 * p, 128 * p + 128)
        value_cols = slice(width + 128 * p, width + 128 * p + 128)
        s = lax.dot_general(
            pairs_ref[:, cols], spread(q_ref[:, cols], low, high), LAST, preferred_element_type=f32
        )
        s = jnp.where(usable, s * scale, -1e30)
        top = jnp.max(s, axis=0, keepdims=True)
        raw = jnp.where(usable, jnp.exp(s - top), 0.0)
        dw = lax.dot_general(
            pairs_ref[:, value_cols],
            spread(d_ref[:, cols], low, high),
            LAST,
            preferred_element_type=f32,
        )
        top_ref[block, p : p + 1, :] = top
        total_ref[block, p : p + 1, :] = jnp.sum(raw, axis=0, keepdims=True)
        moment_ref[block, p : p + 1, :] = jnp.sum(raw * dw, axis=0, keepdims=True)

    @pl.when(block == 3)
    def _():
        own = [groups[i] for i in range(4)]
        slots = slots_of(own)
        left = low_lanes((8, 128))
        lane = lax.broadcasted_iota(jnp.int32, (8, 128), 1)
        note = jnp.full((8, 128), -1.0, f32)
        for i in range(4):
            note = jnp.where(lane == 64 + slots[i], own[i].astype(f32), note)
        for g in range(8):
            tops = [jnp.where(own[i] == g, top_ref[i], -1e30) for i in range(4)]
            top = functools.reduce(jnp.maximum, tops)
            total = jnp.zeros((8, 128), f32)
            moment = jnp.zeros((8, 128), f32)
            for i in range(4):
                factor = jnp.where(own[i] == g, jnp.exp(tops[i] - top), 0.0)
                total = total + factor * total_ref[i]
                moment = moment + factor * moment_ref[i]
            out_ref[g, 0:8, 0:128] = jnp.where(left, top, pltpu.roll(total, 64, 1))
            out_ref[g, 8:16, 0:128] = jnp.where(left, pltpu.roll(top, 64, 1), total)
            out_ref[g, 0:8, 128:256] = jnp.where(left, moment, note)
            out_ref[g, 8:16, 128:256] = jnp.where(left, pltpu.roll(moment, 64, 1), note)


def block_specs(latent_count, width):
    return [
        pl.BlockSpec((latent_count, width), lambda i: (i, 0)),
        pl.BlockSpec((latent_count, width), lambda i: (i, 0)),
        pl.BlockSpec((128, 2 * width), lambda i: (i, 0)),
    ]


def statistics(counts, groups, queries, d_mixed, pairs):
    width = queries.shape[1]
    return pl.pallas_call(
        stats_kernel,
        grid=(4,),
        out_shape=jax.ShapeDtypeStruct((8, 16, 256), f32),
        in_specs=[SMEM, SMEM] + block_specs(queries.shape[0] // 4, width),
        out_specs=pl.BlockSpec((8, 16, 256), lambda i: (0, 0, 0)),
        scratch_shapes=[pltpu.VMEM((4, 8, 128), f32)] * 3,
        cost_estimate=pl.CostEstimate(
            flops=4 * 1024 * 1024 * 1024, bytes_accessed=4 * 1024 * 1024, transcendentals=512 * 1024
        ),
    )(counts, groups, queries, d_mixed, pairs)


def totals_kernel(in_ref, out_ref):
    left = low_lanes((1, 128))
    first = in_ref[:, 0:128]
    top = jnp.max(first, axis=0, keepdims=True)
    top = jnp.where(left, top, pltpu.roll(top, 64, 1))
    factor = jnp.exp(jnp.where(left, first, pltpu.roll(first, 64, 1)) - top)
    total = jnp.sum(factor * first, axis=0, keepdims=True)
    inverse = 1.0 / jnp.where(left, pltpu.roll(total, 64, 1), total)
    delta = jnp.sum(factor * in_ref[:, 128:256], axis=0, keepdims=True) * inverse
    out_ref[:, 0:128] = jnp.broadcast_to(jnp.where(left, top, inverse), first.shape)
    out_ref[:, 128:256] = jnp.broadcast_to(jnp.where(left, delta, 0.0), first.shape)


def totals(stats):
    return pl.pallas_call(
        totals_kernel,
        out_shape=jax.ShapeDtypeStruct(stats.shape, f32),
        in_specs=[VMEM],
        out_specs=VMEM,
    )(stats)


def grads_kernel(
    counts, groups, core, q_ref, d_ref, pairs_ref, reply_ref, d_pairs_ref, slotted_ref, mixed_acc, query_acc
):
    block = pl.program_id(0)
    low, high = half_masks()
    rows, width = q_ref.shape
    scale = (width // H) ** (-0.5)
    usable = lax.broadcasted_iota(jnp.int32, (128, 128), 0) < counts[block]
    left = low_lanes((8, 128))
    wide = low_lanes((rows, 128))

    @pl.when(block == 0)
    def _():
        mixed_acc[...] = jnp.zeros_like(mixed_acc)
        query_acc[...] = jnp.zeros_like(query_acc)

    slots = slots_of([groups[i] for i in range(4)])
    slot = slots[0]
    for i in range(1, 4):
        slot = jnp.where(block == i, slots[i], slot)
    group = groups[block]
    even = reply_ref[group, 0:8, 0:128]
    odd = reply_ref[group, 8:16, 0:128]
    top = jnp.where(left, even, pltpu.roll(odd, 64, 1))
    inverse = jnp.where(left, pltpu.roll(even, 64, 1), odd)
    delta = jnp.where(
        left, reply_ref[group, 0:8, 128:256], pltpu.roll(reply_ref[group, 8:16, 128:256], 64, 1)
    )
    for p in range(width // 128):
        cols = slice(128 * p, 128 * p + 128)
        value_cols = slice(width + 128 * p, width + 128 * p + 128)
        q = spread(q_ref[:, cols], low, high)
        d = spread(d_ref[:, cols], low, high)
        k = pairs_ref[:, cols]
        v = pairs_ref[:, value_cols]
        s = lax.dot_general(k, q, LAST, preferred_element_type=f32) * scale
        dw = lax.dot_general(v, d, LAST, preferred_element_type=f32)
        weights = jnp.where(usable, jnp.exp(s - top[p : p + 1]) * inverse[p : p + 1], 0.0)
        weights_b = weights.astype(bf16)
        d_scores = (weights * (dw - delta[p : p + 1]) * scale).astype(bf16)
        d_pairs_ref[1 - core[0], :, cols] = jnp.dot(
            weights_b, d, preferred_element_type=f32
        ).astype(bf16)
        d_pairs_ref[core[0], :, cols] = jnp.dot(d_scores, q, preferred_element_type=f32).astype(bf16)
        mixed = lax.dot_general(weights_b, v, FIRST, preferred_element_type=f32)
        mixed_acc[slot, :, cols] += jnp.where(wide, mixed[:rows], mixed[rows:])
        query = lax.dot_general(d_scores, k, FIRST, preferred_element_type=f32)
        query_acc[slot, :, cols] += jnp.where(wide, query[:rows], query[rows:])

    @pl.when(block == 3)
    def _():
        for at in range(SLOTS):
            for p in range(width // 128):
                cols = slice(128 * p, 128 * p + 128)
                mixed = mixed_acc[at, :, cols]
                query = query_acc[at, :, cols]
                slotted_ref[2 * p, at] = jnp.where(
                    wide, mixed, pltpu.roll(query, 64, 1)
                ).astype(bf16)
                slotted_ref[2 * p + 1, at] = jnp.where(
                    wide, pltpu.roll(mixed, 64, 1), query
                ).astype(bf16)


def gradients(counts, groups, core, queries, d_mixed, pairs, reply):
    width = queries.shape[1]
    rows = queries.shape[0] // 4
    return pl.pallas_call(
        grads_kernel,
        grid=(4,),
        out_shape=(
            jax.ShapeDtypeStruct((2, pairs.shape[0], width), bf16),
            jax.ShapeDtypeStruct((H, SLOTS, rows, 128), bf16),
        ),
        in_specs=[SMEM, SMEM, SMEM]
        + block_specs(rows, width)
        + [pl.BlockSpec((8, 16, 256), lambda i: (0, 0, 0))],
        out_specs=(
            pl.BlockSpec((2, 128, width), lambda i: (0, i, 0)),
            pl.BlockSpec((H, SLOTS, rows, 128), lambda i: (0, 0, 0, 0)),
        ),
        scratch_shapes=[pltpu.VMEM((SLOTS, rows, width), f32)] * 2,
        cost_estimate=pl.CostEstimate(
            flops=8 * 1024 * 1024 * 1024, bytes_accessed=8 * 1024 * 1024, transcendentals=512 * 1024
        ),
    )(counts, groups, core, queries, d_mixed, pairs, reply)


def local(latents, frames, counts, groups, w_query, w_kv, w_out, d_out):
    blocks, block_rows, feature = frames.shape
    latent_count, model_width = latents.shape[1:]
    head_dim = model_width // H
    group_count, seq_count = 8, 16
    rows = blocks * block_rows
    core = lax.axis_index("core")
    batch_at = lax.axis_index(BATCH)

    latents_all = gather_batch(latents[0])
    d_out_all = gather_batch(d_out[0])
    normed = normalize(frames).reshape(rows, feature)
    pairs = jnp.dot(normed, w_kv, preferred_element_type=f32).astype(bf16)
    places = place_of(groups)
    queries = project(places, latents_all, w_query, True, False)
    d_mixed = project(places, d_out_all, w_out, False, True)
    stats = statistics(counts, groups, queries, d_mixed, pairs)
    normed, stats = lax.optimization_barrier((normed, stats))
    normed_both = jnp.concatenate([normed, other_core(normed)], axis=0)
    stats = exchange(stats.reshape(128, 256), ALL)
    source_groups = lax.dynamic_slice(
        stats, (batch_at * seq_count, 192), (seq_count, SLOTS)
    )
    reply = exchange(totals(stats), ALL).reshape(group_count, seq_count, 256)
    d_pairs, slotted = gradients(
        counts, groups, core.reshape(1), queries, d_mixed, pairs, reply
    )

    d_half = jnp.concatenate([d_pairs[0], other_core(d_pairs[1])], axis=0)
    term = lax.dot_general(normed_both, d_half, FIRST, preferred_element_type=f32).astype(bf16)
    share_rows = feature // 128
    term = term.reshape(4, 2, seq_count, share_rows, 8, 128).transpose(0, 2, 1, 3, 4, 5)
    term = exchange(term.reshape(64, 2 * share_rows, 8, 128), CHIPS)
    chip_sum = jnp.sum(term.astype(f32), axis=0).reshape(2, share_rows, model_width)
    kept_sum = lax.dynamic_index_in_dim(chip_sum, core, 0, False)
    got_sum = other_core(lax.dynamic_index_in_dim(chip_sum, 1 - core, 0, False))
    grad_kv = jnp.where(
        core == 0,
        jnp.concatenate([kept_sum, got_sum], axis=1),
        jnp.concatenate([got_sum, kept_sum], axis=1),
    )

    slotted = exchange(slotted, SEQ)
    chosen = (
        jnp.arange(group_count, dtype=f32)[:, None, None] == source_groups[None]
    ).astype(bf16)
    by_group = jnp.einsum("gsk,sklc->glc", chosen, slotted, preferred_element_type=f32)
    owned = jnp.sum(exchange(by_group, BATCH), axis=0).astype(bf16)
    over_batch = share(owned, BATCH, group_count)
    over_batch = jnp.concatenate(
        [lax.dynamic_index_in_dim(over_batch, group_at(j), 0, False) for j in range(8)], axis=0
    )
    normed_latents = normalize(jnp.concatenate(latents_all, axis=0))
    query_cols = lax.dot_general(
        normed_latents, over_batch[:, head_dim:], FIRST, preferred_element_type=f32
    )
    query_high = query_cols.astype(bf16)
    query_low = (query_cols - query_high.astype(f32)).astype(bf16)
    query_cols = jnp.concatenate([query_high, query_low], axis=1)
    grad_outproj = lax.dot_general(
        over_batch[:, :head_dim],
        jnp.concatenate(d_out_all, axis=0),
        FIRST,
        preferred_element_type=f32,
    )
    over_seq = exchange(
        jnp.stack(
            [
                jnp.broadcast_to(owned[None], (seq_count,) + owned.shape),
                query_cols.reshape(seq_count, head_dim, 128),
            ],
            axis=1,
        ),
        SEQ,
    )

    def joined(part):
        return part.transpose(1, 0, 2).reshape(part.shape[1], model_width)

    mixed_b = joined(over_seq[:, 0, :, :head_dim])
    d_query = joined(over_seq[:, 0, :, head_dim:])
    grad_query = joined(
        over_seq[:, 1, :, :head_dim].astype(f32) + over_seq[:, 1, :, head_dim:].astype(f32)
    )
    latent = latents[0].astype(f32)
    cotangent = d_out[0]
    out = (latent + jnp.dot(mixed_b, w_out, preferred_element_type=f32)).astype(bf16)
    d_normed = lax.dot_general(d_query, w_query, LAST, preferred_element_type=f32)
    d_latents = (cotangent.astype(f32) + rms_back(latent, d_normed)).astype(bf16)
    return (out[None], d_latents[None], grad_query, grad_outproj, grad_kv)


def solution(mesh):
    chips = Mesh(mesh.devices.reshape(4, 2, 4, 4), ("x", "core", "z", "y"))
    in_specs = (
        P(BATCH, None, None),
        P(ALL, None, None),
        P(ALL),
        P(ALL),
        P(),
        P(),
        P(),
        P(BATCH, None, None),
    )
    out_specs = (
        P(BATCH, None, None),
        P(BATCH, None, None),
        P(SEQ, None),
        P(SEQ, None),
        P(ALL, None),
    )
    return jax.shard_map(local, mesh=chips, in_specs=in_specs, out_specs=out_specs, check_vma=False)
```

```python
import functools

import jax
import jax.numpy as jnp
from jax import lax
from jax.experimental import pallas as pl
from jax.experimental.pallas import tpu as pltpu
from jax.sharding import Mesh, PartitionSpec as P

H = 16
BATCH = ("x", "core")
SEQ = ("z", "y")
CHIPS = ("x", "z", "y")
ALL = BATCH + SEQ
SLOTS = 3

epsilon = 1e-06
f32 = jnp.float32
bf16 = jnp.bfloat16


def rms_rows(values):
    return values * lax.rsqrt(jnp.mean(values * values, axis=-1, keepdims=True) + epsilon)


def rms_back(values, grads):
    factor = lax.rsqrt(jnp.mean(values * values, axis=-1, keepdims=True) + epsilon)
    normed = values * factor
    return factor * (grads - normed * jnp.mean(grads * normed, axis=-1, keepdims=True))


def normalize(values):
    return rms_rows(values.astype(f32)).astype(bf16)


def exchange(values, axes):
    return lax.all_to_all(values, axes, 0, 0, tiled=True)


def share(values, axes, count):
    return exchange(jnp.broadcast_to(values[None], (count,) + values.shape), axes)


def other_core(values):
    return lax.ppermute(values, "core", [(0, 1), (1, 0)])


def ring_step(values, axis, step):
    return lax.ppermute(values, axis, [(i, (i + step) % 4) for i in range(4)])


def chip_step(values, step):
    return ring_step(values, "x", step)


def gather_batch(values):
    near = [values, chip_step(values, 1), chip_step(values, 2), chip_step(values, 3)]
    return near + [other_core(piece) for piece in near]


def place_of(group):
    chip = lax.rem(lax.axis_index("x") - group // 2 + 4, 4)
    return jnp.where(group % 2 == lax.axis_index("core"), 0, 4) + chip


def group_at(place):
    chip = lax.rem(lax.axis_index("x") - place % 4 + 4, 4)
    core = lax.axis_index("core")
    return 2 * chip + (core if place < 4 else 1 - core)


SMEM = pl.BlockSpec(memory_space=pltpu.SMEM)
VMEM = pl.BlockSpec(memory_space=pltpu.VMEM)
LAST = (((1,), (1,)), ((), ()))
FIRST = (((0,), (0,)), ((), ()))


def project_kernel(norm, transposed, places, *refs):
    pieces, (w_ref, out_ref, picked) = refs[:8], refs[8:]
    rows = pieces[0].shape[0]
    for i in range(out_ref.shape[0] // rows):
        for j in range(8):

            @pl.when(places[i] == j)
            def _():
                picked[i * rows : (i + 1) * rows, :] = pieces[j][...]

    if norm:
        picked[...] = normalize(picked[...])
    for at in range(0, out_ref.shape[1], 256):
        tile = slice(at, at + 256)
        if transposed:
            part = lax.dot_general(picked[...], w_ref[tile, :], LAST, preferred_element_type=f32)
        else:
            part = jnp.dot(picked[...], w_ref[:, tile], preferred_element_type=f32)
        out_ref[:, tile] = part.astype(bf16)


def project(places, pieces, weight, norm, transposed):
    rows, width = pieces[0].shape
    out = jax.ShapeDtypeStruct((places.shape[0] * rows, weight.shape[0]), bf16)
    return pl.pallas_call(
        functools.partial(project_kernel, norm, transposed),
        out_shape=out,
        in_specs=[SMEM] + [VMEM] * 9,
        out_specs=VMEM,
        scratch_shapes=[pltpu.VMEM((out.shape[0], width), bf16)],
        cost_estimate=pl.CostEstimate(
            flops=2 * out.shape[0] * width * weight.shape[0],
            bytes_accessed=4 * 1024 * 1024,
            transcendentals=0,
        ),
    )(places, *pieces, weight)


def pairs_kernel(frames_ref, w_ref, normed_ref, out_ref):
    @pl.when(pl.program_id(0) == 0)
    def _():
        normed_ref[...] = normalize(frames_ref[...])

    out_ref[...] = jnp.dot(normed_ref[...], w_ref[...], preferred_element_type=f32).astype(bf16)


def project_pairs(frames, w_kv):
    rows, feature = frames.shape
    width, tile = w_kv.shape[1], 256
    return pl.pallas_call(
        pairs_kernel,
        grid=(width // tile,),
        out_shape=(
            jax.ShapeDtypeStruct((rows, feature), bf16),
            jax.ShapeDtypeStruct((rows, width), bf16),
        ),
        in_specs=[
            pl.BlockSpec((rows, feature), lambda i: (0, 0)),
            pl.BlockSpec((feature, tile), lambda i: (0, i)),
        ],
        out_specs=(
            pl.BlockSpec((rows, feature), lambda i: (0, 0)),
            pl.BlockSpec((rows, tile), lambda i: (0, i)),
        ),
        cost_estimate=pl.CostEstimate(
            flops=2 * rows * feature * width, bytes_accessed=9 * 1024 * 1024, transcendentals=0
        ),
    )(frames, w_kv)


def low_lanes(shape):
    return lax.broadcasted_iota(jnp.int32, shape, len(shape) - 1) < 64


def spread(pair, low, high):
    return jnp.concatenate([pair * low, pair * high], axis=0)


def half_masks():
    lane = low_lanes((1, 128))
    return jnp.where(lane, 1.0, 0.0).astype(bf16), jnp.where(lane, 0.0, 1.0).astype(bf16)


def slots_of(groups):
    slots, used = [0], 1
    for i in range(1, 4):
        slot = used
        fresh = True
        for j in reversed(range(i)):
            slot = jnp.where(groups[i] == groups[j], slots[j], slot)
            fresh = fresh & (groups[i] != groups[j])
        slots.append(slot)
        used = used + jnp.where(fresh, 1, 0)
    return slots


def stats_kernel(counts, groups, q_ref, d_ref, pairs_ref, out_ref, top_ref, total_ref, moment_ref):
    block = pl.program_id(0)
    low, high = half_masks()
    width = q_ref.shape[1]
    scale = (width // H) ** (-0.5)
    usable = lax.broadcasted_iota(jnp.int32, (128, 128), 0) < counts[block]
    for p in range(width // 128):
        cols = slice(128 * p, 128 * p + 128)
        value_cols = slice(width + 128 * p, width + 128 * p + 128)
        s = lax.dot_general(
            pairs_ref[:, cols], spread(q_ref[:, cols], low, high), LAST, preferred_element_type=f32
        )
        s = jnp.where(usable, s * scale, -1e30)
        top = jnp.max(s, axis=0, keepdims=True)
        raw = jnp.where(usable, jnp.exp(s - top), 0.0)
        dw = lax.dot_general(
            pairs_ref[:, value_cols],
            spread(d_ref[:, cols], low, high),
            LAST,
            preferred_element_type=f32,
        )
        top_ref[block, p : p + 1, :] = top
        total_ref[block, p : p + 1, :] = jnp.sum(raw, axis=0, keepdims=True)
        moment_ref[block, p : p + 1, :] = jnp.sum(raw * dw, axis=0, keepdims=True)

    @pl.when(block == 3)
    def _():
        own = [groups[i] for i in range(4)]
        slots = slots_of(own)
        left = low_lanes((8, 128))
        lane = lax.broadcasted_iota(jnp.int32, (8, 128), 1)
        note = jnp.full((8, 128), -1.0, f32)
        for i in range(4):
            note = jnp.where(lane == 64 + slots[i], own[i].astype(f32), note)
        for g in range(8):
            tops = [jnp.where(own[i] == g, top_ref[i], -1e30) for i in range(4)]
            top = functools.reduce(jnp.maximum, tops)
            total = jnp.zeros((8, 128), f32)
            moment = jnp.zeros((8, 128), f32)
            for i in range(4):
                factor = jnp.where(own[i] == g, jnp.exp(tops[i] - top), 0.0)
                total = total + factor * total_ref[i]
                moment = moment + factor * moment_ref[i]
            parts = (
                (jnp.where(left, top, pltpu.roll(total, 64, 1)), jnp.where(left, moment, note)),
                (
                    jnp.where(left, pltpu.roll(top, 64, 1), total),
                    jnp.where(left, pltpu.roll(moment, 64, 1), note),
                ),
            )
            for odd in range(2):
                for p in range(8):
                    at = 16 * g + 8 * odd + p
                    out_ref[at, :, 0:128] = parts[odd][0][p : p + 1]
                    out_ref[at, :, 128:256] = parts[odd][1][p : p + 1]


def block_specs(latent_count, width):
    return [
        pl.BlockSpec((latent_count, width), lambda i: (i, 0)),
        pl.BlockSpec((latent_count, width), lambda i: (i, 0)),
        pl.BlockSpec((128, 2 * width), lambda i: (i, 0)),
    ]


def statistics(counts, groups, queries, d_mixed, pairs):
    width = queries.shape[1]
    return pl.pallas_call(
        stats_kernel,
        grid=(4,),
        out_shape=jax.ShapeDtypeStruct((128, 1, 256), f32),
        in_specs=[SMEM, SMEM] + block_specs(queries.shape[0] // 4, width),
        out_specs=pl.BlockSpec((128, 1, 256), lambda i: (0, 0, 0)),
        scratch_shapes=[pltpu.VMEM((4, 8, 128), f32)] * 3,
        cost_estimate=pl.CostEstimate(
            flops=4 * 1024 * 1024 * 1024, bytes_accessed=4 * 1024 * 1024, transcendentals=512 * 1024
        ),
    )(counts, groups, queries, d_mixed, pairs)


def totals_kernel(in_ref, out_ref):
    left = low_lanes((1, 128))
    first = in_ref[:, 0, 0:128]
    top = jnp.max(first, axis=0, keepdims=True)
    top = jnp.where(left, top, pltpu.roll(top, 64, 1))
    factor = jnp.exp(jnp.where(left, first, pltpu.roll(first, 64, 1)) - top)
    total = jnp.sum(factor * first, axis=0, keepdims=True)
    inverse = 1.0 / jnp.where(left, pltpu.roll(total, 64, 1), total)
    delta = jnp.sum(factor * in_ref[:, 0, 128:256], axis=0, keepdims=True) * inverse
    reply = jnp.concatenate(
        [jnp.where(left, top, inverse), jnp.where(left, delta, 0.0)], axis=1
    )
    for at in range(in_ref.shape[0]):
        out_ref[at] = reply


def totals(stats):
    return pl.pallas_call(
        totals_kernel,
        out_shape=jax.ShapeDtypeStruct(stats.shape, f32),
        in_specs=[VMEM],
        out_specs=VMEM,
    )(stats)


def grads_kernel(
    counts,
    groups,
    core,
    q_ref,
    d_ref,
    pairs_ref,
    reply_ref,
    kept_ref,
    sent_ref,
    slotted_ref,
    mixed_acc,
    query_acc,
    mixed_now,
    query_now,
):
    block = pl.program_id(0)
    low, high = half_masks()
    rows, width = q_ref.shape
    scale = (width // H) ** (-0.5)
    usable = lax.broadcasted_iota(jnp.int32, (128, 128), 0) < counts[block]
    left = low_lanes((8, 128))
    wide = low_lanes((rows, 128))

    @pl.when(block == 0)
    def _():
        mixed_acc[...] = jnp.zeros_like(mixed_acc)
        query_acc[...] = jnp.zeros_like(query_acc)

    slots = slots_of([groups[i] for i in range(4)])
    slot = slots[0]
    for i in range(1, 4):
        slot = jnp.where(block == i, slots[i], slot)
    group = groups[block]
    def reply_rows(odd, cols):
        first = 16 * group + 8 * odd
        return jnp.concatenate([reply_ref[first + p, :, cols] for p in range(8)], axis=0)

    even = reply_rows(0, slice(0, 128))
    odd = reply_rows(1, slice(0, 128))
    top = jnp.where(left, even, pltpu.roll(odd, 64, 1))
    inverse = jnp.where(left, pltpu.roll(even, 64, 1), odd)
    delta = jnp.where(
        left, reply_rows(0, slice(128, 256)), pltpu.roll(reply_rows(1, slice(128, 256)), 64, 1)
    )
    for p in range(width // 128):
        cols = slice(128 * p, 128 * p + 128)
        value_cols = slice(width + 128 * p, width + 128 * p + 128)
        q = spread(q_ref[:, cols], low, high)
        d = spread(d_ref[:, cols], low, high)
        k = pairs_ref[:, cols]
        v = pairs_ref[:, value_cols]
        s = lax.dot_general(k, q, LAST, preferred_element_type=f32) * scale
        dw = lax.dot_general(v, d, LAST, preferred_element_type=f32)
        weights = jnp.where(usable, jnp.exp(s - top[p : p + 1]) * inverse[p : p + 1], 0.0)
        weights_b = weights.astype(bf16)
        d_scores = (weights * (dw - delta[p : p + 1]) * scale).astype(bf16)
        d_values = jnp.dot(weights_b, d, preferred_element_type=f32)
        d_keys = jnp.dot(d_scores, q, preferred_element_type=f32)
        kept_ref[:, cols] = jnp.where(core[0] == 0, d_keys, d_values).astype(bf16)
        sent_ref[:, cols] = jnp.where(core[0] == 0, d_values, d_keys).astype(bf16)
        mixed = lax.dot_general(weights_b, v, FIRST, preferred_element_type=f32)
        mixed_now[:, cols] = jnp.where(wide, mixed[:rows], mixed[rows:])
        query = lax.dot_general(d_scores, k, FIRST, preferred_element_type=f32)
        query_now[:, cols] = jnp.where(wide, query[:rows], query[rows:])
    mixed_acc[slot] += mixed_now[...]
    query_acc[slot] += query_now[...]

    @pl.when(block == 3)
    def _():
        for at in range(SLOTS):
            for p in range(width // 128):
                cols = slice(128 * p, 128 * p + 128)
                mixed = mixed_acc[at, :, cols]
                query = query_acc[at, :, cols]
                slotted_ref[2 * p, at] = jnp.where(
                    wide, mixed, pltpu.roll(query, 64, 1)
                ).astype(bf16)
                slotted_ref[2 * p + 1, at] = jnp.where(
                    wide, pltpu.roll(mixed, 64, 1), query
                ).astype(bf16)


def gradients(counts, groups, core, queries, d_mixed, pairs, reply):
    width = queries.shape[1]
    rows = queries.shape[0] // 4
    return pl.pallas_call(
        grads_kernel,
        grid=(4,),
        out_shape=(
            jax.ShapeDtypeStruct((pairs.shape[0], width), bf16),
            jax.ShapeDtypeStruct((pairs.shape[0], width), bf16),
            jax.ShapeDtypeStruct((H, SLOTS, rows, 128), bf16),
        ),
        in_specs=[SMEM, SMEM, SMEM]
        + block_specs(rows, width)
        + [pl.BlockSpec((128, 1, 256), lambda i: (0, 0, 0))],
        out_specs=(
            pl.BlockSpec((128, width), lambda i: (i, 0)),
            pl.BlockSpec((128, width), lambda i: (i, 0)),
            pl.BlockSpec((H, SLOTS, rows, 128), lambda i: (0, 0, 0, 0)),
        ),
        scratch_shapes=[pltpu.VMEM((SLOTS, rows, width), f32)] * 2
        + [pltpu.VMEM((rows, width), f32)] * 2,
        cost_estimate=pl.CostEstimate(
            flops=8 * 1024 * 1024 * 1024, bytes_accessed=8 * 1024 * 1024, transcendentals=512 * 1024
        ),
    )(counts, groups, core, queries, d_mixed, pairs, reply)


def prepare_kernel(owners, *refs):
    latents, d_outs, (latents_ref, d_out_ref) = refs[:8], refs[8:16], refs[16:]
    rows = latents[0].shape[0]
    for j in range(8):
        at = pl.ds(pl.multiple_of(owners[j] * rows, rows), rows)
        latents_ref[at, :] = normalize(latents[j][...])
        d_out_ref[at, :] = d_outs[j][...]


def prepare(owners, latents, d_outs):
    rows, width = latents[0].shape
    out = jax.ShapeDtypeStruct((8 * rows, width), bf16)
    return pl.pallas_call(
        prepare_kernel,
        out_shape=(out, out),
        in_specs=[SMEM] + [VMEM] * 16,
        out_specs=(VMEM, VMEM),
        cost_estimate=pl.CostEstimate(
            flops=4 * 1024 * 1024, bytes_accessed=4 * 1024 * 1024, transcendentals=512
        ),
    )(owners, *latents, *d_outs)


def by_group_kernel(source_groups, in_ref, out_ref):
    out_ref[...] = jnp.zeros_like(out_ref)
    for source in range(in_ref.shape[0]):
        for slot in range(SLOTS):
            group = source_groups[source * SLOTS + slot]

            @pl.when(group >= 0)
            def _():
                out_ref[group] += in_ref[source, slot].astype(f32)


def by_group(source_groups, slotted):
    return pl.pallas_call(
        by_group_kernel,
        out_shape=jax.ShapeDtypeStruct((8,) + slotted.shape[2:], f32),
        in_specs=[SMEM, VMEM],
        out_specs=VMEM,
    )(source_groups, slotted)


def owners_kernel(heads_ref, owned_ref, latents_ref, d_out_ref, outproj_ref, out_ref):
    rows = outproj_ref.shape[0]
    heads = heads_ref[...]
    outproj_ref[...] = lax.dot_general(
        heads, d_out_ref[...], FIRST, preferred_element_type=f32
    )[:rows]
    query = lax.dot_general(latents_ref[...], heads, FIRST, preferred_element_type=f32)
    high = query.astype(bf16).astype(f32)
    query = jnp.where(low_lanes(query.shape), pltpu.roll(high, 64, 1), query - high).astype(bf16)
    for at in range(H):
        out_ref[at, :rows] = owned_ref[...]
        out_ref[at, rows:] = query[rows * at : rows * at + rows]


def owners(heads, owned, normed_latents, d_outs):
    rows = owned.shape[0]
    width = d_outs.shape[1]
    return pl.pallas_call(
        owners_kernel,
        out_shape=(
            jax.ShapeDtypeStruct((rows, width), f32),
            jax.ShapeDtypeStruct((H, 2 * rows, 128), bf16),
        ),
        in_specs=[VMEM] * 4,
        out_specs=(VMEM, VMEM),
        cost_estimate=pl.CostEstimate(
            flops=512 * 1024 * 1024, bytes_accessed=4 * 1024 * 1024, transcendentals=0
        ),
    )(heads, owned, normed_latents, d_outs)


def finish_kernel(in_ref, latent_ref, d_out_ref, w_query_ref, w_out_ref, *refs):
    out_ref, d_latents_ref, grad_query_ref, mixed, d_query = refs
    rows = latent_ref.shape[0]
    left = low_lanes((rows, 128))

    def parts(head):
        both = in_ref[head, rows : 2 * rows].astype(f32)
        return in_ref[head, :rows].astype(f32), both + pltpu.roll(both, 64, 1)

    for p in range(H // 2):
        cols = slice(128 * p, 128 * p + 128)
        even, even_grad = parts(2 * p)
        odd, odd_grad = parts(2 * p + 1)
        mixed[:, cols] = jnp.where(left, even, pltpu.roll(odd, 64, 1)).astype(bf16)
        d_query[:, cols] = jnp.where(left, pltpu.roll(even, 64, 1), odd).astype(bf16)
        grad_query_ref[:, cols] = jnp.where(left, even_grad, odd_grad)
    latent = latent_ref[...].astype(f32)
    update = jnp.dot(mixed[...], w_out_ref[...], preferred_element_type=f32)
    out_ref[...] = (latent + update).astype(bf16)
    d_normed = lax.dot_general(d_query[...], w_query_ref[...], LAST, preferred_element_type=f32)
    d_latents_ref[...] = (d_out_ref[...].astype(f32) + rms_back(latent, d_normed)).astype(bf16)


def finish(over_seq, latent, d_out, w_query, w_out):
    rows, width = latent.shape
    small = jax.ShapeDtypeStruct((rows, width), bf16)
    return pl.pallas_call(
        finish_kernel,
        out_shape=(small, small, jax.ShapeDtypeStruct((rows, width), f32)),
        in_specs=[VMEM] * 5,
        out_specs=(VMEM,) * 3,
        scratch_shapes=[pltpu.VMEM((rows, width), bf16)] * 2,
    )(over_seq, latent, d_out, w_query, w_out)


def local(latents, frames, counts, groups, w_query, w_kv, w_out, d_out):
    blocks, block_rows, feature = frames.shape
    latent_count, model_width = latents.shape[1:]
    head_dim = model_width // H
    group_count, seq_count = 8, 16
    rows = blocks * block_rows
    core = lax.axis_index("core")
    batch_at = lax.axis_index(BATCH)

    latents_all = gather_batch(latents[0])
    d_out_all = gather_batch(d_out[0])
    normed, pairs = project_pairs(frames.reshape(rows, feature), w_kv)
    places = place_of(groups)
    queries = project(places, latents_all, w_query, True, False)
    d_mixed = project(places, d_out_all, w_out, False, True)
    stats = statistics(counts, groups, queries, d_mixed, pairs)
    normed, stats = lax.optimization_barrier((normed, stats))
    normed_both = jnp.concatenate([normed, other_core(normed)], axis=0)
    stats = exchange(stats, ALL)
    source_groups = lax.dynamic_slice(
        stats, (batch_at * seq_count, 0, 192), (seq_count, 1, SLOTS)
    ).reshape(seq_count * SLOTS).astype(jnp.int32)
    all_latents, all_d_out = prepare(
        jnp.stack([group_at(j) for j in range(8)]), latents_all, d_out_all
    )
    reply, all_latents, all_d_out, normed_both = lax.optimization_barrier(
        (totals(stats), all_latents, all_d_out, normed_both)
    )
    reply = exchange(reply, ALL)
    kept, sent, slotted = gradients(
        counts, groups, core.reshape(1), queries, d_mixed, pairs, reply
    )
    slotted = exchange(slotted, SEQ)

    d_half = jnp.concatenate([kept, other_core(sent)], axis=0)
    term = lax.dot_general(normed_both, d_half, FIRST, preferred_element_type=f32).astype(bf16)
    share_rows = feature // 128
    term = term.reshape(group_count, 4, 4 * share_rows, 8, 128)
    z_at = lax.axis_index("z")

    def z_part(step):
        return lax.dynamic_index_in_dim(term, lax.rem(z_at + step, 4), 1, False)

    ring_sum = z_part(0).astype(f32)
    for step in range(1, 4):
        ring_sum = ring_sum + ring_step(z_part(step), "z", step).astype(f32)
    ring_sum = ring_sum.astype(bf16).reshape(4, 2, 4, share_rows, 8, 128)
    ring_sum = ring_sum.transpose(0, 2, 1, 3, 4, 5).reshape(16, 2 * share_rows, 8, 128)
    ring_sum = exchange(ring_sum, ("x", "y"))

    owned = jnp.sum(exchange(by_group(source_groups, slotted), BATCH), axis=0).astype(bf16)
    heads = share(owned, BATCH, group_count).reshape(group_count * latent_count, 128)
    grad_outproj, owned_parts = owners(heads, owned, all_latents, all_d_out)
    over_seq = exchange(owned_parts, SEQ)

    chip_sum = jnp.sum(ring_sum.astype(f32), axis=0).reshape(2, share_rows, model_width)
    kept_sum = lax.dynamic_index_in_dim(chip_sum, core, 0, False)
    got_sum = other_core(lax.dynamic_index_in_dim(chip_sum, 1 - core, 0, False))
    grad_kv = jnp.where(
        core == 0,
        jnp.concatenate([kept_sum, got_sum], axis=1),
        jnp.concatenate([got_sum, kept_sum], axis=1),
    )
    out, d_latents, grad_query = finish(over_seq, latents[0], d_out[0], w_query, w_out)
    return (out[None], d_latents[None], grad_query, grad_outproj, grad_kv)


def solution(mesh):
    chips = Mesh(mesh.devices.reshape(4, 2, 4, 4), ("x", "core", "z", "y"))
    in_specs = (
        P(BATCH, None, None),
        P(ALL, None, None),
        P(ALL),
        P(ALL),
        P(),
        P(),
        P(),
        P(BATCH, None, None),
    )
    out_specs = (
        P(BATCH, None, None),
        P(BATCH, None, None),
        P(SEQ, None),
        P(SEQ, None),
        P(ALL, None),
    )
    return jax.shard_map(local, mesh=chips, in_specs=in_specs, out_specs=out_specs, check_vma=False)
```

```python
import functools

import jax
import jax.numpy as jnp
from jax import lax
from jax.experimental import pallas as pl
from jax.experimental.pallas import tpu as pltpu
from jax.sharding import Mesh, PartitionSpec as P

H = 16
BATCH = ("x", "core")
SEQ = ("z", "y")
CHIPS = ("x", "z", "y")
ALL = BATCH + SEQ
SLOTS = 3
WIDE = 256

epsilon = 1e-06
f32 = jnp.float32
bf16 = jnp.bfloat16


def rms_rows(values):
    return values * lax.rsqrt(jnp.mean(values * values, axis=-1, keepdims=True) + epsilon)


def rms_back(values, grads):
    factor = lax.rsqrt(jnp.mean(values * values, axis=-1, keepdims=True) + epsilon)
    normed = values * factor
    return factor * (grads - normed * jnp.mean(grads * normed, axis=-1, keepdims=True))


def normalize(values):
    return rms_rows(values.astype(f32)).astype(bf16)


def exchange(values, axes):
    return lax.all_to_all(values, axes, 0, 0, tiled=True)


def share(values, axes, count):
    return exchange(jnp.broadcast_to(values[None], (count,) + values.shape), axes)


def other_core(values):
    return lax.ppermute(values, "core", [(0, 1), (1, 0)])


def ring_step(values, axis, step):
    return lax.ppermute(values, axis, [(i, (i + step) % 4) for i in range(4)])


def chip_step(values, step):
    return ring_step(values, "x", step)


def along_chips(values):
    return [values, chip_step(values, 1), chip_step(values, 2), chip_step(values, 3)]


def place_of(group):
    chip = lax.rem(lax.axis_index("x") - group // 2 + 4, 4)
    return jnp.where(group % 2 == lax.axis_index("core"), 0, 4) + chip


def group_at(place):
    chip = lax.rem(lax.axis_index("x") - place % 4 + 4, 4)
    core = lax.axis_index("core")
    return 2 * chip + (core if place < 4 else 1 - core)


SMEM = pl.BlockSpec(memory_space=pltpu.SMEM)
VMEM = pl.BlockSpec(memory_space=pltpu.VMEM)
HBM = pl.BlockSpec(memory_space=pltpu.HBM)
LAST = (((1,), (1,)), ((), ()))
FIRST = (((0,), (0,)), ((), ()))


def room(mebibytes):
    return pltpu.CompilerParams(vmem_limit_bytes=mebibytes * 1024 * 1024)


def pairs_kernel(frames_ref, w_ref, normed_ref, out_ref):
    @pl.when(pl.program_id(0) == 0)
    def _():
        normed_ref[...] = normalize(frames_ref[...])

    out_ref[...] = jnp.dot(normed_ref[...], w_ref[...], preferred_element_type=f32).astype(bf16)


def project_pairs(frames, w_kv):
    rows, feature = frames.shape
    width, tile = w_kv.shape[1], 1024
    return pl.pallas_call(
        pairs_kernel,
        grid=(width // tile,),
        out_shape=(
            jax.ShapeDtypeStruct((rows, feature), bf16),
            jax.ShapeDtypeStruct((rows, width), bf16),
        ),
        in_specs=[
            pl.BlockSpec((rows, feature), lambda i: (0, 0)),
            pl.BlockSpec((feature, tile), lambda i: (0, i)),
        ],
        out_specs=(
            pl.BlockSpec((rows, feature), lambda i: (0, 0)),
            pl.BlockSpec((rows, tile), lambda i: (0, i)),
        ),
        cost_estimate=pl.CostEstimate(
            flops=2 * rows * feature * width, bytes_accessed=9 * 1024 * 1024, transcendentals=0
        ),
    )(frames, w_kv)


def low_lanes(shape):
    return lax.broadcasted_iota(jnp.int32, shape, len(shape) - 1) < 64


def spread(heads, masks):
    return jnp.concatenate([heads * mask for mask in masks], axis=0)


def head_masks():
    head = lax.broadcasted_iota(jnp.int32, (1, WIDE), 1) // 64
    return [jnp.where(head == at, 1.0, 0.0).astype(bf16) for at in range(WIDE // 64)]


def own_heads(product, rows):
    head = lax.broadcasted_iota(jnp.int32, (rows, WIDE), 1) // 64
    result = product[:rows]
    for at in range(1, WIDE // 64):
        result = jnp.where(head == at, product[at * rows : at * rows + rows], result)
    return result


def slots_of(groups):
    slots, used = [0], 1
    for i in range(1, 4):
        slot = used
        fresh = True
        for j in reversed(range(i)):
            slot = jnp.where(groups[i] == groups[j], slots[j], slot)
            fresh = fresh & (groups[i] != groups[j])
        slots.append(slot)
        used = used + jnp.where(fresh, 1, 0)
    return slots


def attend_kernel(counts, groups, places, *refs):
    pieces, (wq_in, wo_in, pairs_in, q_out, d_out, out_ref), scratch = refs[:8], refs[8:14], refs[14:]
    picked, wq, wo, pairs_ref, q_ref, d_ref, top_ref, total_ref, moment_ref, sems = scratch
    copies = [
        pltpu.make_async_copy(wq_in, wq, sems.at[0]),
        pltpu.make_async_copy(wo_in, wo, sems.at[1]),
        pltpu.make_async_copy(pairs_in, pairs_ref, sems.at[2]),
        pltpu.make_async_copy(q_ref, q_out, sems.at[3]),
        pltpu.make_async_copy(d_ref, d_out, sems.at[4]),
    ]
    for copy in copies[:3]:
        copy.start()
    rows, width = pieces[0].shape[1:]
    blocks = q_ref.shape[0] // rows
    for i in range(blocks):
        for j in range(8):

            @pl.when(places[i] == j)
            def _():
                picked[0, i * rows : (i + 1) * rows, :] = normalize(pieces[j][0])
                picked[1, i * rows : (i + 1) * rows, :] = pieces[j][1]

    copies[0].wait()
    for at in range(0, width, 256):
        tile = slice(at, at + 256)
        q_ref[:, tile] = jnp.dot(picked[0], wq[:, tile], preferred_element_type=f32).astype(bf16)
    copies[3].start()
    copies[1].wait()
    for at in range(0, width, 256):
        tile = slice(at, at + 256)
        d_ref[:, tile] = lax.dot_general(
            picked[1], wo[tile, :], LAST, preferred_element_type=f32
        ).astype(bf16)
    copies[4].start()
    copies[2].wait()

    masks = head_masks()
    scale = (width // H) ** (-0.5)
    position = lax.broadcasted_iota(jnp.int32, (128, WIDE), 0)

    def one_block(block, carry):
        usable = position < counts[block]
        here = pl.ds(pl.multiple_of(block * rows, rows), rows)
        there = pl.ds(pl.multiple_of(block * 128, 128), 128)
        for at in range(0, width, WIDE):
            cols = slice(at, at + WIDE)
            value_cols = slice(width + at, width + at + WIDE)
            s = lax.dot_general(
                pairs_ref[there, cols],
                spread(q_ref[here, cols], masks),
                LAST,
                preferred_element_type=f32,
            )
            s = jnp.where(usable, s * scale, -1e30)
            top = jnp.max(s, axis=0, keepdims=True)
            raw = jnp.where(usable, jnp.exp(s - top), 0.0)
            dw = lax.dot_general(
                pairs_ref[there, value_cols],
                spread(d_ref[here, cols], masks),
                LAST,
                preferred_element_type=f32,
            )
            total = jnp.sum(raw, axis=0, keepdims=True)
            moment = jnp.sum(raw * dw, axis=0, keepdims=True)
            for part in range(0, WIDE, 128):
                p = (at + part) // 128
                top_ref[block, p : p + 1, :] = top[:, part : part + 128]
                total_ref[block, p : p + 1, :] = total[:, part : part + 128]
                moment_ref[block, p : p + 1, :] = moment[:, part : part + 128]
        return carry

    lax.fori_loop(0, blocks, one_block, 0)
    own = [groups[i] for i in range(blocks)]
    slots = slots_of(own)
    left = low_lanes((8, 128))
    lane = lax.broadcasted_iota(jnp.int32, (8, 128), 1)
    note = jnp.full((8, 128), -1.0, f32)
    for i in range(blocks):
        note = jnp.where(lane == 64 + slots[i], own[i].astype(f32), note)
    for g in range(8):
        tops = [jnp.where(own[i] == g, top_ref[i], -1e30) for i in range(blocks)]
        top = functools.reduce(jnp.maximum, tops)
        total = jnp.zeros((8, 128), f32)
        moment = jnp.zeros((8, 128), f32)
        for i in range(blocks):
            factor = jnp.where(own[i] == g, jnp.exp(tops[i] - top), 0.0)
            total = total + factor * total_ref[i]
            moment = moment + factor * moment_ref[i]
        parts = (
            (jnp.where(left, top, pltpu.roll(total, 64, 1)), jnp.where(left, moment, note)),
            (
                jnp.where(left, pltpu.roll(top, 64, 1), total),
                jnp.where(left, pltpu.roll(moment, 64, 1), note),
            ),
        )
        for odd in range(2):
            for p in range(8):
                at = 16 * g + 8 * odd + p
                out_ref[at, :, 0:128] = parts[odd][0][p : p + 1]
                out_ref[at, :, 128:256] = parts[odd][1][p : p + 1]
    copies[3].wait()
    copies[4].wait()


def attend(counts, groups, places, pieces, w_query, w_out, pairs):
    rows, width = pieces[0].shape[1:]
    small = jax.ShapeDtypeStruct((groups.shape[0] * rows, width), bf16)
    return pl.pallas_call(
        attend_kernel,
        out_shape=(small, small, jax.ShapeDtypeStruct((128, 1, 256), f32)),
        in_specs=[SMEM] * 3 + [VMEM] * 8 + [HBM] * 3,
        out_specs=(HBM, HBM, VMEM),
        scratch_shapes=[
            pltpu.VMEM((2,) + small.shape, bf16),
            pltpu.VMEM(w_query.shape, bf16),
            pltpu.VMEM(w_out.shape, bf16),
            pltpu.VMEM(pairs.shape, bf16),
            pltpu.VMEM(small.shape, bf16),
            pltpu.VMEM(small.shape, bf16),
        ]
        + [pltpu.VMEM((groups.shape[0], 8, 128), f32)] * 3
        + [pltpu.SemaphoreType.DMA((5,))],
        cost_estimate=pl.CostEstimate(
            flops=6 * 1024 * 1024 * 1024,
            bytes_accessed=10 * 1024 * 1024,
            transcendentals=512 * 1024,
        ),
    )(counts, groups, places, *pieces, w_query, w_out, pairs)


def block_specs(latent_count, width):
    return [
        pl.BlockSpec((latent_count, width), lambda i: (i, 0)),
        pl.BlockSpec((latent_count, width), lambda i: (i, 0)),
        pl.BlockSpec((128, 2 * width), lambda i: (i, 0)),
    ]


def totals_kernel(in_ref, out_ref):
    left = low_lanes((1, 128))
    first = in_ref[:, 0, 0:128]
    top = jnp.max(first, axis=0, keepdims=True)
    top = jnp.where(left, top, pltpu.roll(top, 64, 1))
    factor = jnp.exp(jnp.where(left, first, pltpu.roll(first, 64, 1)) - top)
    total = jnp.sum(factor * first, axis=0, keepdims=True)
    inverse = 1.0 / jnp.where(left, pltpu.roll(total, 64, 1), total)
    delta = jnp.sum(factor * in_ref[:, 0, 128:256], axis=0, keepdims=True) * inverse
    reply = jnp.concatenate(
        [jnp.where(left, top, inverse), jnp.where(left, delta, 0.0)], axis=1
    )
    for at in range(in_ref.shape[0]):
        out_ref[at] = reply


def totals(stats):
    return pl.pallas_call(
        totals_kernel,
        out_shape=jax.ShapeDtypeStruct(stats.shape, f32),
        in_specs=[VMEM],
        out_specs=VMEM,
        compiler_params=room(4),
    )(stats)


def grads_kernel(
    counts,
    groups,
    core,
    q_ref,
    d_ref,
    pairs_ref,
    reply_ref,
    kept_ref,
    sent_ref,
    slotted_ref,
    mixed_acc,
    query_acc,
    mixed_now,
    query_now,
):
    block = pl.program_id(0)
    masks = head_masks()
    rows, width = q_ref.shape
    scale = (width // H) ** (-0.5)
    usable = lax.broadcasted_iota(jnp.int32, (128, WIDE), 0) < counts[block]
    left = low_lanes((8, 128))
    wide = low_lanes((rows, 128))

    @pl.when(block == 0)
    def _():
        mixed_acc[...] = jnp.zeros_like(mixed_acc)
        query_acc[...] = jnp.zeros_like(query_acc)

    slots = slots_of([groups[i] for i in range(4)])
    slot = slots[0]
    for i in range(1, 4):
        slot = jnp.where(block == i, slots[i], slot)
    group = groups[block]
    def reply_rows(odd, cols):
        first = 16 * group + 8 * odd
        return jnp.concatenate([reply_ref[first + p, :, cols] for p in range(8)], axis=0)

    def row(pairs, at):
        first = at // 128
        return jnp.concatenate([pairs[p : p + 1] for p in range(first, first + WIDE // 128)], axis=1)

    even = reply_rows(0, slice(0, 128))
    odd = reply_rows(1, slice(0, 128))
    top = jnp.where(left, even, pltpu.roll(odd, 64, 1))
    inverse = jnp.where(left, pltpu.roll(even, 64, 1), odd)
    delta = jnp.where(
        left, reply_rows(0, slice(128, 256)), pltpu.roll(reply_rows(1, slice(128, 256)), 64, 1)
    )
    for at in range(0, width, WIDE):
        cols = slice(at, at + WIDE)
        value_cols = slice(width + at, width + at + WIDE)
        q = spread(q_ref[:, cols], masks)
        d = spread(d_ref[:, cols], masks)
        k = pairs_ref[:, cols]
        v = pairs_ref[:, value_cols]
        s = lax.dot_general(k, q, LAST, preferred_element_type=f32) * scale
        dw = lax.dot_general(v, d, LAST, preferred_element_type=f32)
        weights = jnp.where(usable, jnp.exp(s - row(top, at)) * row(inverse, at), 0.0)
        weights_b = weights.astype(bf16)
        d_scores = (weights * (dw - row(delta, at)) * scale).astype(bf16)
        d_values = jnp.dot(weights_b, d, preferred_element_type=f32)
        d_keys = jnp.dot(d_scores, q, preferred_element_type=f32)
        kept_ref[:, cols] = jnp.where(core[0] == 0, d_keys, d_values).astype(bf16)
        sent_ref[:, cols] = jnp.where(core[0] == 0, d_values, d_keys).astype(bf16)
        mixed = lax.dot_general(weights_b, v, FIRST, preferred_element_type=f32)
        mixed_now[:, cols] = own_heads(mixed, rows)
        query = lax.dot_general(d_scores, k, FIRST, preferred_element_type=f32)
        query_now[:, cols] = own_heads(query, rows)
    mixed_acc[slot] += mixed_now[...]
    query_acc[slot] += query_now[...]

    @pl.when(block == 3)
    def _():
        for at in range(SLOTS):
            for p in range(width // 128):
                cols = slice(128 * p, 128 * p + 128)
                mixed = mixed_acc[at, :, cols]
                query = query_acc[at, :, cols]
                slotted_ref[2 * p, at] = jnp.where(
                    wide, mixed, pltpu.roll(query, 64, 1)
                ).astype(bf16)
                slotted_ref[2 * p + 1, at] = jnp.where(
                    wide, pltpu.roll(mixed, 64, 1), query
                ).astype(bf16)


def gradients(counts, groups, core, queries, d_mixed, pairs, reply):
    width = queries.shape[1]
    rows = queries.shape[0] // 4
    return pl.pallas_call(
        grads_kernel,
        grid=(4,),
        out_shape=(
            jax.ShapeDtypeStruct((pairs.shape[0], width), bf16),
            jax.ShapeDtypeStruct((pairs.shape[0], width), bf16),
            jax.ShapeDtypeStruct((H, SLOTS, rows, 128), bf16),
        ),
        in_specs=[SMEM, SMEM, SMEM]
        + block_specs(rows, width)
        + [pl.BlockSpec((128, 1, 256), lambda i: (0, 0, 0))],
        out_specs=(
            pl.BlockSpec((128, width), lambda i: (i, 0)),
            pl.BlockSpec((128, width), lambda i: (i, 0)),
            pl.BlockSpec((H, SLOTS, rows, 128), lambda i: (0, 0, 0, 0)),
        ),
        scratch_shapes=[pltpu.VMEM((SLOTS, rows, width), f32)] * 2
        + [pltpu.VMEM((rows, width), f32)] * 2,
        cost_estimate=pl.CostEstimate(
            flops=8 * 1024 * 1024 * 1024, bytes_accessed=8 * 1024 * 1024, transcendentals=512 * 1024
        ),
    )(counts, groups, core, queries, d_mixed, pairs, reply)


def prepare_kernel(owners, *refs):
    pieces, (latents_ref, d_out_ref) = refs[:8], refs[8:]
    rows = pieces[0].shape[1]
    for j in range(8):
        at = pl.ds(pl.multiple_of(owners[j] * rows, rows), rows)
        latents_ref[at, :] = normalize(pieces[j][0])
        d_out_ref[at, :] = pieces[j][1]


def prepare(owners, pieces):
    rows, width = pieces[0].shape[1:]
    out = jax.ShapeDtypeStruct((8 * rows, width), bf16)
    return pl.pallas_call(
        prepare_kernel,
        out_shape=(out, out),
        in_specs=[SMEM] + [VMEM] * 8,
        out_specs=(VMEM, VMEM),
        cost_estimate=pl.CostEstimate(
            flops=4 * 1024 * 1024, bytes_accessed=4 * 1024 * 1024, transcendentals=512
        ),
    )(owners, *pieces)


def owners_kernel(heads_ref, owned_ref, latents_ref, d_out_ref, outproj_ref, out_ref):
    rows = outproj_ref.shape[0]
    heads = heads_ref[...]
    outproj_ref[...] = lax.dot_general(
        heads, d_out_ref[...], FIRST, preferred_element_type=f32
    )[:rows]
    query = lax.dot_general(latents_ref[...], heads, FIRST, preferred_element_type=f32)
    high = query.astype(bf16).astype(f32)
    query = jnp.where(low_lanes(query.shape), pltpu.roll(high, 64, 1), query - high).astype(bf16)
    for at in range(H):
        out_ref[at, :rows] = owned_ref[...]
        out_ref[at, rows:] = query[rows * at : rows * at + rows]


def owners(heads, owned, normed_latents, d_outs):
    rows = owned.shape[0]
    width = d_outs.shape[1]
    return pl.pallas_call(
        owners_kernel,
        out_shape=(
            jax.ShapeDtypeStruct((rows, width), f32),
            jax.ShapeDtypeStruct((H, 2 * rows, 128), bf16),
        ),
        in_specs=[VMEM] * 4,
        out_specs=(VMEM, VMEM),
        cost_estimate=pl.CostEstimate(
            flops=512 * 1024 * 1024, bytes_accessed=4 * 1024 * 1024, transcendentals=0
        ),
    )(heads, owned, normed_latents, d_outs)


def finish_kernel(in_ref, latent_ref, d_out_ref, w_query_ref, w_out_in, *refs):
    out_ref, d_latents_ref, grad_query_ref, mixed, d_query, w_out_ref, sem = refs
    copy = pltpu.make_async_copy(w_out_in, w_out_ref, sem)
    copy.start()
    rows = latent_ref.shape[0]
    left = low_lanes((rows, 128))

    def parts(head):
        both = in_ref[head, rows : 2 * rows].astype(f32)
        return in_ref[head, :rows].astype(f32), both + pltpu.roll(both, 64, 1)

    for p in range(H // 2):
        cols = slice(128 * p, 128 * p + 128)
        even, even_grad = parts(2 * p)
        odd, odd_grad = parts(2 * p + 1)
        mixed[:, cols] = jnp.where(left, even, pltpu.roll(odd, 64, 1)).astype(bf16)
        d_query[:, cols] = jnp.where(left, pltpu.roll(even, 64, 1), odd).astype(bf16)
        grad_query_ref[:, cols] = jnp.where(left, even_grad, odd_grad)
    latent = latent_ref[...].astype(f32)
    d_normed = lax.dot_general(d_query[...], w_query_ref[...], LAST, preferred_element_type=f32)
    d_latents_ref[...] = (d_out_ref[...].astype(f32) + rms_back(latent, d_normed)).astype(bf16)
    copy.wait()
    update = jnp.dot(mixed[...], w_out_ref[...], preferred_element_type=f32)
    out_ref[...] = (latent + update).astype(bf16)


def finish(over_seq, latent, d_out, w_query, w_out):
    rows, width = latent.shape
    small = jax.ShapeDtypeStruct((rows, width), bf16)
    return pl.pallas_call(
        finish_kernel,
        out_shape=(small, small, jax.ShapeDtypeStruct((rows, width), f32)),
        in_specs=[VMEM] * 4 + [HBM],
        out_specs=(VMEM,) * 3,
        compiler_params=room(12),
        scratch_shapes=[pltpu.VMEM((rows, width), bf16)] * 2
        + [pltpu.VMEM(w_out.shape, bf16), pltpu.SemaphoreType.DMA],
    )(over_seq, latent, d_out, w_query, w_out)


def local(latents, frames, counts, groups, w_query, w_kv, w_out, d_out):
    blocks, block_rows, feature = frames.shape
    latent_count, model_width = latents.shape[1:]
    head_dim = model_width // H
    group_count, seq_count = 8, 16
    rows = blocks * block_rows
    core = lax.axis_index("core")
    batch_at = lax.axis_index(BATCH)

    near = along_chips(jnp.concatenate([latents, d_out], axis=0))
    normed, pairs = project_pairs(frames.reshape(rows, feature), w_kv)
    near, normed, pairs = lax.optimization_barrier((near, normed, pairs))
    pieces = near + [other_core(piece) for piece in near]
    queries, d_mixed, stats = attend(
        counts, groups, place_of(groups), pieces, w_query, w_out, pairs
    )
    sources = jnp.stack([group_at(j) for j in range(8)])
    normed, sources, stats = lax.optimization_barrier((normed, sources, stats))
    all_latents, all_d_out = prepare(sources, pieces)
    normed = jnp.concatenate([normed, other_core(normed)], axis=0)
    stats = exchange(stats, ALL)
    source_groups = lax.dynamic_slice(
        stats, (batch_at * seq_count, 0, 192), (seq_count, 1, SLOTS)
    )
    chosen = (
        jnp.arange(group_count, dtype=f32)[:, None, None] == source_groups.reshape(1, seq_count, SLOTS)
    ).astype(bf16)
    reply = exchange(totals(stats), ALL)
    reply, all_latents, all_d_out, normed, chosen = lax.optimization_barrier(
        (reply, all_latents, all_d_out, normed, chosen)
    )
    kept, sent, slotted = gradients(
        counts, groups, core.reshape(1), queries, d_mixed, pairs, reply
    )
    slotted = exchange(slotted, SEQ)

    d_half = jnp.concatenate([kept, other_core(sent)], axis=0)
    term = lax.dot_general(normed, d_half, FIRST, preferred_element_type=f32).astype(bf16)
    share_rows = feature // 128
    term = term.reshape(group_count, 4, 4 * share_rows, 8, 128)
    z_at = lax.axis_index("z")

    def z_part(step):
        return lax.dynamic_index_in_dim(term, lax.rem(z_at + step, 4), 1, False)

    got = [ring_step(z_part(step), "z", step) for step in range(1, 4)]
    by_group = jnp.einsum("gsk,sklc->glc", chosen, slotted, preferred_element_type=f32)
    owned = jnp.sum(exchange(by_group, BATCH), axis=0).astype(bf16)
    heads = share(owned, BATCH, group_count).reshape(group_count * latent_count, 128)
    heads, got = lax.optimization_barrier((heads, got))
    ring_sum = sum([part.astype(f32) for part in got], z_part(0).astype(f32))
    ring_sum = ring_sum.astype(bf16).reshape(4, 2, 4, share_rows, 8, 128)
    ring_sum = ring_sum.transpose(0, 2, 1, 3, 4, 5).reshape(16, 2 * share_rows, 8, 128)
    grad_outproj, owned_parts = owners(heads, owned, all_latents, all_d_out)
    over_seq = exchange(owned_parts, SEQ)
    ring_sum, over_seq = lax.optimization_barrier((ring_sum, over_seq))
    ring_sum = exchange(ring_sum, ("x", "y"))
    out, d_latents, grad_query = finish(over_seq, latents[0], d_out[0], w_query, w_out)
    ring_sum, out, d_latents, grad_query = lax.optimization_barrier(
        (ring_sum, out, d_latents, grad_query)
    )

    chip_sum = jnp.sum(ring_sum.astype(f32), axis=0).reshape(2, share_rows, model_width)
    kept_sum = lax.dynamic_index_in_dim(chip_sum, core, 0, False)
    got_sum = other_core(lax.dynamic_index_in_dim(chip_sum, 1 - core, 0, False))
    grad_kv = jnp.where(
        core == 0,
        jnp.concatenate([kept_sum, got_sum], axis=1),
        jnp.concatenate([got_sum, kept_sum], axis=1),
    )
    return (out[None], d_latents[None], grad_query, grad_outproj, grad_kv)


def solution(mesh):
    chips = Mesh(mesh.devices.reshape(4, 2, 4, 4), ("x", "core", "z", "y"))
    in_specs = (
        P(BATCH, None, None),
        P(ALL, None, None),
        P(ALL),
        P(ALL),
        P(),
        P(),
        P(),
        P(BATCH, None, None),
    )
    out_specs = (
        P(BATCH, None, None),
        P(BATCH, None, None),
        P(SEQ, None),
        P(SEQ, None),
        P(ALL, None),
    )
    return jax.shard_map(local, mesh=chips, in_specs=in_specs, out_specs=out_specs, check_vma=False)
```

```python
import functools

import jax
import jax.numpy as jnp
from jax import lax
from jax.experimental import pallas as pl
from jax.experimental.pallas import tpu as pltpu
from jax.sharding import Mesh, PartitionSpec as P

H = 16
BATCH = ("x", "core")
SEQ = ("z", "y")
CHIPS = ("x", "z", "y")
ALL = BATCH + SEQ
SLOTS = 3
WIDE = 256
PER_STEP = 2

epsilon = 1e-06
f32 = jnp.float32
bf16 = jnp.bfloat16


def rms_rows(values):
    return values * lax.rsqrt(jnp.mean(values * values, axis=-1, keepdims=True) + epsilon)


def rms_back(values, grads):
    factor = lax.rsqrt(jnp.mean(values * values, axis=-1, keepdims=True) + epsilon)
    normed = values * factor
    return factor * (grads - normed * jnp.mean(grads * normed, axis=-1, keepdims=True))


def normalize(values):
    return rms_rows(values.astype(f32)).astype(bf16)


def exchange(values, axes):
    return lax.all_to_all(values, axes, 0, 0, tiled=True)


def share(values, axes, count):
    return exchange(jnp.broadcast_to(values[None], (count,) + values.shape), axes)


def other_core(values):
    return lax.ppermute(values, "core", [(0, 1), (1, 0)])


def ring_step(values, axis, step):
    return lax.ppermute(values, axis, [(i, (i + step) % 4) for i in range(4)])


def chip_step(values, step):
    return ring_step(values, "x", step)


def along_chips(values):
    return [values, chip_step(values, 1), chip_step(values, 2), chip_step(values, 3)]


def place_of(group):
    chip = lax.rem(lax.axis_index("x") - group // 2 + 4, 4)
    return jnp.where(group % 2 == lax.axis_index("core"), 0, 4) + chip


def group_at(place):
    chip = lax.rem(lax.axis_index("x") - place % 4 + 4, 4)
    core = lax.axis_index("core")
    return 2 * chip + (core if place < 4 else 1 - core)


SMEM = pl.BlockSpec(memory_space=pltpu.SMEM)
VMEM = pl.BlockSpec(memory_space=pltpu.VMEM)
HBM = pl.BlockSpec(memory_space=pltpu.HBM)
LAST = (((1,), (1,)), ((), ()))
FIRST = (((0,), (0,)), ((), ()))


def room(mebibytes):
    return pltpu.CompilerParams(vmem_limit_bytes=mebibytes * 1024 * 1024)


def pairs_kernel(frames_ref, w_ref, normed_ref, out_ref):
    @pl.when(pl.program_id(0) == 0)
    def _():
        normed_ref[...] = normalize(frames_ref[...])

    out_ref[...] = jnp.dot(normed_ref[...], w_ref[...], preferred_element_type=f32).astype(bf16)


def project_pairs(frames, w_kv):
    rows, feature = frames.shape
    width, tile = w_kv.shape[1], 1024
    return pl.pallas_call(
        pairs_kernel,
        grid=(width // tile,),
        out_shape=(
            jax.ShapeDtypeStruct((rows, feature), bf16),
            jax.ShapeDtypeStruct((rows, width), bf16),
        ),
        in_specs=[
            pl.BlockSpec((rows, feature), lambda i: (0, 0)),
            pl.BlockSpec((feature, tile), lambda i: (0, i)),
        ],
        out_specs=(
            pl.BlockSpec((rows, feature), lambda i: (0, 0)),
            pl.BlockSpec((rows, tile), lambda i: (0, i)),
        ),
        cost_estimate=pl.CostEstimate(
            flops=2 * rows * feature * width, bytes_accessed=9 * 1024 * 1024, transcendentals=0
        ),
    )(frames, w_kv)


def low_lanes(shape):
    return lax.broadcasted_iota(jnp.int32, shape, len(shape) - 1) < 64


def spread(heads, masks):
    return jnp.concatenate([heads * mask for mask in masks], axis=0)


def head_masks():
    head = lax.broadcasted_iota(jnp.int32, (1, WIDE), 1) // 64
    return [jnp.where(head == at, 1.0, 0.0).astype(bf16) for at in range(WIDE // 64)]


def own_heads(product, rows):
    head = lax.broadcasted_iota(jnp.int32, (rows, WIDE), 1) // 64
    result = product[:rows]
    for at in range(1, WIDE // 64):
        result = jnp.where(head == at, product[at * rows : at * rows + rows], result)
    return result


def slots_of(groups):
    slots, used = [0], 1
    for i in range(1, 4):
        slot = used
        fresh = True
        for j in reversed(range(i)):
            slot = jnp.where(groups[i] == groups[j], slots[j], slot)
            fresh = fresh & (groups[i] != groups[j])
        slots.append(slot)
        used = used + jnp.where(fresh, 1, 0)
    return slots


def attend_kernel(counts, groups, places, *refs):
    pieces, (wq_in, wo_in, pairs_in, q_out, d_out, out_ref), scratch = refs[:8], refs[8:14], refs[14:]
    picked, wq, wo, pairs_ref, q_ref, d_ref, top_ref, total_ref, moment_ref, sems = scratch
    copies = [
        pltpu.make_async_copy(wq_in, wq, sems.at[0]),
        pltpu.make_async_copy(wo_in, wo, sems.at[1]),
        pltpu.make_async_copy(pairs_in, pairs_ref, sems.at[2]),
        pltpu.make_async_copy(q_ref, q_out, sems.at[3]),
        pltpu.make_async_copy(d_ref, d_out, sems.at[4]),
    ]
    for copy in copies[:3]:
        copy.start()
    rows, width = pieces[0].shape[1:]
    blocks = q_ref.shape[0] // rows
    for i in range(blocks):
        for j in range(8):

            @pl.when(places[i] == j)
            def _():
                picked[0, i * rows : (i + 1) * rows, :] = normalize(pieces[j][0])
                picked[1, i * rows : (i + 1) * rows, :] = pieces[j][1]

    copies[0].wait()
    for at in range(0, width, 256):
        tile = slice(at, at + 256)
        q_ref[:, tile] = jnp.dot(picked[0], wq[:, tile], preferred_element_type=f32).astype(bf16)
    copies[3].start()
    copies[1].wait()
    for at in range(0, width, 256):
        tile = slice(at, at + 256)
        d_ref[:, tile] = lax.dot_general(
            picked[1], wo[tile, :], LAST, preferred_element_type=f32
        ).astype(bf16)
    copies[4].start()
    copies[2].wait()

    masks = head_masks()
    scale = (width // H) ** (-0.5)
    position = lax.broadcasted_iota(jnp.int32, (128, WIDE), 0)

    def one_block(block, carry):
        usable = position < counts[block]
        here = pl.ds(pl.multiple_of(block * rows, rows), rows)
        there = pl.ds(pl.multiple_of(block * 128, 128), 128)
        for at in range(0, width, WIDE):
            cols = slice(at, at + WIDE)
            value_cols = slice(width + at, width + at + WIDE)
            s = lax.dot_general(
                pairs_ref[there, cols],
                spread(q_ref[here, cols], masks),
                LAST,
                preferred_element_type=f32,
            )
            s = jnp.where(usable, s * scale, -1e30)
            top = jnp.max(s, axis=0, keepdims=True)
            raw = jnp.where(usable, jnp.exp(s - top), 0.0)
            dw = lax.dot_general(
                pairs_ref[there, value_cols],
                spread(d_ref[here, cols], masks),
                LAST,
                preferred_element_type=f32,
            )
            total = jnp.sum(raw, axis=0, keepdims=True)
            moment = jnp.sum(raw * dw, axis=0, keepdims=True)
            for part in range(0, WIDE, 128):
                p = (at + part) // 128
                top_ref[block, p : p + 1, :] = top[:, part : part + 128]
                total_ref[block, p : p + 1, :] = total[:, part : part + 128]
                moment_ref[block, p : p + 1, :] = moment[:, part : part + 128]
        return carry

    lax.fori_loop(0, blocks, one_block, 0, unroll=2)
    own = [groups[i] for i in range(blocks)]
    slots = slots_of(own)
    left = low_lanes((8, 128))
    lane = lax.broadcasted_iota(jnp.int32, (8, 128), 1)
    note = jnp.full((8, 128), -1.0, f32)
    for i in range(blocks):
        note = jnp.where(lane == 64 + slots[i], own[i].astype(f32), note)
    for g in range(8):
        tops = [jnp.where(own[i] == g, top_ref[i], -1e30) for i in range(blocks)]
        top = functools.reduce(jnp.maximum, tops)
        total = jnp.zeros((8, 128), f32)
        moment = jnp.zeros((8, 128), f32)
        for i in range(blocks):
            factor = jnp.where(own[i] == g, jnp.exp(tops[i] - top), 0.0)
            total = total + factor * total_ref[i]
            moment = moment + factor * moment_ref[i]
        parts = (
            (jnp.where(left, top, pltpu.roll(total, 64, 1)), jnp.where(left, moment, note)),
            (
                jnp.where(left, pltpu.roll(top, 64, 1), total),
                jnp.where(left, pltpu.roll(moment, 64, 1), note),
            ),
        )
        for odd in range(2):
            for p in range(8):
                at = 16 * g + 8 * odd + p
                out_ref[at, :, 0:128] = parts[odd][0][p : p + 1]
                out_ref[at, :, 128:256] = parts[odd][1][p : p + 1]
    copies[3].wait()
    copies[4].wait()


def attend(counts, groups, places, pieces, w_query, w_out, pairs):
    rows, width = pieces[0].shape[1:]
    small = jax.ShapeDtypeStruct((groups.shape[0] * rows, width), bf16)
    return pl.pallas_call(
        attend_kernel,
        out_shape=(small, small, jax.ShapeDtypeStruct((128, 1, 256), f32)),
        in_specs=[SMEM] * 3 + [VMEM] * 8 + [HBM] * 3,
        out_specs=(HBM, HBM, VMEM),
        scratch_shapes=[
            pltpu.VMEM((2,) + small.shape, bf16),
            pltpu.VMEM(w_query.shape, bf16),
            pltpu.VMEM(w_out.shape, bf16),
            pltpu.VMEM(pairs.shape, bf16),
            pltpu.VMEM(small.shape, bf16),
            pltpu.VMEM(small.shape, bf16),
        ]
        + [pltpu.VMEM((groups.shape[0], 8, 128), f32)] * 3
        + [pltpu.SemaphoreType.DMA((5,))],
        cost_estimate=pl.CostEstimate(
            flops=6 * 1024 * 1024 * 1024,
            bytes_accessed=10 * 1024 * 1024,
            transcendentals=512 * 1024,
        ),
    )(counts, groups, places, *pieces, w_query, w_out, pairs)


def block_specs(latent_count, width):
    return [
        pl.BlockSpec((PER_STEP * latent_count, width), lambda i: (i, 0)),
        pl.BlockSpec((PER_STEP * latent_count, width), lambda i: (i, 0)),
        pl.BlockSpec((PER_STEP * 128, 2 * width), lambda i: (i, 0)),
    ]


def products_kernel(q_ref, d_ref, pairs_ref, scores_ref, d_weights_ref):
    masks = head_masks()
    width = q_ref.shape[1]
    rows = q_ref.shape[0] // PER_STEP
    scale = (width // H) ** (-0.5)
    for sub in range(PER_STEP):
        here = slice(sub * rows, sub * rows + rows)
        there = slice(sub * 128, sub * 128 + 128)
        for at in range(0, width, WIDE):
            cols = slice(at, at + WIDE)
            value_cols = slice(width + at, width + at + WIDE)
            scores_ref[there, cols] = scale * lax.dot_general(
                pairs_ref[there, cols],
                spread(q_ref[here, cols], masks),
                LAST,
                preferred_element_type=f32,
            )
            d_weights_ref[there, cols] = lax.dot_general(
                pairs_ref[there, value_cols],
                spread(d_ref[here, cols], masks),
                LAST,
                preferred_element_type=f32,
            )


def products(queries, d_mixed, pairs):
    width = queries.shape[1]
    out = jax.ShapeDtypeStruct((pairs.shape[0], width), f32)
    spec = pl.BlockSpec((PER_STEP * 128, width), lambda i: (i, 0))
    return pl.pallas_call(
        products_kernel,
        grid=(4 // PER_STEP,),
        out_shape=(out, out),
        in_specs=block_specs(queries.shape[0] // 4, width),
        out_specs=(spec, spec),
        cost_estimate=pl.CostEstimate(
            flops=2 * 1024 * 1024 * 1024, bytes_accessed=8 * 1024 * 1024, transcendentals=0
        ),
    )(queries, d_mixed, pairs)


def totals_kernel(in_ref, out_ref):
    left = low_lanes((1, 128))
    first = in_ref[:, 0, 0:128]
    top = jnp.max(first, axis=0, keepdims=True)
    top = jnp.where(left, top, pltpu.roll(top, 64, 1))
    factor = jnp.exp(jnp.where(left, first, pltpu.roll(first, 64, 1)) - top)
    total = jnp.sum(factor * first, axis=0, keepdims=True)
    inverse = 1.0 / jnp.where(left, pltpu.roll(total, 64, 1), total)
    delta = jnp.sum(factor * in_ref[:, 0, 128:256], axis=0, keepdims=True) * inverse
    reply = jnp.concatenate(
        [jnp.where(left, top, inverse), jnp.where(left, delta, 0.0)], axis=1
    )
    for at in range(in_ref.shape[0]):
        out_ref[at] = reply


def totals(stats):
    return pl.pallas_call(
        totals_kernel,
        out_shape=jax.ShapeDtypeStruct(stats.shape, f32),
        in_specs=[VMEM],
        out_specs=VMEM,
        compiler_params=room(4),
    )(stats)


def grads_kernel(
    counts,
    groups,
    core,
    q_ref,
    d_ref,
    pairs_ref,
    scores_ref,
    d_weights_ref,
    reply_ref,
    kept_ref,
    sent_ref,
    slotted_ref,
    mixed_acc,
    query_acc,
    mixed_now,
    query_now,
):
    step = pl.program_id(0)
    masks = head_masks()
    width = q_ref.shape[1]
    rows = q_ref.shape[0] // PER_STEP
    scale = (width // H) ** (-0.5)
    position = lax.broadcasted_iota(jnp.int32, (128, WIDE), 0)
    left = low_lanes((8, 128))
    wide = low_lanes((rows, 128))

    @pl.when(step == 0)
    def _():
        mixed_acc[...] = jnp.zeros_like(mixed_acc)
        query_acc[...] = jnp.zeros_like(query_acc)

    def row(pairs, at):
        first = at // 128
        return jnp.concatenate([pairs[p : p + 1] for p in range(first, first + WIDE // 128)], axis=1)

    slots = slots_of([groups[i] for i in range(4)])
    for sub in range(PER_STEP):
        block = step * PER_STEP + sub
        here = slice(sub * rows, sub * rows + rows)
        there = slice(sub * 128, sub * 128 + 128)
        usable = position < counts[block]
        group = groups[block]

        def reply_rows(odd, cols):
            first = 16 * group + 8 * odd
            return jnp.concatenate([reply_ref[first + p, :, cols] for p in range(8)], axis=0)

        even = reply_rows(0, slice(0, 128))
        odd = reply_rows(1, slice(0, 128))
        top = jnp.where(left, even, pltpu.roll(odd, 64, 1))
        inverse = jnp.where(left, pltpu.roll(even, 64, 1), odd)
        delta = jnp.where(
            left, reply_rows(0, slice(128, 256)), pltpu.roll(reply_rows(1, slice(128, 256)), 64, 1)
        )
        for at in range(0, width, WIDE):
            cols = slice(at, at + WIDE)
            value_cols = slice(width + at, width + at + WIDE)
            q = spread(q_ref[here, cols], masks)
            d = spread(d_ref[here, cols], masks)
            k = pairs_ref[there, cols]
            v = pairs_ref[there, value_cols]
            s = scores_ref[there, cols]
            dw = d_weights_ref[there, cols]
            weights = jnp.where(usable, jnp.exp(s - row(top, at)) * row(inverse, at), 0.0)
            weights_b = weights.astype(bf16)
            d_scores = (weights * (dw - row(delta, at)) * scale).astype(bf16)
            d_values = jnp.dot(weights_b, d, preferred_element_type=f32)
            d_keys = jnp.dot(d_scores, q, preferred_element_type=f32)
            kept_ref[there, cols] = jnp.where(core[0] == 0, d_keys, d_values).astype(bf16)
            sent_ref[there, cols] = jnp.where(core[0] == 0, d_values, d_keys).astype(bf16)
            mixed = lax.dot_general(weights_b, v, FIRST, preferred_element_type=f32)
            mixed_now[sub, :, cols] = own_heads(mixed, rows)
            query = lax.dot_general(d_scores, k, FIRST, preferred_element_type=f32)
            query_now[sub, :, cols] = own_heads(query, rows)
    for sub in range(PER_STEP):
        slot = slots[sub]
        for at in range(1, 4 // PER_STEP):
            slot = jnp.where(step == at, slots[at * PER_STEP + sub], slot)
        mixed_acc[slot] += mixed_now[sub]
        query_acc[slot] += query_now[sub]

    @pl.when(step == 4 // PER_STEP - 1)
    def _():
        for at in range(SLOTS):
            for p in range(width // 128):
                cols = slice(128 * p, 128 * p + 128)
                mixed = mixed_acc[at, :, cols]
                query = query_acc[at, :, cols]
                slotted_ref[2 * p, at] = jnp.where(
                    wide, mixed, pltpu.roll(query, 64, 1)
                ).astype(bf16)
                slotted_ref[2 * p + 1, at] = jnp.where(
                    wide, pltpu.roll(mixed, 64, 1), query
                ).astype(bf16)


def gradients(counts, groups, core, queries, d_mixed, pairs, scores, d_weights, reply):
    width = queries.shape[1]
    rows = queries.shape[0] // 4
    return pl.pallas_call(
        grads_kernel,
        grid=(4 // PER_STEP,),
        out_shape=(
            jax.ShapeDtypeStruct((pairs.shape[0], width), bf16),
            jax.ShapeDtypeStruct((pairs.shape[0], width), bf16),
            jax.ShapeDtypeStruct((H, SLOTS, rows, 128), bf16),
        ),
        in_specs=[SMEM, SMEM, SMEM]
        + block_specs(rows, width)
        + [pl.BlockSpec((PER_STEP * 128, width), lambda i: (i, 0))] * 2
        + [pl.BlockSpec((128, 1, 256), lambda i: (0, 0, 0))],
        out_specs=(
            pl.BlockSpec((PER_STEP * 128, width), lambda i: (i, 0)),
            pl.BlockSpec((PER_STEP * 128, width), lambda i: (i, 0)),
            pl.BlockSpec((H, SLOTS, rows, 128), lambda i: (0, 0, 0, 0)),
        ),
        scratch_shapes=[pltpu.VMEM((SLOTS, rows, width), f32)] * 2
        + [pltpu.VMEM((PER_STEP, rows, width), f32)] * 2,
        cost_estimate=pl.CostEstimate(
            flops=8 * 1024 * 1024 * 1024, bytes_accessed=8 * 1024 * 1024, transcendentals=512 * 1024
        ),
    )(counts, groups, core, queries, d_mixed, pairs, scores, d_weights, reply)


def prepare_kernel(owners, *refs):
    pieces, (latents_ref, d_out_ref) = refs[:8], refs[8:]
    rows = pieces[0].shape[1]
    for j in range(8):
        at = pl.ds(pl.multiple_of(owners[j] * rows, rows), rows)
        latents_ref[at, :] = normalize(pieces[j][0])
        d_out_ref[at, :] = pieces[j][1]


def prepare(owners, pieces):
    rows, width = pieces[0].shape[1:]
    out = jax.ShapeDtypeStruct((8 * rows, width), bf16)
    return pl.pallas_call(
        prepare_kernel,
        out_shape=(out, out),
        in_specs=[SMEM] + [VMEM] * 8,
        out_specs=(VMEM, VMEM),
        cost_estimate=pl.CostEstimate(
            flops=4 * 1024 * 1024, bytes_accessed=4 * 1024 * 1024, transcendentals=512
        ),
    )(owners, *pieces)


def owners_kernel(heads_ref, owned_ref, latents_ref, d_out_ref, outproj_ref, out_ref):
    rows = outproj_ref.shape[0]
    heads = heads_ref[...]
    outproj_ref[...] = lax.dot_general(
        heads, d_out_ref[...], FIRST, preferred_element_type=f32
    )[:rows]
    query = lax.dot_general(latents_ref[...], heads, FIRST, preferred_element_type=f32)
    other = pltpu.roll(query, 64, 1)
    half = rows // 2
    left = low_lanes((half, 128))
    for at in range(H):
        first, second = rows * at, rows * at + half
        out_ref[at, :rows] = owned_ref[...]
        out_ref[at, rows:] = jnp.where(
            left, other[first : first + half], query[second : second + half]
        ).astype(bf16)


def owners(heads, owned, normed_latents, d_outs):
    rows = owned.shape[0]
    width = d_outs.shape[1]
    return pl.pallas_call(
        owners_kernel,
        out_shape=(
            jax.ShapeDtypeStruct((rows, width), f32),
            jax.ShapeDtypeStruct((H, rows + rows // 2, 128), bf16),
        ),
        in_specs=[VMEM] * 4,
        out_specs=(VMEM, VMEM),
        cost_estimate=pl.CostEstimate(
            flops=512 * 1024 * 1024, bytes_accessed=4 * 1024 * 1024, transcendentals=0
        ),
    )(heads, owned, normed_latents, d_outs)


def finish_kernel(in_ref, latent_ref, d_out_ref, w_query_ref, w_out_in, *refs):
    out_ref, d_latents_ref, grad_query_ref, mixed, d_query, w_out_ref, sem = refs
    copy = pltpu.make_async_copy(w_out_in, w_out_ref, sem)
    copy.start()
    rows = latent_ref.shape[0]
    left = low_lanes((rows, 128))

    def parts(head):
        both = in_ref[head, rows:].astype(f32)
        return in_ref[head, :rows].astype(f32), both, pltpu.roll(both, 64, 1)

    for p in range(H // 2):
        cols = slice(128 * p, 128 * p + 128)
        even, even_grad, even_turned = parts(2 * p)
        odd, odd_grad, odd_turned = parts(2 * p + 1)
        mixed[:, cols] = jnp.where(left, even, pltpu.roll(odd, 64, 1)).astype(bf16)
        d_query[:, cols] = jnp.where(left, pltpu.roll(even, 64, 1), odd).astype(bf16)
        half = rows // 2
        narrow = left[:half]
        grad_query_ref[:half, cols] = jnp.where(narrow, even_grad, odd_turned)
        grad_query_ref[half:, cols] = jnp.where(narrow, even_turned, odd_grad)
    latent = latent_ref[...].astype(f32)
    d_normed = lax.dot_general(d_query[...], w_query_ref[...], LAST, preferred_element_type=f32)
    d_latents_ref[...] = (d_out_ref[...].astype(f32) + rms_back(latent, d_normed)).astype(bf16)
    copy.wait()
    update = jnp.dot(mixed[...], w_out_ref[...], preferred_element_type=f32)
    out_ref[...] = (latent + update).astype(bf16)


def finish(over_seq, latent, d_out, w_query, w_out):
    rows, width = latent.shape
    small = jax.ShapeDtypeStruct((rows, width), bf16)
    return pl.pallas_call(
        finish_kernel,
        out_shape=(small, small, jax.ShapeDtypeStruct((rows, width), f32)),
        in_specs=[VMEM] * 4 + [HBM],
        out_specs=(VMEM,) * 3,
        compiler_params=room(12),
        scratch_shapes=[pltpu.VMEM((rows, width), bf16)] * 2
        + [pltpu.VMEM(w_out.shape, bf16), pltpu.SemaphoreType.DMA],
    )(over_seq, latent, d_out, w_query, w_out)


def local(latents, frames, counts, groups, w_query, w_kv, w_out, d_out):
    blocks, block_rows, feature = frames.shape
    latent_count, model_width = latents.shape[1:]
    head_dim = model_width // H
    group_count, seq_count = 8, 16
    rows = blocks * block_rows
    core = lax.axis_index("core")
    batch_at = lax.axis_index(BATCH)

    near = along_chips(jnp.concatenate([latents, d_out], axis=0))
    normed, pairs = project_pairs(frames.reshape(rows, feature), w_kv)
    near = [lax.optimization_barrier((piece, normed, pairs))[0] for piece in near]
    pieces = near + [other_core(piece) for piece in near]
    queries, d_mixed, stats = attend(
        counts, groups, place_of(groups), pieces, w_query, w_out, pairs
    )
    sources = jnp.stack([group_at(j) for j in range(8)])
    normed, stats, queries, d_mixed = lax.optimization_barrier((normed, stats, queries, d_mixed))
    scores, d_weights = products(queries, d_mixed, pairs)
    normed = jnp.concatenate([normed, other_core(normed)], axis=0)
    stats = exchange(stats, ALL)
    source_groups = lax.dynamic_slice(
        stats, (batch_at * seq_count, 0, 192), (seq_count, 1, SLOTS)
    )
    chosen = (
        jnp.arange(group_count, dtype=f32)[:, None, None] == source_groups.reshape(1, seq_count, SLOTS)
    ).astype(bf16)
    reply, sources = lax.optimization_barrier((totals(stats), sources))
    all_latents, all_d_out = prepare(sources, pieces)
    reply = exchange(reply, ALL)
    reply, all_latents, all_d_out, normed, chosen, scores, d_weights = lax.optimization_barrier(
        (reply, all_latents, all_d_out, normed, chosen, scores, d_weights)
    )
    kept, sent, slotted = gradients(
        counts, groups, core.reshape(1), queries, d_mixed, pairs, scores, d_weights, reply
    )
    slotted = exchange(slotted, SEQ)

    d_half = jnp.concatenate([kept, other_core(sent)], axis=0)
    term = lax.dot_general(normed, d_half, FIRST, preferred_element_type=f32).astype(bf16)
    share_rows = feature // 128
    term = term.reshape(group_count, 4, 4 * share_rows, 8, 128)
    z_at = lax.axis_index("z")

    def z_part(step):
        return lax.dynamic_index_in_dim(term, lax.rem(z_at + step, 4), 1, False)

    parts = lax.optimization_barrier([z_part(step) for step in range(4)])
    got = [ring_step(parts[step], "z", step) for step in range(1, 4)]
    by_group = jnp.einsum("gsk,sklc->glc", chosen, slotted, preferred_element_type=f32)
    owned = jnp.sum(exchange(by_group, BATCH), axis=0).astype(bf16)
    heads = share(owned, BATCH, group_count).reshape(group_count * latent_count, 128)
    grad_outproj, owned_parts = owners(heads, owned, all_latents, all_d_out)
    owned_parts, got = lax.optimization_barrier((owned_parts, got))
    ring_sum = sum([part.astype(f32) for part in got], parts[0].astype(f32))
    ring_sum = ring_sum.astype(bf16).reshape(group_count, 4, share_rows, 8, 128)
    ring_sum = ring_sum.reshape(4 * group_count, share_rows, 8, 128)
    over_seq = exchange(owned_parts, SEQ)
    ring_sum, over_seq = lax.optimization_barrier((ring_sum, over_seq))
    ring_sum = exchange(ring_sum, BATCH + ("y",))
    out, d_latents, grad_query = finish(over_seq, latents[0], d_out[0], w_query, w_out)
    ring_sum, out, d_latents, grad_query = lax.optimization_barrier(
        (ring_sum, out, d_latents, grad_query)
    )
    ring_sum = ring_sum.reshape(4, 2, 4, share_rows, 8, 128).astype(f32)
    halves = jnp.sum(ring_sum, axis=(0, 2)).reshape(2, share_rows, model_width)
    grad_kv = jnp.concatenate([halves[0], halves[1]], axis=1)
    return (out[None], d_latents[None], grad_query, grad_outproj, grad_kv)


def solution(mesh):
    chips = Mesh(mesh.devices.reshape(4, 2, 4, 4), ("x", "core", "z", "y"))
    in_specs = (
        P(BATCH, None, None),
        P(ALL, None, None),
        P(ALL),
        P(ALL),
        P(),
        P(),
        P(),
        P(BATCH, None, None),
    )
    out_specs = (
        P(BATCH, None, None),
        P(BATCH, None, None),
        P(SEQ, None),
        P(SEQ, None),
        P(ALL, None),
    )
    return jax.shard_map(local, mesh=chips, in_specs=in_specs, out_specs=out_specs, check_vma=False)
```

```python
import functools

import jax
import jax.numpy as jnp
from jax import lax
from jax.experimental import pallas as pl
from jax.experimental.pallas import tpu as pltpu
from jax.sharding import Mesh, PartitionSpec as P

H = 16
BATCH = ("x", "core")
SEQ = ("z", "y")
CHIPS = ("x", "z", "y")
ALL = BATCH + SEQ
SLOTS = 3
WIDE = 256
PER_STEP = 2

epsilon = 1e-06
f32 = jnp.float32
bf16 = jnp.bfloat16


def rms_rows(values):
    return values * lax.rsqrt(jnp.mean(values * values, axis=-1, keepdims=True) + epsilon)


def rms_back(values, grads):
    factor = lax.rsqrt(jnp.mean(values * values, axis=-1, keepdims=True) + epsilon)
    normed = values * factor
    return factor * (grads - normed * jnp.mean(grads * normed, axis=-1, keepdims=True))


def normalize(values):
    return rms_rows(values.astype(f32)).astype(bf16)


def exchange(values, axes):
    return lax.all_to_all(values, axes, 0, 0, tiled=True)


def share(values, axes, count):
    return exchange(jnp.broadcast_to(values[None], (count,) + values.shape), axes)


def other_core(values):
    return lax.ppermute(values, "core", [(0, 1), (1, 0)])


def ring_step(values, axis, step):
    return lax.ppermute(values, axis, [(i, (i + step) % 4) for i in range(4)])


def chip_step(values, step):
    return ring_step(values, "x", step)


def along_chips(values):
    return [values, chip_step(values, 1), chip_step(values, 2), chip_step(values, 3)]


def place_of(group):
    chip = lax.rem(lax.axis_index("x") - group // 2 + 4, 4)
    return jnp.where(group % 2 == lax.axis_index("core"), 0, 4) + chip


def group_at(place):
    chip = lax.rem(lax.axis_index("x") - place % 4 + 4, 4)
    core = lax.axis_index("core")
    return 2 * chip + (core if place < 4 else 1 - core)


SMEM = pl.BlockSpec(memory_space=pltpu.SMEM)
VMEM = pl.BlockSpec(memory_space=pltpu.VMEM)
HBM = pl.BlockSpec(memory_space=pltpu.HBM)
LAST = (((1,), (1,)), ((), ()))
FIRST = (((0,), (0,)), ((), ()))


def room(mebibytes):
    return pltpu.CompilerParams(vmem_limit_bytes=mebibytes * 1024 * 1024)


def pairs_kernel(frames_ref, w_ref, normed_ref, out_ref):
    @pl.when(pl.program_id(0) == 0)
    def _():
        normed_ref[...] = normalize(frames_ref[...])

    out_ref[...] = jnp.dot(normed_ref[...], w_ref[...], preferred_element_type=f32).astype(bf16)


def pair_up_kernel(first_ref, second_ref, out_ref):
    out_ref[0:1] = first_ref[...]
    out_ref[1:2] = second_ref[...]


def pair_up(first, second):
    return pl.pallas_call(
        pair_up_kernel,
        out_shape=jax.ShapeDtypeStruct((2,) + first.shape[1:], first.dtype),
        in_specs=[VMEM, VMEM],
        out_specs=VMEM,
        cost_estimate=pl.CostEstimate(flops=0, bytes_accessed=512 * 1024, transcendentals=0),
    )(first, second)


def project_pairs(frames, w_kv):
    rows, feature = frames.shape
    width, tile = w_kv.shape[1], 1024
    return pl.pallas_call(
        pairs_kernel,
        grid=(width // tile,),
        out_shape=(
            jax.ShapeDtypeStruct((rows, feature), bf16),
            jax.ShapeDtypeStruct((rows, width), bf16),
        ),
        in_specs=[
            pl.BlockSpec((rows, feature), lambda i: (0, 0)),
            pl.BlockSpec((feature, tile), lambda i: (0, i)),
        ],
        out_specs=(
            pl.BlockSpec((rows, feature), lambda i: (0, 0)),
            pl.BlockSpec((rows, tile), lambda i: (0, i)),
        ),
        cost_estimate=pl.CostEstimate(
            flops=2 * rows * feature * width, bytes_accessed=9 * 1024 * 1024, transcendentals=0
        ),
    )(frames, w_kv)


def low_lanes(shape):
    return lax.broadcasted_iota(jnp.int32, shape, len(shape) - 1) < 64


def spread(heads, masks):
    return jnp.concatenate([heads * mask for mask in masks], axis=0)


def head_masks():
    head = lax.broadcasted_iota(jnp.int32, (1, WIDE), 1) // 64
    return [jnp.where(head == at, 1.0, 0.0).astype(bf16) for at in range(WIDE // 64)]


def own_heads(product, rows):
    head = lax.broadcasted_iota(jnp.int32, (rows, WIDE), 1) // 64
    result = product[:rows]
    for at in range(1, WIDE // 64):
        result = jnp.where(head == at, product[at * rows : at * rows + rows], result)
    return result


def slots_of(groups):
    slots, used = [0], 1
    for i in range(1, 4):
        slot = used
        fresh = True
        for j in reversed(range(i)):
            slot = jnp.where(groups[i] == groups[j], slots[j], slot)
            fresh = fresh & (groups[i] != groups[j])
        slots.append(slot)
        used = used + jnp.where(fresh, 1, 0)
    return slots


def attend_kernel(counts, groups, places, *refs):
    pieces, (wq_in, wo_in, pairs_in, q_out, d_out, out_ref), scratch = refs[:8], refs[8:14], refs[14:]
    picked, wq, wo, pairs_ref, q_ref, d_ref, top_ref, total_ref, moment_ref, sems = scratch
    copies = [
        pltpu.make_async_copy(wq_in, wq, sems.at[0]),
        pltpu.make_async_copy(wo_in, wo, sems.at[1]),
        pltpu.make_async_copy(pairs_in, pairs_ref, sems.at[2]),
        pltpu.make_async_copy(q_ref, q_out, sems.at[3]),
        pltpu.make_async_copy(d_ref, d_out, sems.at[4]),
    ]
    for copy in copies[:3]:
        copy.start()
    rows, width = pieces[0].shape[1:]
    blocks = q_ref.shape[0] // rows
    for i in range(blocks):
        for j in range(8):

            @pl.when(places[i] == j)
            def _():
                picked[0, i * rows : (i + 1) * rows, :] = normalize(pieces[j][0])
                picked[1, i * rows : (i + 1) * rows, :] = pieces[j][1]

    copies[0].wait()
    for at in range(0, width, 256):
        tile = slice(at, at + 256)
        q_ref[:, tile] = jnp.dot(picked[0], wq[:, tile], preferred_element_type=f32).astype(bf16)
    copies[3].start()
    copies[1].wait()
    for at in range(0, width, 256):
        tile = slice(at, at + 256)
        d_ref[:, tile] = lax.dot_general(
            picked[1], wo[tile, :], LAST, preferred_element_type=f32
        ).astype(bf16)
    copies[4].start()
    copies[2].wait()

    masks = head_masks()
    scale = (width // H) ** (-0.5)
    position = lax.broadcasted_iota(jnp.int32, (128, WIDE), 0)

    def one_block(block, carry):
        usable = position < counts[block]
        here = pl.ds(pl.multiple_of(block * rows, rows), rows)
        there = pl.ds(pl.multiple_of(block * 128, 128), 128)
        for at in range(0, width, WIDE):
            cols = slice(at, at + WIDE)
            value_cols = slice(width + at, width + at + WIDE)
            s = lax.dot_general(
                pairs_ref[there, cols],
                spread(q_ref[here, cols], masks),
                LAST,
                preferred_element_type=f32,
            )
            s = jnp.where(usable, s * scale, -1e30)
            top = jnp.max(s, axis=0, keepdims=True)
            raw = jnp.where(usable, jnp.exp(s - top), 0.0)
            dw = lax.dot_general(
                pairs_ref[there, value_cols],
                spread(d_ref[here, cols], masks),
                LAST,
                preferred_element_type=f32,
            )
            total = jnp.sum(raw, axis=0, keepdims=True)
            moment = jnp.sum(raw * dw, axis=0, keepdims=True)
            for part in range(0, WIDE, 128):
                p = (at + part) // 128
                top_ref[block, p : p + 1, :] = top[:, part : part + 128]
                total_ref[block, p : p + 1, :] = total[:, part : part + 128]
                moment_ref[block, p : p + 1, :] = moment[:, part : part + 128]
        return carry

    lax.fori_loop(0, blocks, one_block, 0, unroll=2)
    own = [groups[i] for i in range(blocks)]
    slots = slots_of(own)
    left = low_lanes((8, 128))
    lane = lax.broadcasted_iota(jnp.int32, (8, 128), 1)
    note = jnp.full((8, 128), -1.0, f32)
    for i in range(blocks):
        note = jnp.where(lane == 64 + slots[i], own[i].astype(f32), note)
    for g in range(8):
        tops = [jnp.where(own[i] == g, top_ref[i], -1e30) for i in range(blocks)]
        top = functools.reduce(jnp.maximum, tops)
        total = jnp.zeros((8, 128), f32)
        moment = jnp.zeros((8, 128), f32)
        for i in range(blocks):
            factor = jnp.where(own[i] == g, jnp.exp(tops[i] - top), 0.0)
            total = total + factor * total_ref[i]
            moment = moment + factor * moment_ref[i]
        parts = (
            (jnp.where(left, top, pltpu.roll(total, 64, 1)), jnp.where(left, moment, note)),
            (
                jnp.where(left, pltpu.roll(top, 64, 1), total),
                jnp.where(left, pltpu.roll(moment, 64, 1), note),
            ),
        )
        for odd in range(2):
            for p in range(8):
                at = 16 * g + 8 * odd + p
                out_ref[at, :, 0:128] = parts[odd][0][p : p + 1]
                out_ref[at, :, 128:256] = parts[odd][1][p : p + 1]
    copies[3].wait()
    copies[4].wait()


def attend(counts, groups, places, pieces, w_query, w_out, pairs):
    rows, width = pieces[0].shape[1:]
    small = jax.ShapeDtypeStruct((groups.shape[0] * rows, width), bf16)
    return pl.pallas_call(
        attend_kernel,
        out_shape=(small, small, jax.ShapeDtypeStruct((128, 1, 256), f32)),
        in_specs=[SMEM] * 3 + [VMEM] * 8 + [HBM] * 3,
        out_specs=(HBM, HBM, VMEM),
        scratch_shapes=[
            pltpu.VMEM((2,) + small.shape, bf16),
            pltpu.VMEM(w_query.shape, bf16),
            pltpu.VMEM(w_out.shape, bf16),
            pltpu.VMEM(pairs.shape, bf16),
            pltpu.VMEM(small.shape, bf16),
            pltpu.VMEM(small.shape, bf16),
        ]
        + [pltpu.VMEM((groups.shape[0], 8, 128), f32)] * 3
        + [pltpu.SemaphoreType.DMA((5,))],
        cost_estimate=pl.CostEstimate(
            flops=6 * 1024 * 1024 * 1024,
            bytes_accessed=10 * 1024 * 1024,
            transcendentals=512 * 1024,
        ),
    )(counts, groups, places, *pieces, w_query, w_out, pairs)


def block_specs(latent_count, width):
    return [
        pl.BlockSpec((PER_STEP * latent_count, width), lambda i: (i, 0)),
        pl.BlockSpec((PER_STEP * latent_count, width), lambda i: (i, 0)),
        pl.BlockSpec((PER_STEP * 128, 2 * width), lambda i: (i, 0)),
    ]


def products_kernel(q_ref, d_ref, pairs_ref, scores_ref, d_weights_ref):
    masks = head_masks()
    width = q_ref.shape[1]
    rows = q_ref.shape[0] // PER_STEP
    scale = (width // H) ** (-0.5)
    for sub in range(PER_STEP):
        here = slice(sub * rows, sub * rows + rows)
        there = slice(sub * 128, sub * 128 + 128)
        for at in range(0, width, WIDE):
            cols = slice(at, at + WIDE)
            value_cols = slice(width + at, width + at + WIDE)
            scores_ref[there, cols] = scale * lax.dot_general(
                pairs_ref[there, cols],
                spread(q_ref[here, cols], masks),
                LAST,
                preferred_element_type=f32,
            )
            d_weights_ref[there, cols] = lax.dot_general(
                pairs_ref[there, value_cols],
                spread(d_ref[here, cols], masks),
                LAST,
                preferred_element_type=f32,
            )


def products(queries, d_mixed, pairs):
    width = queries.shape[1]
    out = jax.ShapeDtypeStruct((pairs.shape[0], width), f32)
    spec = pl.BlockSpec((PER_STEP * 128, width), lambda i: (i, 0))
    return pl.pallas_call(
        products_kernel,
        grid=(4 // PER_STEP,),
        out_shape=(out, out),
        in_specs=block_specs(queries.shape[0] // 4, width),
        out_specs=(spec, spec),
        cost_estimate=pl.CostEstimate(
            flops=2 * 1024 * 1024 * 1024, bytes_accessed=8 * 1024 * 1024, transcendentals=0
        ),
    )(queries, d_mixed, pairs)


def totals_kernel(in_ref, out_ref):
    left = low_lanes((1, 128))
    first = in_ref[:, 0, 0:128]
    top = jnp.max(first, axis=0, keepdims=True)
    top = jnp.where(left, top, pltpu.roll(top, 64, 1))
    factor = jnp.exp(jnp.where(left, first, pltpu.roll(first, 64, 1)) - top)
    total = jnp.sum(factor * first, axis=0, keepdims=True)
    inverse = 1.0 / jnp.where(left, pltpu.roll(total, 64, 1), total)
    delta = jnp.sum(factor * in_ref[:, 0, 128:256], axis=0, keepdims=True) * inverse
    reply = jnp.concatenate(
        [jnp.where(left, top, inverse), jnp.where(left, delta, 0.0)], axis=1
    )
    for at in range(in_ref.shape[0]):
        out_ref[at] = reply


def totals(stats):
    return pl.pallas_call(
        totals_kernel,
        out_shape=jax.ShapeDtypeStruct(stats.shape, f32),
        in_specs=[VMEM],
        out_specs=VMEM,
        compiler_params=room(4),
    )(stats)


def grads_kernel(
    counts,
    groups,
    core,
    q_ref,
    d_ref,
    pairs_ref,
    scores_ref,
    d_weights_ref,
    reply_ref,
    kept_ref,
    sent_ref,
    slotted_ref,
    mixed_acc,
    query_acc,
    mixed_now,
    query_now,
):
    step = pl.program_id(0)
    masks = head_masks()
    width = q_ref.shape[1]
    rows = q_ref.shape[0] // PER_STEP
    scale = (width // H) ** (-0.5)
    position = lax.broadcasted_iota(jnp.int32, (128, WIDE), 0)
    left = low_lanes((8, 128))
    wide = low_lanes((rows, 128))

    @pl.when(step == 0)
    def _():
        mixed_acc[...] = jnp.zeros_like(mixed_acc)
        query_acc[...] = jnp.zeros_like(query_acc)

    def row(pairs, at):
        first = at // 128
        return jnp.concatenate([pairs[p : p + 1] for p in range(first, first + WIDE // 128)], axis=1)

    slots = slots_of([groups[i] for i in range(4)])
    for sub in range(PER_STEP):
        block = step * PER_STEP + sub
        here = slice(sub * rows, sub * rows + rows)
        there = slice(sub * 128, sub * 128 + 128)
        usable = position < counts[block]
        group = groups[block]

        def reply_rows(odd, cols):
            first = 16 * group + 8 * odd
            return jnp.concatenate([reply_ref[first + p, :, cols] for p in range(8)], axis=0)

        even = reply_rows(0, slice(0, 128))
        odd = reply_rows(1, slice(0, 128))
        top = jnp.where(left, even, pltpu.roll(odd, 64, 1))
        inverse = jnp.where(left, pltpu.roll(even, 64, 1), odd)
        delta = jnp.where(
            left, reply_rows(0, slice(128, 256)), pltpu.roll(reply_rows(1, slice(128, 256)), 64, 1)
        )
        for at in range(0, width, WIDE):
            cols = slice(at, at + WIDE)
            value_cols = slice(width + at, width + at + WIDE)
            q = spread(q_ref[here, cols], masks)
            d = spread(d_ref[here, cols], masks)
            k = pairs_ref[there, cols]
            v = pairs_ref[there, value_cols]
            s = scores_ref[there, cols]
            dw = d_weights_ref[there, cols]
            weights = jnp.where(usable, jnp.exp(s - row(top, at)) * row(inverse, at), 0.0)
            weights_b = weights.astype(bf16)
            d_scores = (weights * (dw - row(delta, at)) * scale).astype(bf16)
            d_values = jnp.dot(weights_b, d, preferred_element_type=f32)
            d_keys = jnp.dot(d_scores, q, preferred_element_type=f32)
            kept_ref[there, cols] = jnp.where(core[0] == 0, d_keys, d_values).astype(bf16)
            sent_ref[there, cols] = jnp.where(core[0] == 0, d_values, d_keys).astype(bf16)
            mixed = lax.dot_general(weights_b, v, FIRST, preferred_element_type=f32)
            mixed_now[sub, :, cols] = own_heads(mixed, rows)
            query = lax.dot_general(d_scores, k, FIRST, preferred_element_type=f32)
            query_now[sub, :, cols] = own_heads(query, rows)
    for sub in range(PER_STEP):
        slot = slots[sub]
        for at in range(1, 4 // PER_STEP):
            slot = jnp.where(step == at, slots[at * PER_STEP + sub], slot)
        mixed_acc[slot] += mixed_now[sub]
        query_acc[slot] += query_now[sub]

    @pl.when(step == 4 // PER_STEP - 1)
    def _():
        for at in range(SLOTS):
            for p in range(width // 128):
                cols = slice(128 * p, 128 * p + 128)
                mixed = mixed_acc[at, :, cols]
                query = query_acc[at, :, cols]
                slotted_ref[2 * p, at] = jnp.where(
                    wide, mixed, pltpu.roll(query, 64, 1)
                ).astype(bf16)
                slotted_ref[2 * p + 1, at] = jnp.where(
                    wide, pltpu.roll(mixed, 64, 1), query
                ).astype(bf16)


def gradients(counts, groups, core, queries, d_mixed, pairs, scores, d_weights, reply):
    width = queries.shape[1]
    rows = queries.shape[0] // 4
    return pl.pallas_call(
        grads_kernel,
        grid=(4 // PER_STEP,),
        out_shape=(
            jax.ShapeDtypeStruct((pairs.shape[0], width), bf16),
            jax.ShapeDtypeStruct((pairs.shape[0], width), bf16),
            jax.ShapeDtypeStruct((H, SLOTS, rows, 128), bf16),
        ),
        in_specs=[SMEM, SMEM, SMEM]
        + block_specs(rows, width)
        + [pl.BlockSpec((PER_STEP * 128, width), lambda i: (i, 0))] * 2
        + [pl.BlockSpec((128, 1, 256), lambda i: (0, 0, 0))],
        out_specs=(
            pl.BlockSpec((PER_STEP * 128, width), lambda i: (i, 0)),
            pl.BlockSpec((PER_STEP * 128, width), lambda i: (i, 0)),
            pl.BlockSpec((H, SLOTS, rows, 128), lambda i: (0, 0, 0, 0)),
        ),
        scratch_shapes=[pltpu.VMEM((SLOTS, rows, width), f32)] * 2
        + [pltpu.VMEM((PER_STEP, rows, width), f32)] * 2,
        cost_estimate=pl.CostEstimate(
            flops=8 * 1024 * 1024 * 1024, bytes_accessed=8 * 1024 * 1024, transcendentals=512 * 1024
        ),
    )(counts, groups, core, queries, d_mixed, pairs, scores, d_weights, reply)


def prepare_kernel(owners, *refs):
    pieces, (latents_ref, d_out_ref) = refs[:8], refs[8:]
    rows = pieces[0].shape[1]
    for j in range(8):
        at = pl.ds(pl.multiple_of(owners[j] * rows, rows), rows)
        latents_ref[at, :] = normalize(pieces[j][0])
        d_out_ref[at, :] = pieces[j][1]


def prepare(owners, pieces):
    rows, width = pieces[0].shape[1:]
    out = jax.ShapeDtypeStruct((8 * rows, width), bf16)
    return pl.pallas_call(
        prepare_kernel,
        out_shape=(out, out),
        in_specs=[SMEM] + [VMEM] * 8,
        out_specs=(VMEM, VMEM),
        cost_estimate=pl.CostEstimate(
            flops=4 * 1024 * 1024, bytes_accessed=4 * 1024 * 1024, transcendentals=512
        ),
    )(owners, *pieces)


def owners_kernel(heads_ref, owned_ref, latents_ref, d_out_ref, outproj_ref, out_ref):
    rows = outproj_ref.shape[0]
    heads = heads_ref[...]
    outproj_ref[...] = lax.dot_general(
        heads, d_out_ref[...], FIRST, preferred_element_type=f32
    )[:rows]
    query = lax.dot_general(latents_ref[...], heads, FIRST, preferred_element_type=f32)
    other = pltpu.roll(query, 64, 1)
    half = rows // 2
    left = low_lanes((half, 128))
    for at in range(H):
        first, second = rows * at, rows * at + half
        out_ref[at, :rows] = owned_ref[...]
        out_ref[at, rows:] = jnp.where(
            left, other[first : first + half], query[second : second + half]
        ).astype(bf16)


def owners(heads, owned, normed_latents, d_outs):
    rows = owned.shape[0]
    width = d_outs.shape[1]
    return pl.pallas_call(
        owners_kernel,
        out_shape=(
            jax.ShapeDtypeStruct((rows, width), f32),
            jax.ShapeDtypeStruct((H, rows + rows // 2, 128), bf16),
        ),
        in_specs=[VMEM] * 4,
        out_specs=(VMEM, VMEM),
        cost_estimate=pl.CostEstimate(
            flops=512 * 1024 * 1024, bytes_accessed=4 * 1024 * 1024, transcendentals=0
        ),
    )(heads, owned, normed_latents, d_outs)


def finish_kernel(in_ref, latent_ref, d_out_ref, w_query_ref, w_out_in, *refs):
    out_ref, d_latents_ref, grad_query_ref, mixed, d_query, w_out_ref, sem = refs
    copy = pltpu.make_async_copy(w_out_in, w_out_ref, sem)
    copy.start()
    rows = latent_ref.shape[0]
    left = low_lanes((rows, 128))

    def parts(head):
        both = in_ref[head, rows:].astype(f32)
        return in_ref[head, :rows].astype(f32), both, pltpu.roll(both, 64, 1)

    for p in range(H // 2):
        cols = slice(128 * p, 128 * p + 128)
        even, even_grad, even_turned = parts(2 * p)
        odd, odd_grad, odd_turned = parts(2 * p + 1)
        mixed[:, cols] = jnp.where(left, even, pltpu.roll(odd, 64, 1)).astype(bf16)
        d_query[:, cols] = jnp.where(left, pltpu.roll(even, 64, 1), odd).astype(bf16)
        half = rows // 2
        narrow = left[:half]
        grad_query_ref[:half, cols] = jnp.where(narrow, even_grad, odd_turned)
        grad_query_ref[half:, cols] = jnp.where(narrow, even_turned, odd_grad)
    latent = latent_ref[...].astype(f32)
    d_normed = lax.dot_general(d_query[...], w_query_ref[...], LAST, preferred_element_type=f32)
    d_latents_ref[...] = (d_out_ref[...].astype(f32) + rms_back(latent, d_normed)).astype(bf16)
    copy.wait()
    update = jnp.dot(mixed[...], w_out_ref[...], preferred_element_type=f32)
    out_ref[...] = (latent + update).astype(bf16)


def finish(over_seq, latent, d_out, w_query, w_out):
    rows, width = latent.shape
    small = jax.ShapeDtypeStruct((rows, width), bf16)
    return pl.pallas_call(
        finish_kernel,
        out_shape=(small, small, jax.ShapeDtypeStruct((rows, width), f32)),
        in_specs=[VMEM] * 4 + [HBM],
        out_specs=(VMEM,) * 3,
        compiler_params=room(12),
        scratch_shapes=[pltpu.VMEM((rows, width), bf16)] * 2
        + [pltpu.VMEM(w_out.shape, bf16), pltpu.SemaphoreType.DMA],
    )(over_seq, latent, d_out, w_query, w_out)


def local(latents, frames, counts, groups, w_query, w_kv, w_out, d_out):
    blocks, block_rows, feature = frames.shape
    latent_count, model_width = latents.shape[1:]
    head_dim = model_width // H
    group_count, seq_count = 8, 16
    rows = blocks * block_rows
    core = lax.axis_index("core")
    batch_at = lax.axis_index(BATCH)

    near = along_chips(pair_up(latents, d_out))
    normed, pairs = project_pairs(frames.reshape(rows, feature), w_kv)
    sources = jnp.stack([group_at(j) for j in range(8)])
    places = place_of(groups)
    near = [lax.optimization_barrier((piece, normed, pairs))[0] for piece in near]
    near[0], sources, places = lax.optimization_barrier((near[0], sources, places))
    pieces = near + [other_core(piece) for piece in near]
    queries, d_mixed, stats = attend(
        counts, groups, places, pieces, w_query, w_out, pairs
    )
    normed, stats, queries, d_mixed = lax.optimization_barrier((normed, stats, queries, d_mixed))
    scores, d_weights = products(queries, d_mixed, pairs)
    normed = jnp.concatenate([normed, other_core(normed)], axis=0)
    stats = exchange(stats, ALL)
    source_groups = lax.dynamic_slice(
        stats, (batch_at * seq_count, 0, 192), (seq_count, 1, SLOTS)
    )
    chosen = (
        jnp.arange(group_count, dtype=f32)[:, None, None] == source_groups.reshape(1, seq_count, SLOTS)
    ).astype(bf16)
    reply, sources = lax.optimization_barrier((totals(stats), sources))
    all_latents, all_d_out = prepare(sources, pieces)
    reply = exchange(reply, ALL)
    reply, all_latents, all_d_out, normed, chosen, scores, d_weights = lax.optimization_barrier(
        (reply, all_latents, all_d_out, normed, chosen, scores, d_weights)
    )
    kept, sent, slotted = gradients(
        counts, groups, core.reshape(1), queries, d_mixed, pairs, scores, d_weights, reply
    )
    slotted = exchange(slotted, SEQ)

    d_half = jnp.concatenate([kept, other_core(sent)], axis=0)
    term = lax.dot_general(normed, d_half, FIRST, preferred_element_type=f32).astype(bf16)
    share_rows = feature // 128
    term = term.reshape(group_count, 4, 4 * share_rows, 8, 128)
    z_at = lax.axis_index("z")

    def z_part(step):
        return lax.dynamic_index_in_dim(term, lax.rem(z_at + step, 4), 1, False)

    parts = lax.optimization_barrier([z_part(step) for step in range(4)])
    got = [ring_step(parts[step], "z", step) for step in range(1, 4)]
    by_group = jnp.einsum("gsk,sklc->glc", chosen, slotted, preferred_element_type=f32)
    owned = jnp.sum(exchange(by_group, BATCH), axis=0).astype(bf16)
    heads = share(owned, BATCH, group_count).reshape(group_count * latent_count, 128)
    grad_outproj, owned_parts = owners(heads, owned, all_latents, all_d_out)
    owned_parts, got = lax.optimization_barrier((owned_parts, got))
    ring_sum = sum([part.astype(f32) for part in got], parts[0].astype(f32))
    ring_sum = ring_sum.astype(bf16).reshape(group_count, 4, share_rows, 8, 128)
    ring_sum = ring_sum.reshape(4 * group_count, share_rows, 8, 128)
    over_seq = exchange(owned_parts, SEQ)
    ring_sum, over_seq = lax.optimization_barrier((ring_sum, over_seq))
    ring_sum = exchange(ring_sum, BATCH + ("y",))
    out, d_latents, grad_query = finish(over_seq, latents[0], d_out[0], w_query, w_out)
    ring_sum, out, d_latents, grad_query = lax.optimization_barrier(
        (ring_sum, out, d_latents, grad_query)
    )
    ring_sum = ring_sum.reshape(4, 2, 4, share_rows, 8, 128).astype(f32)
    halves = jnp.sum(ring_sum, axis=(0, 2)).reshape(2, share_rows, model_width)
    grad_kv = jnp.concatenate([halves[0], halves[1]], axis=1)
    return (out[None], d_latents[None], grad_query, grad_outproj, grad_kv)


def solution(mesh):
    chips = Mesh(mesh.devices.reshape(4, 2, 4, 4), ("x", "core", "z", "y"))
    in_specs = (
        P(BATCH, None, None),
        P(ALL, None, None),
        P(ALL),
        P(ALL),
        P(),
        P(),
        P(),
        P(BATCH, None, None),
    )
    out_specs = (
        P(BATCH, None, None),
        P(BATCH, None, None),
        P(SEQ, None),
        P(SEQ, None),
        P(ALL, None),
    )
    return jax.shard_map(local, mesh=chips, in_specs=in_specs, out_specs=out_specs, check_vma=False)
```

```python
import functools

import jax
import jax.numpy as jnp
from jax import lax
from jax.experimental import pallas as pl
from jax.experimental.pallas import tpu as pltpu
from jax.sharding import Mesh, PartitionSpec as P

H = 16
BATCH = ("x", "core")
SEQ = ("z", "y")
CHIPS = ("x", "z", "y")
ALL = BATCH + SEQ
SLOTS = 3
WIDE = 256
PER_STEP = 2

epsilon = 1e-06
f32 = jnp.float32
bf16 = jnp.bfloat16


def rms_rows(values):
    return values * lax.rsqrt(jnp.mean(values * values, axis=-1, keepdims=True) + epsilon)


def rms_back(values, grads):
    factor = lax.rsqrt(jnp.mean(values * values, axis=-1, keepdims=True) + epsilon)
    normed = values * factor
    return factor * (grads - normed * jnp.mean(grads * normed, axis=-1, keepdims=True))


def normalize(values):
    return rms_rows(values.astype(f32)).astype(bf16)


def exchange(values, axes):
    return lax.all_to_all(values, axes, 0, 0, tiled=True)


def share(values, axes, count):
    return exchange(jnp.broadcast_to(values[None], (count,) + values.shape), axes)


def other_core(values):
    return lax.ppermute(values, "core", [(0, 1), (1, 0)])


def ring_step(values, axis, step):
    return lax.ppermute(values, axis, [(i, (i + step) % 4) for i in range(4)])


def chip_step(values, step):
    return ring_step(values, "x", step)


def along_chips(values):
    return [values, chip_step(values, 1), chip_step(values, 2), chip_step(values, 3)]


def place_of(group):
    chip = lax.rem(lax.axis_index("x") - group // 2 + 4, 4)
    return jnp.where(group % 2 == lax.axis_index("core"), 0, 4) + chip


def group_at(place):
    chip = lax.rem(lax.axis_index("x") - place % 4 + 4, 4)
    core = lax.axis_index("core")
    return 2 * chip + (core if place < 4 else 1 - core)


SMEM = pl.BlockSpec(memory_space=pltpu.SMEM)
VMEM = pl.BlockSpec(memory_space=pltpu.VMEM)
HBM = pl.BlockSpec(memory_space=pltpu.HBM)
LAST = (((1,), (1,)), ((), ()))
FIRST = (((0,), (0,)), ((), ()))


def room(mebibytes):
    return pltpu.CompilerParams(vmem_limit_bytes=mebibytes * 1024 * 1024)


def pairs_kernel(frames_ref, w_ref, normed_ref, out_ref):
    @pl.when(pl.program_id(0) == 0)
    def _():
        normed_ref[...] = normalize(frames_ref[...])

    out_ref[...] = jnp.dot(normed_ref[...], w_ref[...], preferred_element_type=f32).astype(bf16)


def pair_up_kernel(first_ref, second_ref, out_ref):
    out_ref[0:1] = first_ref[...]
    out_ref[1:2] = second_ref[...]


def pair_up(first, second):
    return pl.pallas_call(
        pair_up_kernel,
        out_shape=jax.ShapeDtypeStruct((2,) + first.shape[1:], first.dtype),
        in_specs=[VMEM, VMEM],
        out_specs=VMEM,
        cost_estimate=pl.CostEstimate(flops=0, bytes_accessed=512 * 1024, transcendentals=0),
    )(first, second)


def project_pairs(frames, w_kv):
    rows, feature = frames.shape
    width, tile = w_kv.shape[1], 1024
    return pl.pallas_call(
        pairs_kernel,
        grid=(width // tile,),
        out_shape=(
            jax.ShapeDtypeStruct((rows, feature), bf16),
            jax.ShapeDtypeStruct((rows, width), bf16),
        ),
        in_specs=[
            pl.BlockSpec((rows, feature), lambda i: (0, 0)),
            pl.BlockSpec((feature, tile), lambda i: (0, i)),
        ],
        out_specs=(
            pl.BlockSpec((rows, feature), lambda i: (0, 0)),
            pl.BlockSpec((rows, tile), lambda i: (0, i)),
        ),
        cost_estimate=pl.CostEstimate(
            flops=2 * rows * feature * width, bytes_accessed=9 * 1024 * 1024, transcendentals=0
        ),
    )(frames, w_kv)


def low_lanes(shape):
    return lax.broadcasted_iota(jnp.int32, shape, len(shape) - 1) < 64


def spread(heads, masks):
    return jnp.concatenate([heads * mask for mask in masks], axis=0)


def head_masks():
    head = lax.broadcasted_iota(jnp.int32, (1, WIDE), 1) // 64
    return [jnp.where(head == at, 1.0, 0.0).astype(bf16) for at in range(WIDE // 64)]


def own_heads(product, rows):
    head = lax.broadcasted_iota(jnp.int32, (rows, WIDE), 1) // 64
    result = product[:rows]
    for at in range(1, WIDE // 64):
        result = jnp.where(head == at, product[at * rows : at * rows + rows], result)
    return result


def slots_of(groups):
    slots, used = [0], 1
    for i in range(1, 4):
        slot = used
        fresh = True
        for j in reversed(range(i)):
            slot = jnp.where(groups[i] == groups[j], slots[j], slot)
            fresh = fresh & (groups[i] != groups[j])
        slots.append(slot)
        used = used + jnp.where(fresh, 1, 0)
    return slots


def attend_kernel(counts, groups, places, *refs):
    pieces, (wq_in, wo_in, pairs_in, q_out, d_out, out_ref), scratch = refs[:8], refs[8:14], refs[14:]
    picked, wq, wo, pairs_ref, q_ref, d_ref, top_ref, total_ref, moment_ref, sems = scratch
    copies = [
        pltpu.make_async_copy(wq_in, wq, sems.at[0]),
        pltpu.make_async_copy(wo_in, wo, sems.at[1]),
        pltpu.make_async_copy(pairs_in, pairs_ref, sems.at[2]),
        pltpu.make_async_copy(q_ref, q_out, sems.at[3]),
        pltpu.make_async_copy(d_ref, d_out, sems.at[4]),
    ]
    for copy in copies[:3]:
        copy.start()
    rows, width = pieces[0].shape[1:]
    blocks = q_ref.shape[0] // rows
    for i in range(blocks):
        for j in range(8):

            @pl.when(places[i] == j)
            def _():
                picked[0, i * rows : (i + 1) * rows, :] = normalize(pieces[j][0])
                picked[1, i * rows : (i + 1) * rows, :] = pieces[j][1]

    copies[0].wait()
    for at in range(0, width, 256):
        tile = slice(at, at + 256)
        q_ref[:, tile] = jnp.dot(picked[0], wq[:, tile], preferred_element_type=f32).astype(bf16)
    copies[3].start()
    copies[1].wait()
    for at in range(0, width, 256):
        tile = slice(at, at + 256)
        d_ref[:, tile] = lax.dot_general(
            picked[1], wo[tile, :], LAST, preferred_element_type=f32
        ).astype(bf16)
    copies[4].start()
    copies[2].wait()

    masks = head_masks()
    scale = (width // H) ** (-0.5)
    position = lax.broadcasted_iota(jnp.int32, (128, WIDE), 0)

    def one_block(block, carry):
        usable = position < counts[block]
        here = pl.ds(pl.multiple_of(block * rows, rows), rows)
        there = pl.ds(pl.multiple_of(block * 128, 128), 128)
        for at in range(0, width, WIDE):
            cols = slice(at, at + WIDE)
            value_cols = slice(width + at, width + at + WIDE)
            s = lax.dot_general(
                pairs_ref[there, cols],
                spread(q_ref[here, cols], masks),
                LAST,
                preferred_element_type=f32,
            )
            s = jnp.where(usable, s * scale, -1e30)
            top = jnp.max(s, axis=0, keepdims=True)
            raw = jnp.where(usable, jnp.exp(s - top), 0.0)
            dw = lax.dot_general(
                pairs_ref[there, value_cols],
                spread(d_ref[here, cols], masks),
                LAST,
                preferred_element_type=f32,
            )
            total = jnp.sum(raw, axis=0, keepdims=True)
            moment = jnp.sum(raw * dw, axis=0, keepdims=True)
            for part in range(0, WIDE, 128):
                p = (at + part) // 128
                top_ref[block, p : p + 1, :] = top[:, part : part + 128]
                total_ref[block, p : p + 1, :] = total[:, part : part + 128]
                moment_ref[block, p : p + 1, :] = moment[:, part : part + 128]
        return carry

    lax.fori_loop(0, blocks, one_block, 0, unroll=2)
    own = [groups[i] for i in range(blocks)]
    slots = slots_of(own)
    left = low_lanes((8, 128))
    lane = lax.broadcasted_iota(jnp.int32, (8, 128), 1)
    note = jnp.full((8, 128), -1.0, f32)
    for i in range(blocks):
        note = jnp.where(lane == 64 + slots[i], own[i].astype(f32), note)
    for g in range(8):
        tops = [jnp.where(own[i] == g, top_ref[i], -1e30) for i in range(blocks)]
        top = functools.reduce(jnp.maximum, tops)
        total = jnp.zeros((8, 128), f32)
        moment = jnp.zeros((8, 128), f32)
        for i in range(blocks):
            factor = jnp.where(own[i] == g, jnp.exp(tops[i] - top), 0.0)
            total = total + factor * total_ref[i]
            moment = moment + factor * moment_ref[i]
        parts = (
            (jnp.where(left, top, pltpu.roll(total, 64, 1)), jnp.where(left, moment, note)),
            (
                jnp.where(left, pltpu.roll(top, 64, 1), total),
                jnp.where(left, pltpu.roll(moment, 64, 1), note),
            ),
        )
        for odd in range(2):
            for p in range(8):
                at = 16 * g + 8 * odd + p
                out_ref[at, :, 0:128] = parts[odd][0][p : p + 1]
                out_ref[at, :, 128:256] = parts[odd][1][p : p + 1]
    copies[3].wait()
    copies[4].wait()


def attend(counts, groups, places, pieces, w_query, w_out, pairs):
    rows, width = pieces[0].shape[1:]
    small = jax.ShapeDtypeStruct((groups.shape[0] * rows, width), bf16)
    return pl.pallas_call(
        attend_kernel,
        out_shape=(small, small, jax.ShapeDtypeStruct((128, 1, 256), f32)),
        in_specs=[SMEM] * 3 + [VMEM] * 8 + [HBM] * 3,
        out_specs=(HBM, HBM, VMEM),
        scratch_shapes=[
            pltpu.VMEM((2,) + small.shape, bf16),
            pltpu.VMEM(w_query.shape, bf16),
            pltpu.VMEM(w_out.shape, bf16),
            pltpu.VMEM(pairs.shape, bf16),
            pltpu.VMEM(small.shape, bf16),
            pltpu.VMEM(small.shape, bf16),
        ]
        + [pltpu.VMEM((groups.shape[0], 8, 128), f32)] * 3
        + [pltpu.SemaphoreType.DMA((5,))],
        cost_estimate=pl.CostEstimate(
            flops=6 * 1024 * 1024 * 1024,
            bytes_accessed=10 * 1024 * 1024,
            transcendentals=512 * 1024,
        ),
    )(counts, groups, places, *pieces, w_query, w_out, pairs)


def block_specs(latent_count, width):
    return [
        pl.BlockSpec((PER_STEP * latent_count, width), lambda i: (i, 0)),
        pl.BlockSpec((PER_STEP * latent_count, width), lambda i: (i, 0)),
        pl.BlockSpec((PER_STEP * 128, 2 * width), lambda i: (i, 0)),
    ]


def products_kernel(q_ref, d_ref, pairs_ref, scores_ref, d_weights_ref):
    masks = head_masks()
    width = q_ref.shape[1]
    rows = q_ref.shape[0] // PER_STEP
    scale = (width // H) ** (-0.5)
    for sub in range(PER_STEP):
        here = slice(sub * rows, sub * rows + rows)
        there = slice(sub * 128, sub * 128 + 128)
        for at in range(0, width, WIDE):
            cols = slice(at, at + WIDE)
            value_cols = slice(width + at, width + at + WIDE)
            scores_ref[there, cols] = scale * lax.dot_general(
                pairs_ref[there, cols],
                spread(q_ref[here, cols], masks),
                LAST,
                preferred_element_type=f32,
            )
            d_weights_ref[there, cols] = lax.dot_general(
                pairs_ref[there, value_cols],
                spread(d_ref[here, cols], masks),
                LAST,
                preferred_element_type=f32,
            )


def products(queries, d_mixed, pairs):
    width = queries.shape[1]
    out = jax.ShapeDtypeStruct((pairs.shape[0], width), f32)
    spec = pl.BlockSpec((PER_STEP * 128, width), lambda i: (i, 0))
    return pl.pallas_call(
        products_kernel,
        grid=(4 // PER_STEP,),
        out_shape=(out, out),
        in_specs=block_specs(queries.shape[0] // 4, width),
        out_specs=(spec, spec),
        cost_estimate=pl.CostEstimate(
            flops=2 * 1024 * 1024 * 1024, bytes_accessed=8 * 1024 * 1024, transcendentals=0
        ),
    )(queries, d_mixed, pairs)


def totals_kernel(in_ref, out_ref):
    left = low_lanes((1, 128))
    first = in_ref[:, 0, 0:128]
    top = jnp.max(first, axis=0, keepdims=True)
    top = jnp.where(left, top, pltpu.roll(top, 64, 1))
    factor = jnp.exp(jnp.where(left, first, pltpu.roll(first, 64, 1)) - top)
    total = jnp.sum(factor * first, axis=0, keepdims=True)
    inverse = 1.0 / jnp.where(left, pltpu.roll(total, 64, 1), total)
    delta = jnp.sum(factor * in_ref[:, 0, 128:256], axis=0, keepdims=True) * inverse
    reply = jnp.concatenate(
        [jnp.where(left, top, inverse), jnp.where(left, delta, 0.0)], axis=1
    )
    for at in range(in_ref.shape[0]):
        out_ref[at] = reply


def totals(stats):
    return pl.pallas_call(
        totals_kernel,
        out_shape=jax.ShapeDtypeStruct(stats.shape, f32),
        in_specs=[VMEM],
        out_specs=VMEM,
        compiler_params=room(4),
    )(stats)


def grads_kernel(
    counts,
    groups,
    core,
    q_ref,
    d_ref,
    pairs_ref,
    scores_ref,
    d_weights_ref,
    reply_ref,
    kept_ref,
    sent_ref,
    slotted_ref,
    mixed_acc,
    query_acc,
    mixed_now,
    query_now,
):
    step = pl.program_id(0)
    masks = head_masks()
    width = q_ref.shape[1]
    rows = q_ref.shape[0] // PER_STEP
    scale = (width // H) ** (-0.5)
    position = lax.broadcasted_iota(jnp.int32, (128, WIDE), 0)
    left = low_lanes((8, 128))
    wide = low_lanes((rows, 128))

    @pl.when(step == 0)
    def _():
        mixed_acc[...] = jnp.zeros_like(mixed_acc)
        query_acc[...] = jnp.zeros_like(query_acc)

    def row(pairs, at):
        first = at // 128
        return jnp.concatenate([pairs[p : p + 1] for p in range(first, first + WIDE // 128)], axis=1)

    slots = slots_of([groups[i] for i in range(4)])
    for sub in range(PER_STEP):
        block = step * PER_STEP + sub
        here = slice(sub * rows, sub * rows + rows)
        there = slice(sub * 128, sub * 128 + 128)
        usable = position < counts[block]
        group = groups[block]

        def reply_rows(odd, cols):
            first = 16 * group + 8 * odd
            return jnp.concatenate([reply_ref[first + p, :, cols] for p in range(8)], axis=0)

        even = reply_rows(0, slice(0, 128))
        odd = reply_rows(1, slice(0, 128))
        top = jnp.where(left, even, pltpu.roll(odd, 64, 1))
        inverse = jnp.where(left, pltpu.roll(even, 64, 1), odd)
        delta = jnp.where(
            left, reply_rows(0, slice(128, 256)), pltpu.roll(reply_rows(1, slice(128, 256)), 64, 1)
        )
        for at in range(0, width, WIDE):
            cols = slice(at, at + WIDE)
            value_cols = slice(width + at, width + at + WIDE)
            q = spread(q_ref[here, cols], masks)
            d = spread(d_ref[here, cols], masks)
            k = pairs_ref[there, cols]
            v = pairs_ref[there, value_cols]
            s = scores_ref[there, cols]
            dw = d_weights_ref[there, cols]
            weights = jnp.where(usable, jnp.exp(s - row(top, at)) * row(inverse, at), 0.0)
            weights_b = weights.astype(bf16)
            d_scores = (weights * (dw - row(delta, at)) * scale).astype(bf16)
            d_values = jnp.dot(weights_b, d, preferred_element_type=f32)
            d_keys = jnp.dot(d_scores, q, preferred_element_type=f32)
            kept_ref[there, cols] = jnp.where(core[0] == 0, d_keys, d_values).astype(bf16)
            sent_ref[there, cols] = jnp.where(core[0] == 0, d_values, d_keys).astype(bf16)
            mixed = lax.dot_general(weights_b, v, FIRST, preferred_element_type=f32)
            mixed_now[sub, :, cols] = own_heads(mixed, rows)
            query = lax.dot_general(d_scores, k, FIRST, preferred_element_type=f32)
            query_now[sub, :, cols] = own_heads(query, rows)
    for sub in range(PER_STEP):
        slot = slots[sub]
        for at in range(1, 4 // PER_STEP):
            slot = jnp.where(step == at, slots[at * PER_STEP + sub], slot)
        mixed_acc[slot] += mixed_now[sub]
        query_acc[slot] += query_now[sub]

    @pl.when(step == 4 // PER_STEP - 1)
    def _():
        for at in range(SLOTS):
            for p in range(width // 128):
                cols = slice(128 * p, 128 * p + 128)
                mixed = mixed_acc[at, :, cols]
                query = query_acc[at, :, cols]
                slotted_ref[2 * p, at] = jnp.where(
                    wide, mixed, pltpu.roll(query, 64, 1)
                ).astype(bf16)
                slotted_ref[2 * p + 1, at] = jnp.where(
                    wide, pltpu.roll(mixed, 64, 1), query
                ).astype(bf16)


def gradients(counts, groups, core, queries, d_mixed, pairs, scores, d_weights, reply):
    width = queries.shape[1]
    rows = queries.shape[0] // 4
    return pl.pallas_call(
        grads_kernel,
        grid=(4 // PER_STEP,),
        out_shape=(
            jax.ShapeDtypeStruct((pairs.shape[0], width), bf16),
            jax.ShapeDtypeStruct((pairs.shape[0], width), bf16),
            jax.ShapeDtypeStruct((H, SLOTS, rows, 128), bf16),
        ),
        in_specs=[SMEM, SMEM, SMEM]
        + block_specs(rows, width)
        + [pl.BlockSpec((PER_STEP * 128, width), lambda i: (i, 0))] * 2
        + [pl.BlockSpec((128, 1, 256), lambda i: (0, 0, 0))],
        out_specs=(
            pl.BlockSpec((PER_STEP * 128, width), lambda i: (i, 0)),
            pl.BlockSpec((PER_STEP * 128, width), lambda i: (i, 0)),
            pl.BlockSpec((H, SLOTS, rows, 128), lambda i: (0, 0, 0, 0)),
        ),
        scratch_shapes=[pltpu.VMEM((SLOTS, rows, width), f32)] * 2
        + [pltpu.VMEM((PER_STEP, rows, width), f32)] * 2,
        cost_estimate=pl.CostEstimate(
            flops=8 * 1024 * 1024 * 1024, bytes_accessed=8 * 1024 * 1024, transcendentals=512 * 1024
        ),
    )(counts, groups, core, queries, d_mixed, pairs, scores, d_weights, reply)


def prepare_kernel(owners, *refs):
    pieces, (latents_ref, d_out_ref) = refs[:8], refs[8:]
    rows = pieces[0].shape[1]
    for j in range(8):
        at = pl.ds(pl.multiple_of(owners[j] * rows, rows), rows)
        latents_ref[at, :] = normalize(pieces[j][0])
        d_out_ref[at, :] = pieces[j][1]


def prepare(owners, pieces):
    rows, width = pieces[0].shape[1:]
    out = jax.ShapeDtypeStruct((8 * rows, width), bf16)
    return pl.pallas_call(
        prepare_kernel,
        out_shape=(out, out),
        in_specs=[SMEM] + [VMEM] * 8,
        out_specs=(VMEM, VMEM),
        cost_estimate=pl.CostEstimate(
            flops=4 * 1024 * 1024, bytes_accessed=4 * 1024 * 1024, transcendentals=512
        ),
    )(owners, *pieces)


def owners_kernel(heads_ref, owned_ref, latents_ref, out_ref):
    rows = owned_ref.shape[0]
    query = lax.dot_general(
        latents_ref[...], heads_ref[...], FIRST, preferred_element_type=f32
    )
    other = pltpu.roll(query, 64, 1)
    half = rows // 2
    left = low_lanes((half, 128))
    for at in range(H):
        first, second = rows * at, rows * at + half
        out_ref[at, :rows] = owned_ref[...]
        out_ref[at, rows:] = jnp.where(
            left, other[first : first + half], query[second : second + half]
        ).astype(bf16)


def owners(heads, owned, normed_latents):
    rows = owned.shape[0]
    return pl.pallas_call(
        owners_kernel,
        out_shape=jax.ShapeDtypeStruct((H, rows + rows // 2, 128), bf16),
        in_specs=[VMEM] * 3,
        out_specs=VMEM,
        cost_estimate=pl.CostEstimate(
            flops=256 * 1024 * 1024, bytes_accessed=2 * 1024 * 1024, transcendentals=0
        ),
    )(heads, owned, normed_latents)


def finish_kernel(in_ref, latent_ref, d_out_ref, w_query_ref, w_out_in, *refs):
    out_ref, d_latents_ref, grad_query_ref, mixed, d_query, w_out_ref, sem = refs
    copy = pltpu.make_async_copy(w_out_in, w_out_ref, sem)
    copy.start()
    rows = latent_ref.shape[0]
    left = low_lanes((rows, 128))

    def parts(head):
        both = in_ref[head, rows:].astype(f32)
        return in_ref[head, :rows].astype(f32), both, pltpu.roll(both, 64, 1)

    for p in range(H // 2):
        cols = slice(128 * p, 128 * p + 128)
        even, even_grad, even_turned = parts(2 * p)
        odd, odd_grad, odd_turned = parts(2 * p + 1)
        mixed[:, cols] = jnp.where(left, even, pltpu.roll(odd, 64, 1)).astype(bf16)
        d_query[:, cols] = jnp.where(left, pltpu.roll(even, 64, 1), odd).astype(bf16)
        half = rows // 2
        narrow = left[:half]
        grad_query_ref[:half, cols] = jnp.where(narrow, even_grad, odd_turned)
        grad_query_ref[half:, cols] = jnp.where(narrow, even_turned, odd_grad)
    latent = latent_ref[...].astype(f32)
    d_normed = lax.dot_general(d_query[...], w_query_ref[...], LAST, preferred_element_type=f32)
    d_latents_ref[...] = (d_out_ref[...].astype(f32) + rms_back(latent, d_normed)).astype(bf16)
    copy.wait()
    update = jnp.dot(mixed[...], w_out_ref[...], preferred_element_type=f32)
    out_ref[...] = (latent + update).astype(bf16)


def finish(over_seq, latent, d_out, w_query, w_out):
    rows, width = latent.shape
    small = jax.ShapeDtypeStruct((rows, width), bf16)
    return pl.pallas_call(
        finish_kernel,
        out_shape=(small, small, jax.ShapeDtypeStruct((rows, width), f32)),
        in_specs=[VMEM] * 4 + [HBM],
        out_specs=(VMEM,) * 3,
        compiler_params=room(12),
        scratch_shapes=[pltpu.VMEM((rows, width), bf16)] * 2
        + [pltpu.VMEM(w_out.shape, bf16), pltpu.SemaphoreType.DMA],
    )(over_seq, latent, d_out, w_query, w_out)


def local(latents, frames, counts, groups, w_query, w_kv, w_out, d_out):
    blocks, block_rows, feature = frames.shape
    latent_count, model_width = latents.shape[1:]
    head_dim = model_width // H
    group_count, seq_count = 8, 16
    rows = blocks * block_rows
    core = lax.axis_index("core")
    batch_at = lax.axis_index(BATCH)

    near = along_chips(pair_up(latents, d_out))
    normed, pairs = project_pairs(frames.reshape(rows, feature), w_kv)
    sources = jnp.stack([group_at(j) for j in range(8)])
    places = place_of(groups)
    near = [lax.optimization_barrier((piece, normed, pairs))[0] for piece in near]
    near[0], sources, places = lax.optimization_barrier((near[0], sources, places))
    pieces = near + [other_core(piece) for piece in near]
    queries, d_mixed, stats = attend(
        counts, groups, places, pieces, w_query, w_out, pairs
    )
    normed, stats, queries, d_mixed = lax.optimization_barrier((normed, stats, queries, d_mixed))
    scores, d_weights = products(queries, d_mixed, pairs)
    normed = jnp.concatenate([normed, other_core(normed)], axis=0)
    stats = exchange(stats, ALL)
    source_groups = lax.dynamic_slice(
        stats, (batch_at * seq_count, 0, 192), (seq_count, 1, SLOTS)
    )
    chosen = (
        jnp.arange(group_count, dtype=f32)[:, None, None] == source_groups.reshape(1, seq_count, SLOTS)
    ).astype(bf16)
    reply, sources = lax.optimization_barrier((totals(stats), sources))
    all_latents, all_d_out = prepare(sources, pieces)
    reply = exchange(reply, ALL)
    reply, all_latents, all_d_out, normed, chosen, scores, d_weights = lax.optimization_barrier(
        (reply, all_latents, all_d_out, normed, chosen, scores, d_weights)
    )
    kept, sent, slotted = gradients(
        counts, groups, core.reshape(1), queries, d_mixed, pairs, scores, d_weights, reply
    )
    slotted = exchange(slotted, SEQ)

    d_half = jnp.concatenate([kept, other_core(sent)], axis=0)
    term = lax.dot_general(normed, d_half, FIRST, preferred_element_type=f32).astype(bf16)
    share_rows = feature // 128
    term = term.reshape(group_count, 4, 4 * share_rows, 8, 128)
    z_at = lax.axis_index("z")

    def z_part(step):
        return lax.dynamic_index_in_dim(term, lax.rem(z_at + step, 4), 1, False)

    parts = lax.optimization_barrier([z_part(step) for step in range(4)])
    got = [ring_step(parts[step], "z", step) for step in range(1, 4)]
    by_group = jnp.einsum("gsk,sklc->glc", chosen, slotted, preferred_element_type=f32)
    by_group = exchange(by_group.astype(bf16), BATCH).astype(f32)
    owned = jnp.sum(by_group, axis=0).astype(bf16)
    heads = share(owned, BATCH, group_count).reshape(group_count * latent_count, 128)
    owned_parts = owners(heads, owned, all_latents)
    owned_parts, got[1] = lax.optimization_barrier((owned_parts, got[1]))
    ring_sum = sum([part.astype(f32) for part in got], parts[0].astype(f32))
    ring_sum = ring_sum.astype(bf16).reshape(group_count, 4, share_rows, 8, 128)
    ring_sum = ring_sum.reshape(4 * group_count, share_rows, 8, 128)
    over_seq = exchange(owned_parts, SEQ)
    ring_sum, over_seq = lax.optimization_barrier((ring_sum, over_seq))
    ring_sum = exchange(ring_sum, BATCH + ("y",))
    grad_outproj = lax.dot_general(
        heads[:, :head_dim], all_d_out, FIRST, preferred_element_type=f32
    )
    out, d_latents, grad_query = finish(over_seq, latents[0], d_out[0], w_query, w_out)
    ring_sum, out, d_latents, grad_query, grad_outproj = lax.optimization_barrier(
        (ring_sum, out, d_latents, grad_query, grad_outproj)
    )
    ring_sum = ring_sum.reshape(4, 2, 4, share_rows, 8, 128).astype(f32)
    halves = jnp.sum(ring_sum, axis=(0, 2)).reshape(2, share_rows, model_width)
    grad_kv = jnp.concatenate([halves[0], halves[1]], axis=1)
    return (out[None], d_latents[None], grad_query, grad_outproj, grad_kv)


def solution(mesh):
    chips = Mesh(mesh.devices.reshape(4, 2, 4, 4), ("x", "core", "z", "y"))
    in_specs = (
        P(BATCH, None, None),
        P(ALL, None, None),
        P(ALL),
        P(ALL),
        P(),
        P(),
        P(),
        P(BATCH, None, None),
    )
    out_specs = (
        P(BATCH, None, None),
        P(BATCH, None, None),
        P(SEQ, None),
        P(SEQ, None),
        P(ALL, None),
    )
    return jax.shard_map(local, mesh=chips, in_specs=in_specs, out_specs=out_specs, check_vma=False)
```

```python
import functools

import jax
import jax.numpy as jnp
from jax import lax
from jax.experimental import pallas as pl
from jax.experimental.pallas import tpu as pltpu
from jax.sharding import Mesh, PartitionSpec as P

H = 16
BATCH = ("x", "core")
SEQ = ("z", "y")
CHIPS = ("x", "z", "y")
ALL = BATCH + SEQ
SLOTS = 3
WIDE = 256
PER_STEP = 2

epsilon = 1e-06
f32 = jnp.float32
bf16 = jnp.bfloat16


def rms_rows(values):
    return values * lax.rsqrt(jnp.mean(values * values, axis=-1, keepdims=True) + epsilon)


def rms_back(values, grads):
    factor = lax.rsqrt(jnp.mean(values * values, axis=-1, keepdims=True) + epsilon)
    normed = values * factor
    return factor * (grads - normed * jnp.mean(grads * normed, axis=-1, keepdims=True))


def normalize(values):
    return rms_rows(values.astype(f32)).astype(bf16)


def exchange(values, axes):
    return lax.all_to_all(values, axes, 0, 0, tiled=True)


def share(values, axes, count):
    return exchange(jnp.broadcast_to(values[None], (count,) + values.shape), axes)


def other_core(values):
    return lax.ppermute(values, "core", [(0, 1), (1, 0)])


def ring_step(values, axis, step):
    return lax.ppermute(values, axis, [(i, (i + step) % 4) for i in range(4)])


def chip_step(values, step):
    return ring_step(values, "x", step)


def along_chips(values):
    return [values, chip_step(values, 1), chip_step(values, 2), chip_step(values, 3)]


def place_of(group):
    chip = lax.rem(lax.axis_index("x") - group // 2 + 4, 4)
    return jnp.where(group % 2 == lax.axis_index("core"), 0, 4) + chip


def group_at(place):
    chip = lax.rem(lax.axis_index("x") - place % 4 + 4, 4)
    core = lax.axis_index("core")
    return 2 * chip + (core if place < 4 else 1 - core)


SMEM = pl.BlockSpec(memory_space=pltpu.SMEM)
VMEM = pl.BlockSpec(memory_space=pltpu.VMEM)
HBM = pl.BlockSpec(memory_space=pltpu.HBM)
LAST = (((1,), (1,)), ((), ()))
FIRST = (((0,), (0,)), ((), ()))


def room(mebibytes):
    return pltpu.CompilerParams(vmem_limit_bytes=mebibytes * 1024 * 1024)


def pairs_kernel(frames_ref, w_ref, normed_ref, out_ref):
    @pl.when(pl.program_id(0) == 0)
    def _():
        normed_ref[...] = normalize(frames_ref[...])

    out_ref[...] = jnp.dot(normed_ref[...], w_ref[...], preferred_element_type=f32).astype(bf16)


def pair_up_kernel(first_ref, second_ref, out_ref):
    out_ref[0:1] = first_ref[...]
    out_ref[1:2] = second_ref[...]


def pair_up(first, second):
    return pl.pallas_call(
        pair_up_kernel,
        out_shape=jax.ShapeDtypeStruct((2,) + first.shape[1:], first.dtype),
        in_specs=[VMEM, VMEM],
        out_specs=VMEM,
        cost_estimate=pl.CostEstimate(flops=0, bytes_accessed=512 * 1024, transcendentals=0),
    )(first, second)


def project_pairs(frames, w_kv):
    rows, feature = frames.shape
    width, tile = w_kv.shape[1], 1024
    return pl.pallas_call(
        pairs_kernel,
        grid=(width // tile,),
        out_shape=(
            jax.ShapeDtypeStruct((rows, feature), bf16),
            jax.ShapeDtypeStruct((rows, width), bf16),
        ),
        in_specs=[
            pl.BlockSpec((rows, feature), lambda i: (0, 0)),
            pl.BlockSpec((feature, tile), lambda i: (0, i)),
        ],
        out_specs=(
            pl.BlockSpec((rows, feature), lambda i: (0, 0)),
            pl.BlockSpec((rows, tile), lambda i: (0, i)),
        ),
        cost_estimate=pl.CostEstimate(
            flops=2 * rows * feature * width, bytes_accessed=9 * 1024 * 1024, transcendentals=0
        ),
    )(frames, w_kv)


def low_lanes(shape):
    return lax.broadcasted_iota(jnp.int32, shape, len(shape) - 1) < 64


def spread(heads, masks):
    return jnp.concatenate([heads * mask for mask in masks], axis=0)


def head_masks():
    head = lax.broadcasted_iota(jnp.int32, (1, WIDE), 1) // 64
    return [jnp.where(head == at, 1.0, 0.0).astype(bf16) for at in range(WIDE // 64)]


def own_heads(product, rows):
    head = lax.broadcasted_iota(jnp.int32, (rows, WIDE), 1) // 64
    result = product[:rows]
    for at in range(1, WIDE // 64):
        result = jnp.where(head == at, product[at * rows : at * rows + rows], result)
    return result


def slots_of(groups):
    slots, used = [0], 1
    for i in range(1, 4):
        slot = used
        fresh = True
        for j in reversed(range(i)):
            slot = jnp.where(groups[i] == groups[j], slots[j], slot)
            fresh = fresh & (groups[i] != groups[j])
        slots.append(slot)
        used = used + jnp.where(fresh, 1, 0)
    return slots


def attend_kernel(counts, groups, places, *refs):
    pieces, (wq_in, wo_in, pairs_in, q_out, d_out, out_ref), scratch = refs[:8], refs[8:14], refs[14:]
    picked, wq, wo, pairs_ref, q_ref, d_ref, top_ref, total_ref, moment_ref, sems = scratch
    copies = [
        pltpu.make_async_copy(wq_in, wq, sems.at[0]),
        pltpu.make_async_copy(wo_in, wo, sems.at[1]),
        pltpu.make_async_copy(pairs_in, pairs_ref, sems.at[2]),
        pltpu.make_async_copy(q_ref, q_out, sems.at[3]),
        pltpu.make_async_copy(d_ref, d_out, sems.at[4]),
    ]
    for copy in copies[:3]:
        copy.start()
    rows, width = pieces[0].shape[1:]
    blocks = q_ref.shape[0] // rows
    for i in range(blocks):
        for j in range(8):

            @pl.when(places[i] == j)
            def _():
                picked[0, i * rows : (i + 1) * rows, :] = normalize(pieces[j][0])
                picked[1, i * rows : (i + 1) * rows, :] = pieces[j][1]

    copies[0].wait()
    for at in range(0, width, 256):
        tile = slice(at, at + 256)
        q_ref[:, tile] = jnp.dot(picked[0], wq[:, tile], preferred_element_type=f32).astype(bf16)
    copies[3].start()
    copies[1].wait()
    for at in range(0, width, 256):
        tile = slice(at, at + 256)
        d_ref[:, tile] = lax.dot_general(
            picked[1], wo[tile, :], LAST, preferred_element_type=f32
        ).astype(bf16)
    copies[4].start()
    copies[2].wait()

    masks = head_masks()
    scale = (width // H) ** (-0.5)
    position = lax.broadcasted_iota(jnp.int32, (128, WIDE), 0)

    def one_block(block, carry):
        usable = position < counts[block]
        here = pl.ds(pl.multiple_of(block * rows, rows), rows)
        there = pl.ds(pl.multiple_of(block * 128, 128), 128)
        for at in range(0, width, WIDE):
            cols = slice(at, at + WIDE)
            value_cols = slice(width + at, width + at + WIDE)
            s = lax.dot_general(
                pairs_ref[there, cols],
                spread(q_ref[here, cols], masks),
                LAST,
                preferred_element_type=f32,
            )
            s = jnp.where(usable, s * scale, -1e30)
            top = jnp.max(s, axis=0, keepdims=True)
            raw = jnp.where(usable, jnp.exp(s - top), 0.0)
            dw = lax.dot_general(
                pairs_ref[there, value_cols],
                spread(d_ref[here, cols], masks),
                LAST,
                preferred_element_type=f32,
            )
            total = jnp.sum(raw, axis=0, keepdims=True)
            moment = jnp.sum(raw * dw, axis=0, keepdims=True)
            for part in range(0, WIDE, 128):
                p = (at + part) // 128
                top_ref[block, p : p + 1, :] = top[:, part : part + 128]
                total_ref[block, p : p + 1, :] = total[:, part : part + 128]
                moment_ref[block, p : p + 1, :] = moment[:, part : part + 128]
        return carry

    lax.fori_loop(0, blocks, one_block, 0, unroll=2)
    own = [groups[i] for i in range(blocks)]
    slots = slots_of(own)
    left = low_lanes((8, 128))
    lane = lax.broadcasted_iota(jnp.int32, (8, 128), 1)
    note = jnp.full((8, 128), -1.0, f32)
    for i in range(blocks):
        note = jnp.where(lane == 64 + slots[i], own[i].astype(f32), note)
    for g in range(8):
        tops = [jnp.where(own[i] == g, top_ref[i], -1e30) for i in range(blocks)]
        top = functools.reduce(jnp.maximum, tops)
        total = jnp.zeros((8, 128), f32)
        moment = jnp.zeros((8, 128), f32)
        for i in range(blocks):
            factor = jnp.where(own[i] == g, jnp.exp(tops[i] - top), 0.0)
            total = total + factor * total_ref[i]
            moment = moment + factor * moment_ref[i]
        parts = (
            (jnp.where(left, top, pltpu.roll(total, 64, 1)), jnp.where(left, moment, note)),
            (
                jnp.where(left, pltpu.roll(top, 64, 1), total),
                jnp.where(left, pltpu.roll(moment, 64, 1), note),
            ),
        )
        for odd in range(2):
            for p in range(8):
                at = 16 * g + 8 * odd + p
                out_ref[at, :, 0:128] = parts[odd][0][p : p + 1]
                out_ref[at, :, 128:256] = parts[odd][1][p : p + 1]
    copies[3].wait()
    copies[4].wait()


def attend(counts, groups, places, pieces, w_query, w_out, pairs):
    rows, width = pieces[0].shape[1:]
    small = jax.ShapeDtypeStruct((groups.shape[0] * rows, width), bf16)
    return pl.pallas_call(
        attend_kernel,
        out_shape=(small, small, jax.ShapeDtypeStruct((128, 1, 256), f32)),
        in_specs=[SMEM] * 3 + [VMEM] * 8 + [HBM] * 3,
        out_specs=(HBM, HBM, VMEM),
        scratch_shapes=[
            pltpu.VMEM((2,) + small.shape, bf16),
            pltpu.VMEM(w_query.shape, bf16),
            pltpu.VMEM(w_out.shape, bf16),
            pltpu.VMEM(pairs.shape, bf16),
            pltpu.VMEM(small.shape, bf16),
            pltpu.VMEM(small.shape, bf16),
        ]
        + [pltpu.VMEM((groups.shape[0], 8, 128), f32)] * 3
        + [pltpu.SemaphoreType.DMA((5,))],
        cost_estimate=pl.CostEstimate(
            flops=6 * 1024 * 1024 * 1024,
            bytes_accessed=10 * 1024 * 1024,
            transcendentals=512 * 1024,
        ),
    )(counts, groups, places, *pieces, w_query, w_out, pairs)


def block_specs(latent_count, width):
    return [
        pl.BlockSpec((PER_STEP * latent_count, width), lambda i: (i, 0)),
        pl.BlockSpec((PER_STEP * latent_count, width), lambda i: (i, 0)),
        pl.BlockSpec((PER_STEP * 128, 2 * width), lambda i: (i, 0)),
    ]


def products_kernel(q_ref, d_ref, pairs_ref, scores_ref, d_weights_ref):
    masks = head_masks()
    width = q_ref.shape[1]
    rows = q_ref.shape[0] // PER_STEP
    scale = (width // H) ** (-0.5)
    for sub in range(PER_STEP):
        here = slice(sub * rows, sub * rows + rows)
        there = slice(sub * 128, sub * 128 + 128)
        for at in range(0, width, WIDE):
            cols = slice(at, at + WIDE)
            value_cols = slice(width + at, width + at + WIDE)
            scores_ref[there, cols] = scale * lax.dot_general(
                pairs_ref[there, cols],
                spread(q_ref[here, cols], masks),
                LAST,
                preferred_element_type=f32,
            )
            d_weights_ref[there, cols] = lax.dot_general(
                pairs_ref[there, value_cols],
                spread(d_ref[here, cols], masks),
                LAST,
                preferred_element_type=f32,
            )


def products(queries, d_mixed, pairs):
    width = queries.shape[1]
    out = jax.ShapeDtypeStruct((pairs.shape[0], width), f32)
    spec = pl.BlockSpec((PER_STEP * 128, width), lambda i: (i, 0))
    return pl.pallas_call(
        products_kernel,
        grid=(4 // PER_STEP,),
        out_shape=(out, out),
        in_specs=block_specs(queries.shape[0] // 4, width),
        out_specs=(spec, spec),
        cost_estimate=pl.CostEstimate(
            flops=2 * 1024 * 1024 * 1024, bytes_accessed=8 * 1024 * 1024, transcendentals=0
        ),
    )(queries, d_mixed, pairs)


def totals_kernel(in_ref, out_ref):
    left = low_lanes((1, 128))
    first = in_ref[:, 0, 0:128]
    top = jnp.max(first, axis=0, keepdims=True)
    top = jnp.where(left, top, pltpu.roll(top, 64, 1))
    factor = jnp.exp(jnp.where(left, first, pltpu.roll(first, 64, 1)) - top)
    total = jnp.sum(factor * first, axis=0, keepdims=True)
    inverse = 1.0 / jnp.where(left, pltpu.roll(total, 64, 1), total)
    delta = jnp.sum(factor * in_ref[:, 0, 128:256], axis=0, keepdims=True) * inverse
    reply = jnp.concatenate(
        [jnp.where(left, top, inverse), jnp.where(left, delta, 0.0)], axis=1
    )
    for at in range(in_ref.shape[0]):
        out_ref[at] = reply


def totals(stats):
    return pl.pallas_call(
        totals_kernel,
        out_shape=jax.ShapeDtypeStruct(stats.shape, f32),
        in_specs=[VMEM],
        out_specs=VMEM,
        compiler_params=room(4),
    )(stats)


def grads_kernel(
    counts,
    groups,
    core,
    q_ref,
    d_ref,
    pairs_ref,
    scores_ref,
    d_weights_ref,
    reply_ref,
    kept_ref,
    sent_ref,
    slotted_ref,
    mixed_acc,
    query_acc,
    mixed_now,
    query_now,
):
    step = pl.program_id(0)
    masks = head_masks()
    width = q_ref.shape[1]
    rows = q_ref.shape[0] // PER_STEP
    scale = (width // H) ** (-0.5)
    position = lax.broadcasted_iota(jnp.int32, (128, WIDE), 0)
    left = low_lanes((8, 128))
    wide = low_lanes((rows, 128))

    @pl.when(step == 0)
    def _():
        mixed_acc[...] = jnp.zeros_like(mixed_acc)
        query_acc[...] = jnp.zeros_like(query_acc)

    def row(pairs, at):
        first = at // 128
        return jnp.concatenate([pairs[p : p + 1] for p in range(first, first + WIDE // 128)], axis=1)

    slots = slots_of([groups[i] for i in range(4)])
    for sub in range(PER_STEP):
        block = step * PER_STEP + sub
        here = slice(sub * rows, sub * rows + rows)
        there = slice(sub * 128, sub * 128 + 128)
        usable = position < counts[block]
        group = groups[block]

        def reply_rows(odd, cols):
            first = 16 * group + 8 * odd
            return jnp.concatenate([reply_ref[first + p, :, cols] for p in range(8)], axis=0)

        even = reply_rows(0, slice(0, 128))
        odd = reply_rows(1, slice(0, 128))
        top = jnp.where(left, even, pltpu.roll(odd, 64, 1))
        inverse = jnp.where(left, pltpu.roll(even, 64, 1), odd)
        delta = jnp.where(
            left, reply_rows(0, slice(128, 256)), pltpu.roll(reply_rows(1, slice(128, 256)), 64, 1)
        )
        for at in range(0, width, WIDE):
            cols = slice(at, at + WIDE)
            value_cols = slice(width + at, width + at + WIDE)
            q = spread(q_ref[here, cols], masks)
            d = spread(d_ref[here, cols], masks)
            k = pairs_ref[there, cols]
            v = pairs_ref[there, value_cols]
            s = scores_ref[there, cols]
            dw = d_weights_ref[there, cols]
            weights = jnp.where(usable, jnp.exp(s - row(top, at)) * row(inverse, at), 0.0)
            weights_b = weights.astype(bf16)
            d_scores = (weights * (dw - row(delta, at)) * scale).astype(bf16)
            d_values = jnp.dot(weights_b, d, preferred_element_type=f32)
            d_keys = jnp.dot(d_scores, q, preferred_element_type=f32)
            kept_ref[there, cols] = jnp.where(core[0] == 0, d_keys, d_values).astype(bf16)
            sent_ref[there, cols] = jnp.where(core[0] == 0, d_values, d_keys).astype(bf16)
            mixed = lax.dot_general(weights_b, v, FIRST, preferred_element_type=f32)
            mixed_now[sub, :, cols] = own_heads(mixed, rows)
            query = lax.dot_general(d_scores, k, FIRST, preferred_element_type=f32)
            query_now[sub, :, cols] = own_heads(query, rows)
    for sub in range(PER_STEP):
        slot = slots[sub]
        for at in range(1, 4 // PER_STEP):
            slot = jnp.where(step == at, slots[at * PER_STEP + sub], slot)
        mixed_acc[slot] += mixed_now[sub]
        query_acc[slot] += query_now[sub]

    @pl.when(step == 4 // PER_STEP - 1)
    def _():
        for at in range(SLOTS):
            for p in range(width // 128):
                cols = slice(128 * p, 128 * p + 128)
                mixed = mixed_acc[at, :, cols]
                query = query_acc[at, :, cols]
                slotted_ref[2 * p, at] = jnp.where(
                    wide, mixed, pltpu.roll(query, 64, 1)
                ).astype(bf16)
                slotted_ref[2 * p + 1, at] = jnp.where(
                    wide, pltpu.roll(mixed, 64, 1), query
                ).astype(bf16)


def gradients(counts, groups, core, queries, d_mixed, pairs, scores, d_weights, reply):
    width = queries.shape[1]
    rows = queries.shape[0] // 4
    return pl.pallas_call(
        grads_kernel,
        grid=(4 // PER_STEP,),
        out_shape=(
            jax.ShapeDtypeStruct((pairs.shape[0], width), bf16),
            jax.ShapeDtypeStruct((pairs.shape[0], width), bf16),
            jax.ShapeDtypeStruct((H, SLOTS, rows, 128), bf16),
        ),
        in_specs=[SMEM, SMEM, SMEM]
        + block_specs(rows, width)
        + [pl.BlockSpec((PER_STEP * 128, width), lambda i: (i, 0))] * 2
        + [pl.BlockSpec((128, 1, 256), lambda i: (0, 0, 0))],
        out_specs=(
            pl.BlockSpec((PER_STEP * 128, width), lambda i: (i, 0)),
            pl.BlockSpec((PER_STEP * 128, width), lambda i: (i, 0)),
            pl.BlockSpec((H, SLOTS, rows, 128), lambda i: (0, 0, 0, 0)),
        ),
        scratch_shapes=[pltpu.VMEM((SLOTS, rows, width), f32)] * 2
        + [pltpu.VMEM((PER_STEP, rows, width), f32)] * 2,
        cost_estimate=pl.CostEstimate(
            flops=8 * 1024 * 1024 * 1024, bytes_accessed=8 * 1024 * 1024, transcendentals=512 * 1024
        ),
    )(counts, groups, core, queries, d_mixed, pairs, scores, d_weights, reply)


def prepare_kernel(owners, *refs):
    pieces, (latents_ref, d_out_ref) = refs[:8], refs[8:]
    rows = pieces[0].shape[1]
    for j in range(8):
        at = pl.ds(pl.multiple_of(owners[j] * rows, rows), rows)
        latents_ref[at, :] = normalize(pieces[j][0])
        d_out_ref[at, :] = pieces[j][1]


def prepare(owners, pieces):
    rows, width = pieces[0].shape[1:]
    out = jax.ShapeDtypeStruct((8 * rows, width), bf16)
    return pl.pallas_call(
        prepare_kernel,
        out_shape=(out, out),
        in_specs=[SMEM] + [VMEM] * 8,
        out_specs=(VMEM, VMEM),
        cost_estimate=pl.CostEstimate(
            flops=4 * 1024 * 1024, bytes_accessed=4 * 1024 * 1024, transcendentals=512
        ),
    )(owners, *pieces)


def owners_kernel(heads_ref, owned_ref, latents_ref, out_ref):
    rows = owned_ref.shape[0]
    query = lax.dot_general(
        latents_ref[...], heads_ref[...], FIRST, preferred_element_type=f32
    )
    other = pltpu.roll(query, 64, 1)
    half = rows // 2
    left = low_lanes((half, 128))
    for at in range(H):
        first, second = rows * at, rows * at + half
        out_ref[at, :rows] = owned_ref[...]
        out_ref[at, rows:] = jnp.where(
            left, other[first : first + half], query[second : second + half]
        ).astype(bf16)


def owners(heads, owned, normed_latents):
    rows = owned.shape[0]
    return pl.pallas_call(
        owners_kernel,
        out_shape=jax.ShapeDtypeStruct((H, rows + rows // 2, 128), bf16),
        in_specs=[VMEM] * 3,
        out_specs=VMEM,
        compiler_params=room(12),
        cost_estimate=pl.CostEstimate(
            flops=256 * 1024 * 1024, bytes_accessed=2 * 1024 * 1024, transcendentals=0
        ),
    )(heads, owned, normed_latents)


def finish_kernel(in_ref, latent_ref, d_out_ref, w_query_ref, w_out_in, *refs):
    out_ref, d_latents_ref, grad_query_ref, mixed, d_query, w_out_ref, sem = refs
    copy = pltpu.make_async_copy(w_out_in, w_out_ref, sem)
    copy.start()
    rows = latent_ref.shape[0]
    left = low_lanes((rows, 128))

    def parts(head):
        both = in_ref[head, rows:].astype(f32)
        return in_ref[head, :rows].astype(f32), both, pltpu.roll(both, 64, 1)

    for p in range(H // 2):
        cols = slice(128 * p, 128 * p + 128)
        even, even_grad, even_turned = parts(2 * p)
        odd, odd_grad, odd_turned = parts(2 * p + 1)
        mixed[:, cols] = jnp.where(left, even, pltpu.roll(odd, 64, 1)).astype(bf16)
        d_query[:, cols] = jnp.where(left, pltpu.roll(even, 64, 1), odd).astype(bf16)
        half = rows // 2
        narrow = left[:half]
        grad_query_ref[:half, cols] = jnp.where(narrow, even_grad, odd_turned)
        grad_query_ref[half:, cols] = jnp.where(narrow, even_turned, odd_grad)
    latent = latent_ref[...].astype(f32)
    d_normed = lax.dot_general(d_query[...], w_query_ref[...], LAST, preferred_element_type=f32)
    d_latents_ref[...] = (d_out_ref[...].astype(f32) + rms_back(latent, d_normed)).astype(bf16)
    copy.wait()
    update = jnp.dot(mixed[...], w_out_ref[...], preferred_element_type=f32)
    out_ref[...] = (latent + update).astype(bf16)


def finish(over_seq, latent, d_out, w_query, w_out):
    rows, width = latent.shape
    small = jax.ShapeDtypeStruct((rows, width), bf16)
    return pl.pallas_call(
        finish_kernel,
        out_shape=(small, small, jax.ShapeDtypeStruct((rows, width), f32)),
        in_specs=[VMEM] * 4 + [HBM],
        out_specs=(VMEM,) * 3,
        compiler_params=room(12),
        scratch_shapes=[pltpu.VMEM((rows, width), bf16)] * 2
        + [pltpu.VMEM(w_out.shape, bf16), pltpu.SemaphoreType.DMA],
    )(over_seq, latent, d_out, w_query, w_out)


def local(latents, frames, counts, groups, w_query, w_kv, w_out, d_out):
    blocks, block_rows, feature = frames.shape
    latent_count, model_width = latents.shape[1:]
    head_dim = model_width // H
    group_count, seq_count = 8, 16
    rows = blocks * block_rows
    core = lax.axis_index("core")
    batch_at = lax.axis_index(BATCH)

    near = along_chips(pair_up(latents, d_out))
    normed, pairs = project_pairs(frames.reshape(rows, feature), w_kv)
    sources = jnp.stack([group_at(j) for j in range(8)])
    places = place_of(groups)
    near = [lax.optimization_barrier((piece, normed, pairs))[0] for piece in near]
    near[0], sources, places = lax.optimization_barrier((near[0], sources, places))
    pieces = near + [other_core(piece) for piece in near]
    queries, d_mixed, stats = attend(
        counts, groups, places, pieces, w_query, w_out, pairs
    )
    normed, stats, queries, d_mixed = lax.optimization_barrier((normed, stats, queries, d_mixed))
    scores, d_weights = products(queries, d_mixed, pairs)
    normed = jnp.concatenate([normed, other_core(normed)], axis=0)
    stats = exchange(stats, ALL)
    source_groups = lax.dynamic_slice(
        stats, (batch_at * seq_count, 0, 192), (seq_count, 1, SLOTS)
    )
    chosen = (
        jnp.arange(group_count, dtype=f32)[:, None, None] == source_groups.reshape(1, seq_count, SLOTS)
    ).astype(bf16)
    reply, sources = lax.optimization_barrier((totals(stats), sources))
    all_latents, all_d_out = prepare(sources, pieces)
    reply = exchange(reply, ALL)
    reply, all_latents, all_d_out, normed, chosen, scores, d_weights = lax.optimization_barrier(
        (reply, all_latents, all_d_out, normed, chosen, scores, d_weights)
    )
    kept, sent, slotted = gradients(
        counts, groups, core.reshape(1), queries, d_mixed, pairs, scores, d_weights, reply
    )
    slotted = exchange(slotted, SEQ)

    d_half = jnp.concatenate([kept, other_core(sent)], axis=0)
    term = lax.dot_general(normed, d_half, FIRST, preferred_element_type=f32).astype(bf16)
    share_rows = feature // 128
    term = term.reshape(group_count, 4, 4 * share_rows, 8, 128)
    z_at = lax.axis_index("z")

    def z_part(step):
        return lax.dynamic_index_in_dim(term, lax.rem(z_at + step, 4), 1, False)

    parts = lax.optimization_barrier([z_part(step) for step in range(4)])
    got = [ring_step(parts[step], "z", step) for step in range(1, 4)]
    by_group = jnp.einsum("gsk,sklc->glc", chosen, slotted, preferred_element_type=f32)
    by_group = exchange(by_group.astype(bf16), BATCH).astype(f32)
    owned = jnp.sum(by_group, axis=0).astype(bf16)
    heads = share(owned, BATCH, group_count).reshape(group_count * latent_count, 128)
    owned_parts = owners(heads, owned, all_latents)
    owned_parts, got[1] = lax.optimization_barrier((owned_parts, got[1]))
    ring_sum = sum([part.astype(f32) for part in got], parts[0].astype(f32))
    ring_sum = ring_sum.astype(bf16).reshape(group_count, 4, share_rows, 8, 128)
    ring_sum = ring_sum.reshape(4 * group_count, share_rows, 8, 128)
    over_seq = exchange(owned_parts, SEQ)
    ring_sum, over_seq = lax.optimization_barrier((ring_sum, over_seq))
    ring_sum = exchange(ring_sum, BATCH + ("y",))
    grad_outproj = lax.dot_general(
        heads[:, :head_dim], all_d_out, FIRST, preferred_element_type=f32
    )
    out, d_latents, grad_query = finish(over_seq, latents[0], d_out[0], w_query, w_out)
    ring_sum, out, d_latents, grad_query, grad_outproj = lax.optimization_barrier(
        (ring_sum, out, d_latents, grad_query, grad_outproj)
    )
    ring_sum = ring_sum.reshape(4, 2, 4, share_rows, 8, 128).astype(f32)
    halves = jnp.sum(ring_sum, axis=(0, 2)).reshape(2, share_rows, model_width)
    grad_kv = jnp.concatenate([halves[0], halves[1]], axis=1)
    return (out[None], d_latents[None], grad_query, grad_outproj, grad_kv)


def solution(mesh):
    chips = Mesh(mesh.devices.reshape(4, 2, 4, 4), ("x", "core", "z", "y"))
    in_specs = (
        P(BATCH, None, None),
        P(ALL, None, None),
        P(ALL),
        P(ALL),
        P(),
        P(),
        P(),
        P(BATCH, None, None),
    )
    out_specs = (
        P(BATCH, None, None),
        P(BATCH, None, None),
        P(SEQ, None),
        P(SEQ, None),
        P(ALL, None),
    )
    return jax.shard_map(local, mesh=chips, in_specs=in_specs, out_specs=out_specs, check_vma=False)
```

```python
import functools

import jax
import jax.numpy as jnp
from jax import lax
from jax.experimental import pallas as pl
from jax.experimental.pallas import tpu as pltpu
from jax.sharding import Mesh, PartitionSpec as P

H = 16
BATCH = ("x", "core")
SEQ = ("z", "y")
CHIPS = ("x", "z", "y")
ALL = BATCH + SEQ
SLOTS = 3
WIDE = 256
PER_STEP = 2

epsilon = 1e-06
f32 = jnp.float32
bf16 = jnp.bfloat16


def rms_rows(values):
    return values * lax.rsqrt(jnp.mean(values * values, axis=-1, keepdims=True) + epsilon)


def rms_back(values, grads):
    factor = lax.rsqrt(jnp.mean(values * values, axis=-1, keepdims=True) + epsilon)
    normed = values * factor
    return factor * (grads - normed * jnp.mean(grads * normed, axis=-1, keepdims=True))


def normalize(values):
    return rms_rows(values.astype(f32)).astype(bf16)


def exchange(values, axes):
    return lax.all_to_all(values, axes, 0, 0, tiled=True)


def share(values, axes, count):
    return exchange(jnp.broadcast_to(values[None], (count,) + values.shape), axes)


def other_core(values):
    return lax.ppermute(values, "core", [(0, 1), (1, 0)])


def ring_step(values, axis, step):
    return lax.ppermute(values, axis, [(i, (i + step) % 4) for i in range(4)])


def chip_step(values, step):
    return ring_step(values, "x", step)


def along_chips(values):
    return [values, chip_step(values, 1), chip_step(values, 2), chip_step(values, 3)]


def place_of(group):
    chip = lax.rem(lax.axis_index("x") - group // 2 + 4, 4)
    return jnp.where(group % 2 == lax.axis_index("core"), 0, 4) + chip


def group_at(place):
    chip = lax.rem(lax.axis_index("x") - place % 4 + 4, 4)
    core = lax.axis_index("core")
    return 2 * chip + (core if place < 4 else 1 - core)


SMEM = pl.BlockSpec(memory_space=pltpu.SMEM)
VMEM = pl.BlockSpec(memory_space=pltpu.VMEM)
HBM = pl.BlockSpec(memory_space=pltpu.HBM)
LAST = (((1,), (1,)), ((), ()))
FIRST = (((0,), (0,)), ((), ()))


def room(mebibytes):
    return pltpu.CompilerParams(vmem_limit_bytes=mebibytes * 1024 * 1024)


def pairs_kernel(frames_ref, w_ref, normed_ref, out_ref):
    @pl.when(pl.program_id(0) == 0)
    def _():
        normed_ref[...] = normalize(frames_ref[...])

    out_ref[...] = jnp.dot(normed_ref[...], w_ref[...], preferred_element_type=f32).astype(bf16)


def pair_up_kernel(first_ref, second_ref, out_ref):
    out_ref[0:1] = first_ref[...]
    out_ref[1:2] = second_ref[...]


def pair_up(first, second):
    return pl.pallas_call(
        pair_up_kernel,
        out_shape=jax.ShapeDtypeStruct((2,) + first.shape[1:], first.dtype),
        in_specs=[VMEM, VMEM],
        out_specs=VMEM,
        cost_estimate=pl.CostEstimate(flops=0, bytes_accessed=512 * 1024, transcendentals=0),
    )(first, second)


def project_pairs(frames, w_kv):
    rows, feature = frames.shape
    width, tile = w_kv.shape[1], 1024
    return pl.pallas_call(
        pairs_kernel,
        grid=(width // tile,),
        out_shape=(
            jax.ShapeDtypeStruct((rows, feature), bf16),
            jax.ShapeDtypeStruct((rows, width), bf16),
        ),
        in_specs=[
            pl.BlockSpec((rows, feature), lambda i: (0, 0)),
            pl.BlockSpec((feature, tile), lambda i: (0, i)),
        ],
        out_specs=(
            pl.BlockSpec((rows, feature), lambda i: (0, 0)),
            pl.BlockSpec((rows, tile), lambda i: (0, i)),
        ),
        cost_estimate=pl.CostEstimate(
            flops=2 * rows * feature * width, bytes_accessed=9 * 1024 * 1024, transcendentals=0
        ),
    )(frames, w_kv)


def low_lanes(shape):
    return lax.broadcasted_iota(jnp.int32, shape, len(shape) - 1) < 64


def spread(heads, masks):
    return jnp.concatenate([heads * mask for mask in masks], axis=0)


def head_masks():
    head = lax.broadcasted_iota(jnp.int32, (1, WIDE), 1) // 64
    return [jnp.where(head == at, 1.0, 0.0).astype(bf16) for at in range(WIDE // 64)]


def own_heads(product, rows):
    head = lax.broadcasted_iota(jnp.int32, (rows, WIDE), 1) // 64
    result = product[:rows]
    for at in range(1, WIDE // 64):
        result = jnp.where(head == at, product[at * rows : at * rows + rows], result)
    return result


def slots_of(groups):
    slots, used = [0], 1
    for i in range(1, 4):
        slot = used
        fresh = True
        for j in reversed(range(i)):
            slot = jnp.where(groups[i] == groups[j], slots[j], slot)
            fresh = fresh & (groups[i] != groups[j])
        slots.append(slot)
        used = used + jnp.where(fresh, 1, 0)
    return slots


def attend_kernel(counts, groups, places, *refs):
    pieces, (wq_in, wo_in, pairs_in, q_out, d_out, out_ref), scratch = refs[:8], refs[8:14], refs[14:]
    picked, wq, wo, pairs_ref, q_ref, d_ref, top_ref, total_ref, moment_ref, sems = scratch
    copies = [
        pltpu.make_async_copy(wq_in, wq, sems.at[0]),
        pltpu.make_async_copy(wo_in, wo, sems.at[1]),
        pltpu.make_async_copy(pairs_in, pairs_ref, sems.at[2]),
        pltpu.make_async_copy(q_ref, q_out, sems.at[3]),
        pltpu.make_async_copy(d_ref, d_out, sems.at[4]),
    ]
    for copy in copies[:3]:
        copy.start()
    rows, width = pieces[0].shape[1:]
    blocks = q_ref.shape[0] // rows
    for i in range(blocks):
        for j in range(8):

            @pl.when(places[i] == j)
            def _():
                picked[0, i * rows : (i + 1) * rows, :] = normalize(pieces[j][0])
                picked[1, i * rows : (i + 1) * rows, :] = pieces[j][1]

    copies[0].wait()
    for at in range(0, width, 256):
        tile = slice(at, at + 256)
        q_ref[:, tile] = jnp.dot(picked[0], wq[:, tile], preferred_element_type=f32).astype(bf16)
    copies[3].start()
    copies[1].wait()
    for at in range(0, width, 256):
        tile = slice(at, at + 256)
        d_ref[:, tile] = lax.dot_general(
            picked[1], wo[tile, :], LAST, preferred_element_type=f32
        ).astype(bf16)
    copies[4].start()
    copies[2].wait()

    masks = head_masks()
    scale = (width // H) ** (-0.5)
    position = lax.broadcasted_iota(jnp.int32, (128, WIDE), 0)

    def one_block(block, carry):
        usable = position < counts[block]
        here = pl.ds(pl.multiple_of(block * rows, rows), rows)
        there = pl.ds(pl.multiple_of(block * 128, 128), 128)
        for at in range(0, width, WIDE):
            cols = slice(at, at + WIDE)
            value_cols = slice(width + at, width + at + WIDE)
            s = lax.dot_general(
                pairs_ref[there, cols],
                spread(q_ref[here, cols], masks),
                LAST,
                preferred_element_type=f32,
            )
            s = jnp.where(usable, s * scale, -1e30)
            top = jnp.max(s, axis=0, keepdims=True)
            raw = jnp.where(usable, jnp.exp(s - top), 0.0)
            dw = lax.dot_general(
                pairs_ref[there, value_cols],
                spread(d_ref[here, cols], masks),
                LAST,
                preferred_element_type=f32,
            )
            total = jnp.sum(raw, axis=0, keepdims=True)
            moment = jnp.sum(raw * dw, axis=0, keepdims=True)
            for part in range(0, WIDE, 128):
                p = (at + part) // 128
                top_ref[block, p : p + 1, :] = top[:, part : part + 128]
                total_ref[block, p : p + 1, :] = total[:, part : part + 128]
                moment_ref[block, p : p + 1, :] = moment[:, part : part + 128]
        return carry

    lax.fori_loop(0, blocks, one_block, 0, unroll=4)
    own = [groups[i] for i in range(blocks)]
    slots = slots_of(own)
    left = low_lanes((8, 128))
    lane = lax.broadcasted_iota(jnp.int32, (8, 128), 1)
    note = jnp.full((8, 128), -1.0, f32)
    for i in range(blocks):
        note = jnp.where(lane == 64 + slots[i], own[i].astype(f32), note)
    for g in range(8):
        tops = [jnp.where(own[i] == g, top_ref[i], -1e30) for i in range(blocks)]
        top = functools.reduce(jnp.maximum, tops)
        total = jnp.zeros((8, 128), f32)
        moment = jnp.zeros((8, 128), f32)
        for i in range(blocks):
            factor = jnp.where(own[i] == g, jnp.exp(tops[i] - top), 0.0)
            total = total + factor * total_ref[i]
            moment = moment + factor * moment_ref[i]
        parts = (
            (jnp.where(left, top, pltpu.roll(total, 64, 1)), jnp.where(left, moment, note)),
            (
                jnp.where(left, pltpu.roll(top, 64, 1), total),
                jnp.where(left, pltpu.roll(moment, 64, 1), note),
            ),
        )
        for odd in range(2):
            for p in range(8):
                at = 16 * g + 8 * odd + p
                out_ref[at, :, 0:128] = parts[odd][0][p : p + 1]
                out_ref[at, :, 128:256] = parts[odd][1][p : p + 1]
    copies[3].wait()
    copies[4].wait()


def attend(counts, groups, places, pieces, w_query, w_out, pairs):
    rows, width = pieces[0].shape[1:]
    small = jax.ShapeDtypeStruct((groups.shape[0] * rows, width), bf16)
    return pl.pallas_call(
        attend_kernel,
        out_shape=(small, small, jax.ShapeDtypeStruct((128, 1, 256), f32)),
        in_specs=[SMEM] * 3 + [VMEM] * 8 + [HBM] * 3,
        out_specs=(HBM, HBM, VMEM),
        scratch_shapes=[
            pltpu.VMEM((2,) + small.shape, bf16),
            pltpu.VMEM(w_query.shape, bf16),
            pltpu.VMEM(w_out.shape, bf16),
            pltpu.VMEM(pairs.shape, bf16),
            pltpu.VMEM(small.shape, bf16),
            pltpu.VMEM(small.shape, bf16),
        ]
        + [pltpu.VMEM((groups.shape[0], 8, 128), f32)] * 3
        + [pltpu.SemaphoreType.DMA((5,))],
        cost_estimate=pl.CostEstimate(
            flops=6 * 1024 * 1024 * 1024,
            bytes_accessed=10 * 1024 * 1024,
            transcendentals=512 * 1024,
        ),
    )(counts, groups, places, *pieces, w_query, w_out, pairs)


def block_specs(latent_count, width):
    return [
        pl.BlockSpec((PER_STEP * latent_count, width), lambda i: (i, 0)),
        pl.BlockSpec((PER_STEP * latent_count, width), lambda i: (i, 0)),
        pl.BlockSpec((PER_STEP * 128, 2 * width), lambda i: (i, 0)),
    ]


def products_kernel(q_ref, d_ref, pairs_ref, scores_ref, d_weights_ref):
    masks = head_masks()
    width = q_ref.shape[1]
    rows = q_ref.shape[0] // PER_STEP
    scale = (width // H) ** (-0.5)
    for sub in range(PER_STEP):
        here = slice(sub * rows, sub * rows + rows)
        there = slice(sub * 128, sub * 128 + 128)
        for at in range(0, width, WIDE):
            cols = slice(at, at + WIDE)
            value_cols = slice(width + at, width + at + WIDE)
            scores_ref[there, cols] = scale * lax.dot_general(
                pairs_ref[there, cols],
                spread(q_ref[here, cols], masks),
                LAST,
                preferred_element_type=f32,
            )
            d_weights_ref[there, cols] = lax.dot_general(
                pairs_ref[there, value_cols],
                spread(d_ref[here, cols], masks),
                LAST,
                preferred_element_type=f32,
            )


def products(queries, d_mixed, pairs):
    width = queries.shape[1]
    out = jax.ShapeDtypeStruct((pairs.shape[0], width), f32)
    spec = pl.BlockSpec((PER_STEP * 128, width), lambda i: (i, 0))
    return pl.pallas_call(
        products_kernel,
        grid=(4 // PER_STEP,),
        out_shape=(out, out),
        in_specs=block_specs(queries.shape[0] // 4, width),
        out_specs=(spec, spec),
        cost_estimate=pl.CostEstimate(
            flops=2 * 1024 * 1024 * 1024, bytes_accessed=8 * 1024 * 1024, transcendentals=0
        ),
    )(queries, d_mixed, pairs)


def totals_kernel(in_ref, out_ref):
    left = low_lanes((1, 128))
    first = in_ref[:, 0, 0:128]
    top = jnp.max(first, axis=0, keepdims=True)
    top = jnp.where(left, top, pltpu.roll(top, 64, 1))
    factor = jnp.exp(jnp.where(left, first, pltpu.roll(first, 64, 1)) - top)
    total = jnp.sum(factor * first, axis=0, keepdims=True)
    inverse = 1.0 / jnp.where(left, pltpu.roll(total, 64, 1), total)
    delta = jnp.sum(factor * in_ref[:, 0, 128:256], axis=0, keepdims=True) * inverse
    reply = jnp.concatenate(
        [jnp.where(left, top, inverse), jnp.where(left, delta, 0.0)], axis=1
    )
    for at in range(in_ref.shape[0]):
        out_ref[at] = reply


def totals(stats):
    return pl.pallas_call(
        totals_kernel,
        out_shape=jax.ShapeDtypeStruct(stats.shape, f32),
        in_specs=[VMEM],
        out_specs=VMEM,
        compiler_params=room(4),
    )(stats)


def grads_kernel(
    counts,
    groups,
    core,
    q_ref,
    d_ref,
    pairs_ref,
    scores_ref,
    d_weights_ref,
    reply_ref,
    kept_ref,
    sent_ref,
    slotted_ref,
    mixed_acc,
    query_acc,
    mixed_now,
    query_now,
):
    step = pl.program_id(0)
    masks = head_masks()
    width = q_ref.shape[1]
    rows = q_ref.shape[0] // PER_STEP
    scale = (width // H) ** (-0.5)
    position = lax.broadcasted_iota(jnp.int32, (128, WIDE), 0)
    left = low_lanes((8, 128))
    wide = low_lanes((rows, 128))

    @pl.when(step == 0)
    def _():
        mixed_acc[...] = jnp.zeros_like(mixed_acc)
        query_acc[...] = jnp.zeros_like(query_acc)

    def row(pairs, at):
        first = at // 128
        return jnp.concatenate([pairs[p : p + 1] for p in range(first, first + WIDE // 128)], axis=1)

    slots = slots_of([groups[i] for i in range(4)])
    for sub in range(PER_STEP):
        block = step * PER_STEP + sub
        here = slice(sub * rows, sub * rows + rows)
        there = slice(sub * 128, sub * 128 + 128)
        usable = position < counts[block]
        group = groups[block]

        def reply_rows(odd, cols):
            first = 16 * group + 8 * odd
            return jnp.concatenate([reply_ref[first + p, :, cols] for p in range(8)], axis=0)

        even = reply_rows(0, slice(0, 128))
        odd = reply_rows(1, slice(0, 128))
        top = jnp.where(left, even, pltpu.roll(odd, 64, 1))
        inverse = jnp.where(left, pltpu.roll(even, 64, 1), odd)
        delta = jnp.where(
            left, reply_rows(0, slice(128, 256)), pltpu.roll(reply_rows(1, slice(128, 256)), 64, 1)
        )
        for at in range(0, width, WIDE):
            cols = slice(at, at + WIDE)
            value_cols = slice(width + at, width + at + WIDE)
            q = spread(q_ref[here, cols], masks)
            d = spread(d_ref[here, cols], masks)
            k = pairs_ref[there, cols]
            v = pairs_ref[there, value_cols]
            s = scores_ref[there, cols]
            dw = d_weights_ref[there, cols]
            weights = jnp.where(usable, jnp.exp(s - row(top, at)) * row(inverse, at), 0.0)
            weights_b = weights.astype(bf16)
            d_scores = (weights * (dw - row(delta, at)) * scale).astype(bf16)
            d_values = jnp.dot(weights_b, d, preferred_element_type=f32)
            d_keys = jnp.dot(d_scores, q, preferred_element_type=f32)
            kept_ref[there, cols] = jnp.where(core[0] == 0, d_keys, d_values).astype(bf16)
            sent_ref[there, cols] = jnp.where(core[0] == 0, d_values, d_keys).astype(bf16)
            mixed = lax.dot_general(weights_b, v, FIRST, preferred_element_type=f32)
            mixed_now[sub, :, cols] = own_heads(mixed, rows)
            query = lax.dot_general(d_scores, k, FIRST, preferred_element_type=f32)
            query_now[sub, :, cols] = own_heads(query, rows)
    for sub in range(PER_STEP):
        slot = slots[sub]
        for at in range(1, 4 // PER_STEP):
            slot = jnp.where(step == at, slots[at * PER_STEP + sub], slot)
        mixed_acc[slot] += mixed_now[sub]
        query_acc[slot] += query_now[sub]

    @pl.when(step == 4 // PER_STEP - 1)
    def _():
        for at in range(SLOTS):
            for p in range(width // 128):
                cols = slice(128 * p, 128 * p + 128)
                mixed = mixed_acc[at, :, cols]
                query = query_acc[at, :, cols]
                slotted_ref[2 * p, at] = jnp.where(
                    wide, mixed, pltpu.roll(query, 64, 1)
                ).astype(bf16)
                slotted_ref[2 * p + 1, at] = jnp.where(
                    wide, pltpu.roll(mixed, 64, 1), query
                ).astype(bf16)


def gradients(counts, groups, core, queries, d_mixed, pairs, scores, d_weights, reply):
    width = queries.shape[1]
    rows = queries.shape[0] // 4
    return pl.pallas_call(
        grads_kernel,
        grid=(4 // PER_STEP,),
        out_shape=(
            jax.ShapeDtypeStruct((pairs.shape[0], width), bf16),
            jax.ShapeDtypeStruct((pairs.shape[0], width), bf16),
            jax.ShapeDtypeStruct((H, SLOTS, rows, 128), bf16),
        ),
        in_specs=[SMEM, SMEM, SMEM]
        + block_specs(rows, width)
        + [pl.BlockSpec((PER_STEP * 128, width), lambda i: (i, 0))] * 2
        + [pl.BlockSpec((128, 1, 256), lambda i: (0, 0, 0))],
        out_specs=(
            pl.BlockSpec((PER_STEP * 128, width), lambda i: (i, 0)),
            pl.BlockSpec((PER_STEP * 128, width), lambda i: (i, 0)),
            pl.BlockSpec((H, SLOTS, rows, 128), lambda i: (0, 0, 0, 0)),
        ),
        scratch_shapes=[pltpu.VMEM((SLOTS, rows, width), f32)] * 2
        + [pltpu.VMEM((PER_STEP, rows, width), f32)] * 2,
        cost_estimate=pl.CostEstimate(
            flops=8 * 1024 * 1024 * 1024, bytes_accessed=8 * 1024 * 1024, transcendentals=512 * 1024
        ),
    )(counts, groups, core, queries, d_mixed, pairs, scores, d_weights, reply)


def prepare_kernel(owners, *refs):
    pieces, (latents_ref, d_out_ref) = refs[:8], refs[8:]
    rows = pieces[0].shape[1]
    for j in range(8):
        at = pl.ds(pl.multiple_of(owners[j] * rows, rows), rows)
        latents_ref[at, :] = normalize(pieces[j][0])
        d_out_ref[at, :] = pieces[j][1]


def prepare(owners, pieces):
    rows, width = pieces[0].shape[1:]
    out = jax.ShapeDtypeStruct((8 * rows, width), bf16)
    return pl.pallas_call(
        prepare_kernel,
        out_shape=(out, out),
        in_specs=[SMEM] + [VMEM] * 8,
        out_specs=(VMEM, VMEM),
        cost_estimate=pl.CostEstimate(
            flops=4 * 1024 * 1024, bytes_accessed=4 * 1024 * 1024, transcendentals=512
        ),
    )(owners, *pieces)


def owners_kernel(heads_ref, owned_ref, latents_ref, out_ref):
    rows = owned_ref.shape[0]
    query = lax.dot_general(
        latents_ref[...], heads_ref[...], FIRST, preferred_element_type=f32
    )
    other = pltpu.roll(query, 64, 1)
    half = rows // 2
    left = low_lanes((half, 128))
    for at in range(H):
        first, second = rows * at, rows * at + half
        out_ref[at, :rows] = owned_ref[...]
        out_ref[at, rows:] = jnp.where(
            left, other[first : first + half], query[second : second + half]
        ).astype(bf16)


def owners(heads, owned, normed_latents):
    rows = owned.shape[0]
    return pl.pallas_call(
        owners_kernel,
        out_shape=jax.ShapeDtypeStruct((H, rows + rows // 2, 128), bf16),
        in_specs=[VMEM] * 3,
        out_specs=VMEM,
        compiler_params=room(12),
        cost_estimate=pl.CostEstimate(
            flops=256 * 1024 * 1024, bytes_accessed=2 * 1024 * 1024, transcendentals=0
        ),
    )(heads, owned, normed_latents)


def finish_kernel(in_ref, latent_ref, d_out_ref, w_query_ref, w_out_in, *refs):
    out_ref, d_latents_ref, grad_query_ref, mixed, d_query, w_out_ref, sem = refs
    copy = pltpu.make_async_copy(w_out_in, w_out_ref, sem)
    copy.start()
    rows = latent_ref.shape[0]
    left = low_lanes((rows, 128))

    def parts(head):
        both = in_ref[head, rows:].astype(f32)
        return in_ref[head, :rows].astype(f32), both, pltpu.roll(both, 64, 1)

    for p in range(H // 2):
        cols = slice(128 * p, 128 * p + 128)
        even, even_grad, even_turned = parts(2 * p)
        odd, odd_grad, odd_turned = parts(2 * p + 1)
        mixed[:, cols] = jnp.where(left, even, pltpu.roll(odd, 64, 1)).astype(bf16)
        d_query[:, cols] = jnp.where(left, pltpu.roll(even, 64, 1), odd).astype(bf16)
        half = rows // 2
        narrow = left[:half]
        grad_query_ref[:half, cols] = jnp.where(narrow, even_grad, odd_turned)
        grad_query_ref[half:, cols] = jnp.where(narrow, even_turned, odd_grad)
    latent = latent_ref[...].astype(f32)
    d_normed = lax.dot_general(d_query[...], w_query_ref[...], LAST, preferred_element_type=f32)
    d_latents_ref[...] = (d_out_ref[...].astype(f32) + rms_back(latent, d_normed)).astype(bf16)
    copy.wait()
    update = jnp.dot(mixed[...], w_out_ref[...], preferred_element_type=f32)
    out_ref[...] = (latent + update).astype(bf16)


def finish(over_seq, latent, d_out, w_query, w_out):
    rows, width = latent.shape
    small = jax.ShapeDtypeStruct((rows, width), bf16)
    return pl.pallas_call(
        finish_kernel,
        out_shape=(small, small, jax.ShapeDtypeStruct((rows, width), f32)),
        in_specs=[VMEM] * 4 + [HBM],
        out_specs=(VMEM,) * 3,
        compiler_params=room(12),
        scratch_shapes=[pltpu.VMEM((rows, width), bf16)] * 2
        + [pltpu.VMEM(w_out.shape, bf16), pltpu.SemaphoreType.DMA],
    )(over_seq, latent, d_out, w_query, w_out)


def local(latents, frames, counts, groups, w_query, w_kv, w_out, d_out):
    blocks, block_rows, feature = frames.shape
    latent_count, model_width = latents.shape[1:]
    head_dim = model_width // H
    group_count, seq_count = 8, 16
    rows = blocks * block_rows
    core = lax.axis_index("core")
    batch_at = lax.axis_index(BATCH)

    near = along_chips(pair_up(latents, d_out))
    normed, pairs = project_pairs(frames.reshape(rows, feature), w_kv)
    sources = jnp.stack([group_at(j) for j in range(8)])
    places = place_of(groups)
    near = [lax.optimization_barrier((piece, normed, pairs))[0] for piece in near]
    near[0], sources, places = lax.optimization_barrier((near[0], sources, places))
    pieces = near + [other_core(piece) for piece in near]
    queries, d_mixed, stats = attend(
        counts, groups, places, pieces, w_query, w_out, pairs
    )
    normed, stats, queries, d_mixed = lax.optimization_barrier((normed, stats, queries, d_mixed))
    scores, d_weights = products(queries, d_mixed, pairs)
    normed = jnp.concatenate([normed, other_core(normed)], axis=0)
    stats = exchange(stats, ALL)
    source_groups = lax.dynamic_slice(
        stats, (batch_at * seq_count, 0, 192), (seq_count, 1, SLOTS)
    )
    chosen = (
        jnp.arange(group_count, dtype=f32)[:, None, None] == source_groups.reshape(1, seq_count, SLOTS)
    ).astype(bf16)
    reply, sources = lax.optimization_barrier((totals(stats), sources))
    all_latents, all_d_out = prepare(sources, pieces)
    reply = exchange(reply, ALL)
    reply, all_latents, all_d_out, normed, chosen, scores, d_weights = lax.optimization_barrier(
        (reply, all_latents, all_d_out, normed, chosen, scores, d_weights)
    )
    kept, sent, slotted = gradients(
        counts, groups, core.reshape(1), queries, d_mixed, pairs, scores, d_weights, reply
    )
    slotted = exchange(slotted, SEQ)

    d_half = jnp.concatenate([kept, other_core(sent)], axis=0)
    term = lax.dot_general(normed, d_half, FIRST, preferred_element_type=f32).astype(bf16)
    share_rows = feature // 128
    term = term.reshape(group_count, 4, 4 * share_rows, 8, 128)
    z_at = lax.axis_index("z")

    def z_part(step):
        return lax.dynamic_index_in_dim(term, lax.rem(z_at + step, 4), 1, False)

    parts = lax.optimization_barrier([z_part(step) for step in range(4)])
    got = [ring_step(parts[step], "z", step) for step in range(1, 4)]
    by_group = jnp.einsum("gsk,sklc->glc", chosen, slotted, preferred_element_type=f32)
    by_group = exchange(by_group.astype(bf16), BATCH).astype(f32)
    owned = jnp.sum(by_group, axis=0).astype(bf16)
    heads = share(owned, BATCH, group_count).reshape(group_count * latent_count, 128)
    owned_parts = owners(heads, owned, all_latents)
    owned_parts, got[1] = lax.optimization_barrier((owned_parts, got[1]))
    ring_sum = sum([part.astype(f32) for part in got], parts[0].astype(f32))
    ring_sum = ring_sum.astype(bf16).reshape(group_count, 4, share_rows, 8, 128)
    ring_sum = ring_sum.reshape(4 * group_count, share_rows, 8, 128)
    over_seq = exchange(owned_parts, SEQ)
    ring_sum, over_seq = lax.optimization_barrier((ring_sum, over_seq))
    ring_sum = exchange(ring_sum, BATCH + ("y",))
    grad_outproj = lax.dot_general(
        heads[:, :head_dim], all_d_out, FIRST, preferred_element_type=f32
    )
    out, d_latents, grad_query = finish(over_seq, latents[0], d_out[0], w_query, w_out)
    ring_sum, out, d_latents, grad_query, grad_outproj = lax.optimization_barrier(
        (ring_sum, out, d_latents, grad_query, grad_outproj)
    )
    ring_sum = ring_sum.reshape(4, 2, 4, share_rows, 8, 128).astype(f32)
    halves = jnp.sum(ring_sum, axis=(0, 2)).reshape(2, share_rows, model_width)
    grad_kv = jnp.concatenate([halves[0], halves[1]], axis=1)
    return (out[None], d_latents[None], grad_query, grad_outproj, grad_kv)


def solution(mesh):
    chips = Mesh(mesh.devices.reshape(4, 2, 4, 4), ("x", "core", "z", "y"))
    in_specs = (
        P(BATCH, None, None),
        P(ALL, None, None),
        P(ALL),
        P(ALL),
        P(),
        P(),
        P(),
        P(BATCH, None, None),
    )
    out_specs = (
        P(BATCH, None, None),
        P(BATCH, None, None),
        P(SEQ, None),
        P(SEQ, None),
        P(ALL, None),
    )
    return jax.shard_map(local, mesh=chips, in_specs=in_specs, out_specs=out_specs, check_vma=False)
```
